32 devices in a mesh: gx: 8 (over z, x), gy: 4 (over y, core).
Axes of the slice: x: 2, y: 2, z: 4, core: 2. Of those that a mesh axis runs over, the one named last changes fastest.
Arguments:
- features: float32 [16, 64, 64, 128], P(None, 'gx', 'gy'), may hold values from -6 to 6
- conv_weight: float32 [27, 16, 16], replicated, may hold values from -0.3125 to 0.3125
- mix_weight: float32 [2, 16, 16, 4, 1728], P(None, None, None, 'gy', 'gx'), may hold values from -1 to 1
Outputs:
- layer_out: float32 [16, 64, 64, 128], P(None, 'gx', 'gy')
The draws below stay inside these ranges and needn't reach their ends.
All inputs are finite; a program needn't handle non-finite values.
Results may differ from the reference program's by a relative error of at most 0.0001.
Values sent between devices are 32-bit elements; how exact they have to be, the bound alone decides.
No kernel may reach another device: no remote copies, remote signals or barrier semaphores. Data moves between devices by JAX's collectives and lax.ppermute only.
A program may use at most 128 MiB of HBM per device.

```python
import math
import jax
import jax.numpy as jnp
from jax import lax

C = 16
NZ = 128
KX = 24
KY = 24
KZ = 12
NX = 64
NY = 64
KYZ_DEV = 72
N_GY = 4


def shard_levels(key, dims, pieces, low, high):
    level = 1.0
    for axis_at, shards_of in pieces:
        draws = jax.random.uniform(jax.random.fold_in(jax.random.fold_in(key, 6), axis_at), (shards_of,), jnp.float32, low / len(pieces), high / len(pieces))
        level = level * jnp.repeat(jnp.exp(draws), dims[axis_at] // shards_of).reshape((-1,) + (1,) * (len(dims) - 1 - axis_at))
    return level


def normal_values(key, dims, deviation, limit, cuts=(), kind=jnp.bfloat16):
    array = jax.random.normal(key, dims, jnp.float32) * deviation
    if len(cuts) > 0:
        array = shard_levels(key, dims, cuts, -0.22, 0.18) * array
    return jnp.clip(array, min=-limit, max=limit).astype(kind)


def setup_inputs(seed: int = 0) -> dict:
    keys = jax.random.split(jax.random.key(seed), 4)
    features = normal_values(keys[0], (C, NX, NY, NZ), 1.0, 6.0, ((1, 8), (2, 4)), jnp.float32)
    conv_weight = normal_values(keys[1], (27, C, C), (27 * C) ** -0.5, 0.3125, (), jnp.float32)
    mix_weight = normal_values(keys[2], (2, C, C, N_GY, KX * KYZ_DEV), 0.177, 1.0, ((3, 4), (4, 8)), jnp.float32)
    return dict(features=features, conv_weight=conv_weight, mix_weight=mix_weight)


PRECISE = lax.Precision.HIGHEST

def angle_tables(positions, frequencies, length):
    product = positions[:, None] * frequencies[None, :] % length
    angles = product.astype(jnp.float32) * (2.0 * math.pi / length)
    return (jnp.cos(angles), jnp.sin(angles))

def kept_frequencies(amount, length):
    index = jnp.arange(amount, dtype=jnp.int32)
    return jnp.where(index < amount // 2, index, length - amount + index).astype(jnp.int32)

def reference(features, conv_weight, mix_weight):
    conv_sum = jnp.zeros(features.shape, jnp.float32)
    for shift_x in (-1, 0, 1):
        for shift_y in (-1, 0, 1):
            for shift_z in (-1, 0, 1):
                offset = 9 * (shift_x + 1) + 3 * (shift_y + 1) + (shift_z + 1)
                moved = jnp.roll(features, (-shift_x, -shift_y, -shift_z), axis=(1, 2, 3))
                conv_sum = conv_sum + jnp.einsum('oi,ixyz->oxyz', conv_weight[offset], moved, precision=PRECISE)
    length_x = features.shape[1]
    length_y = features.shape[2]
    length_z = features.shape[3]
    cos_z, sin_z = angle_tables(jnp.arange(length_z, dtype=jnp.int32), jnp.arange(KZ, dtype=jnp.int32), length_z)
    cos_y, sin_y = angle_tables(jnp.arange(length_y, dtype=jnp.int32), kept_frequencies(KY, length_y), length_y)
    cos_x, sin_x = angle_tables(jnp.arange(length_x, dtype=jnp.int32), kept_frequencies(KX, length_x), length_x)
    z_real = jnp.dot(features, cos_z, precision=PRECISE)
    z_imag = -jnp.dot(features, sin_z, precision=PRECISE)
    y_real = jnp.einsum('cxyk,yq->cxqk', z_real, cos_y, precision=PRECISE) + jnp.einsum('cxyk,yq->cxqk', z_imag, sin_y, precision=PRECISE)
    y_imag = jnp.einsum('cxyk,yq->cxqk', z_imag, cos_y, precision=PRECISE) - jnp.einsum('cxyk,yq->cxqk', z_real, sin_y, precision=PRECISE)
    forward_scale = 1.0 / math.sqrt(length_x * length_y * length_z)
    coef_real = (jnp.einsum('cxqk,xp->cpqk', y_real, cos_x, precision=PRECISE) + jnp.einsum('cxqk,xp->cpqk', y_imag, sin_x, precision=PRECISE)) * forward_scale
    coef_imag = (jnp.einsum('cxqk,xp->cpqk', y_imag, cos_x, precision=PRECISE) - jnp.einsum('cxqk,xp->cpqk', y_real, sin_x, precision=PRECISE)) * forward_scale
    channels = features.shape[0]
    weights = mix_weight.reshape(2, channels, channels, N_GY, KX, KY * KZ // N_GY)
    weights = weights.transpose(0, 1, 2, 4, 3, 5).reshape(2, channels, channels, KX, KY, KZ)
    weight_real = weights[0]
    weight_imag = weights[1]
    mixed_real = jnp.einsum('oipqk,ipqk->opqk', weight_real, coef_real, precision=PRECISE) - jnp.einsum('oipqk,ipqk->opqk', weight_imag, coef_imag, precision=PRECISE)
    mixed_imag = jnp.einsum('oipqk,ipqk->opqk', weight_real, coef_imag, precision=PRECISE) + jnp.einsum('oipqk,ipqk->opqk', weight_imag, coef_real, precision=PRECISE)
    back_real = jnp.einsum('cpqk,xp->cxqk', mixed_real, cos_x, precision=PRECISE) - jnp.einsum('cpqk,xp->cxqk', mixed_imag, sin_x, precision=PRECISE)
    back_imag = jnp.einsum('cpqk,xp->cxqk', mixed_imag, cos_x, precision=PRECISE) + jnp.einsum('cpqk,xp->cxqk', mixed_real, sin_x, precision=PRECISE)
    plane_real = jnp.einsum('cxqk,yq->cxyk', back_real, cos_y, precision=PRECISE) - jnp.einsum('cxqk,yq->cxyk', back_imag, sin_y, precision=PRECISE)
    plane_imag = jnp.einsum('cxqk,yq->cxyk', back_imag, cos_y, precision=PRECISE) + jnp.einsum('cxqk,yq->cxyk', back_real, sin_y, precision=PRECISE)
    inverse_scale = 1.0 / math.sqrt(KX * KY * KZ)
    spectral = (jnp.dot(plane_real, cos_z.T, precision=PRECISE) - jnp.dot(plane_imag, sin_z.T, precision=PRECISE)) * inverse_scale
    return jax.nn.gelu(conv_sum + spectral, approximate=False)
```

```python
import functools
import math

import jax
import jax.numpy as jnp
import ml_dtypes
import numpy as np
from jax import lax
from jax.experimental import pallas as pl
from jax.experimental.pallas import tpu as pltpu
from jax.sharding import PartitionSpec as P

KX = 24
KY = 24
KZ = 12
LANES = 128
F32 = jnp.float32
BF16 = jnp.bfloat16
PRECISE = lax.Precision.HIGHEST
VMEM_LIMIT = 48 * 1024 * 1024
NN = (((1,), (0,)), ((), ()))
NT = (((1,), (1,)), ((), ()))


def kernel_call(body, out_shape, scratch=(), grid_spec=None, **kw):
    params = pltpu.CompilerParams(vmem_limit_bytes=VMEM_LIMIT)
    if grid_spec is not None:
        kw["grid_spec"] = grid_spec
    else:
        kw["scratch_shapes"] = list(scratch)
    return pl.pallas_call(body, out_shape=out_shape, compiler_params=params, **kw)


def halves(value):
    high = value.astype(BF16)
    return high, (value - high.astype(F32)).astype(BF16)


def dot(a, b, dims=NN):
    return lax.dot_general(a, b, dims, preferred_element_type=F32)


def dot3(a, b, dims=NN):
    return dot(a[0], b[0], dims) + (dot(a[0], b[1], dims) + dot(a[1], b[0], dims))


def table_halves(table):
    table = np.asarray(table, np.float64)
    high = table.astype(ml_dtypes.bfloat16)
    low = (table - high.astype(np.float64)).astype(ml_dtypes.bfloat16)
    return high, low


def kept_np(amount, length):
    index = np.arange(amount)
    return np.where(index < amount // 2, index, length - amount + index)


def angles_np(positions, frequencies, length):
    return 2.0 * np.pi * ((positions[:, None] * frequencies[None, :]) % length) / length


def band_kernel(channels, cells_y, weight_ref, main_h, main_l, side_h, side_l, base_h, base_l):
    main = channels * cells_y
    width = main + 2 * channels
    w_h, w_l = halves(weight_ref[...])
    row = lax.broadcasted_iota(jnp.int32, (channels, width), 0)
    col = lax.broadcasted_iota(jnp.int32, (channels, width), 1)
    source = jnp.where(col < main, col // cells_y, (col - main) % channels)
    spread = jnp.where(row == source, 1.0, 0.0).astype(BF16)
    base_h[...] = dot(w_h, spread)
    base_l[...] = dot(w_l, spread)
    y_out = lax.broadcasted_iota(jnp.int32, (cells_y, main), 0)
    y_in = lax.broadcasted_iota(jnp.int32, (cells_y, main), 1) % cells_y
    tap = y_in - y_out + 1
    side_y = lax.broadcasted_iota(jnp.int32, (cells_y, 2 * channels), 0)
    side_c = lax.broadcasted_iota(jnp.int32, (cells_y, 2 * channels), 1)
    first = (side_y == 0) & (side_c < channels)
    last = (side_y == cells_y - 1) & (side_c >= channels)

    def step(o, carry):
        for base, out_main, out_side in ((base_h, main_h, side_h), (base_l, main_l, side_l)):
            for c in range(3):
                at = pl.multiple_of(c * main + o * cells_y, cells_y)
                for a in range(3):
                    taps = [base[pl.ds((9 * a + 3 * b + c) * channels + o, 1), :] for b in range(3)]
                    block = jnp.zeros((cells_y, main), F32)
                    for b in range(3):
                        block = jnp.where(tap == b, taps[b][:, :main], block)
                    out_main[pl.ds(at, cells_y), a * main : (a + 1) * main] = block.astype(BF16)
                    edge = jnp.where(first, taps[0][:, main:], jnp.where(last, taps[2][:, main:], 0.0))
                    out_side[a, pl.ds(at, cells_y), :] = edge.astype(BF16)
        return carry

    lax.fori_loop(0, channels, step, 0)


def band_weights(conv_weight, cells_y):
    channels = conv_weight.shape[1]
    main = channels * cells_y
    shapes = [
        jax.ShapeDtypeStruct((3 * main, 3 * main), BF16),
        jax.ShapeDtypeStruct((3 * main, 3 * main), BF16),
        jax.ShapeDtypeStruct((3, 3 * main, 2 * channels), BF16),
        jax.ShapeDtypeStruct((3, 3 * main, 2 * channels), BF16),
    ]
    return kernel_call(
        functools.partial(band_kernel, channels, cells_y),
        shapes,
        [pltpu.VMEM((27 * channels, main + 2 * channels), F32)] * 2,
    )(conv_weight.reshape(27 * channels, channels))


def conv_kernel(feat, x_low, x_high, y_low, y_high, main_h, main_l, side_h, side_l, out, rows_h, rows_l, edge_h, edge_l):
    channels, cells_x, cells_y, length_z = feat.shape
    main = channels * cells_y
    side = 2 * channels
    for x in range(cells_x + 2):
        if x == 0:
            plane = x_low[:, 0]
        elif x == cells_x + 1:
            plane = x_high[:, 0]
        else:
            plane = feat[:, x - 1]
        high, low = halves(plane.reshape(main, length_z))
        rows_h[x * main : (x + 1) * main, :] = high
        rows_l[x * main : (x + 1) * main, :] = low
        edge = jnp.concatenate([y_low[x], y_high[x]], axis=0)
        high, low = halves(edge)
        edge_h[x * side : (x + 1) * side, :] = high
        edge_l[x * side : (x + 1) * side, :] = low
    for x in range(0, cells_x, 2):
        def pair(ref, size, count):
            return jnp.concatenate([ref[(x + p) * size : (x + p + count) * size, :] for p in (0, 1)], axis=1)

        body = (pair(rows_h, main, 3), pair(rows_l, main, 3))
        total = [None, None]
        for c in range(3):
            part = dot3((main_h[c * main : (c + 1) * main, :], main_l[c * main : (c + 1) * main, :]), body)
            for a in range(3):
                rim_at = [jnp.concatenate([ref[(x + p + a) * side : (x + p + a + 1) * side, :] for p in (0, 1)], axis=1) for ref in (edge_h, edge_l)]
                part = part + dot3((side_h[a, c * main : (c + 1) * main, :], side_l[a, c * main : (c + 1) * main, :]), rim_at)
            for p in (0, 1):
                piece = part[:, p * length_z : (p + 1) * length_z]
                if c != 1:
                    piece = pltpu.roll(piece, (1 - c) % length_z, 1)
                total[p] = piece if total[p] is None else total[p] + piece
        for p in (0, 1):
            out[:, x + p] = total[p].reshape(channels, cells_y, length_z)


def conv_bricks(feat, x_low, x_high, y_low, y_high, bands):
    channels, cells_x, cells_y, length_z = feat.shape
    main = channels * cells_y
    side = 2 * channels
    reach = cells_x + 2
    return kernel_call(
        conv_kernel,
        jax.ShapeDtypeStruct(feat.shape, F32),
        [
            pltpu.VMEM((reach * main, length_z), BF16),
            pltpu.VMEM((reach * main, length_z), BF16),
            pltpu.VMEM((reach * side, length_z), BF16),
            pltpu.VMEM((reach * side, length_z), BF16),
        ],
    )(feat, x_low, x_high, y_low, y_high, *bands)


def ring(value, axis, step):
    size = lax.axis_size(axis)
    return lax.ppermute(value, axis, [(i, (i + step) % size) for i in range(size)])


def halos(features):
    cells_x, cells_y = features.shape[1:3]
    with jax.named_scope("halo_x"):
        x_low = ring(features[:, cells_x - 1 :], "gx", 1)
        x_high = ring(features[:, :1], "gx", -1)
    with jax.named_scope("halo_y"):
        def face(y):
            whole = jnp.concatenate([x_low[:, :, y], features[:, :, y], x_high[:, :, y]], axis=1)
            return whole.transpose(1, 0, 2)

        y_low = ring(face(cells_y - 1), "gy", 1)
        y_high = ring(face(0), "gy", -1)
    return x_low, x_high, y_low, y_high


def angle_tables(positions, frequencies, length):
    product = positions[:, None] * frequencies[None, :] % length
    angles = product.astype(jnp.float32) * (2.0 * math.pi / length)
    return (jnp.cos(angles), jnp.sin(angles))


def kept_frequencies(amount, length):
    index = jnp.arange(amount, dtype=jnp.int32)
    return jnp.where(index < amount // 2, index, length - amount + index)


def times(form, a, b, c, d):
    one = functools.partial(jnp.einsum, form, precision=PRECISE)
    return one(a, c) + one(b, d)


def spectral_any(features, mix_weight):
    channels, cells_x, cells_y, length_z = features.shape
    count_gx = lax.axis_size("gx")
    count_gy = lax.axis_size("gy")
    length_x = cells_x * count_gx
    length_y = cells_y * count_gy
    block_yz = KY * KZ // count_gy
    cos_z, sin_z = angle_tables(jnp.arange(length_z, dtype=jnp.int32), jnp.arange(KZ, dtype=jnp.int32), length_z)
    y_places = lax.axis_index("gy") * cells_y + jnp.arange(cells_y, dtype=jnp.int32)
    x_places = lax.axis_index("gx") * cells_x + jnp.arange(cells_x, dtype=jnp.int32)
    cos_y, sin_y = angle_tables(y_places, kept_frequencies(KY, length_y), length_y)
    cos_x, sin_x = angle_tables(x_places, kept_frequencies(KX, length_x), length_x)
    along_z = jnp.dot(features, jnp.concatenate([cos_z, -sin_z], axis=1), precision=PRECISE)
    z_real = along_z[..., :KZ]
    z_imag = along_z[..., KZ:]
    y_real = times("cxyk,yq->cxqk", z_real, z_imag, cos_y, sin_y)
    y_imag = times("cxyk,yq->cxqk", z_imag, z_real, cos_y, -sin_y)
    partial_value = jnp.stack([y_real, y_imag], axis=2).reshape(channels, cells_x, 2, KY * KZ)
    y_share = lax.psum_scatter(partial_value, "gy", scatter_dimension=3, tiled=True)
    x_real = times("cxm,xp->cpm", y_share[:, :, 0], y_share[:, :, 1], cos_x, sin_x)
    x_imag = times("cxm,xp->cpm", y_share[:, :, 1], y_share[:, :, 0], cos_x, -sin_x)
    x_partial = jnp.stack([x_real, x_imag], axis=1).reshape(channels, 2, KX * block_yz)
    owned_modes = lax.psum_scatter(x_partial, "gx", scatter_dimension=2, tiled=True)
    owned_modes = owned_modes * (1.0 / math.sqrt(length_x * length_y * length_z))
    coef_real = owned_modes[:, 0]
    coef_imag = owned_modes[:, 1]
    weight_real = mix_weight[0, :, :, 0, :]
    weight_imag = mix_weight[1, :, :, 0, :]
    mixed_real = times("oim,im->om", weight_real, weight_imag, coef_real, -coef_imag)
    mixed_imag = times("oim,im->om", weight_real, weight_imag, coef_imag, coef_real)
    mixed_modes = jnp.stack([mixed_real, mixed_imag], axis=1)
    row_modes = lax.all_gather(mixed_modes, "gx", axis=2, tiled=True).reshape(channels, 2, KX, block_yz)
    back_real = times("cpm,xp->cxm", row_modes[:, 0], row_modes[:, 1], cos_x, -sin_x)
    back_imag = times("cpm,xp->cxm", row_modes[:, 1], row_modes[:, 0], cos_x, sin_x)
    gathered = lax.all_gather(jnp.stack([back_real, back_imag], axis=2), "gy", axis=3, tiled=True)
    back_real = gathered[:, :, 0].reshape(channels, cells_x, KY, KZ)
    back_imag = gathered[:, :, 1].reshape(channels, cells_x, KY, KZ)
    plane_real = times("cxqk,yq->cxyk", back_real, back_imag, cos_y, -sin_y)
    plane_imag = times("cxqk,yq->cxyk", back_imag, back_real, cos_y, sin_y)
    table_back = jnp.concatenate([cos_z.T, -sin_z.T], axis=0)
    planes = jnp.concatenate([plane_real, plane_imag], axis=3)
    return jnp.dot(planes, table_back, precision=PRECISE) * (1.0 / math.sqrt(KX * KY * KZ))


class Plan:
    def __init__(self, feature_shape, count_gx, count_gy):
        self.channels, self.cells_x, self.cells_y, self.length_z = feature_shape
        self.count_gx, self.count_gy = count_gx, count_gy
        self.outer = count_gx // 2
        self.block = KY * KZ // count_gy
        self.part = self.block // 2
        self.per_gx = KX // count_gx
        self.rows = 2 * self.part
        self.pad_k = -(-2 * KZ // 32) * 32
        self.length_x = self.cells_x * count_gx
        self.length_y = self.cells_y * count_gy

    @staticmethod
    def fits(feature_shape, count_gx, count_gy):
        channels, cells_x, cells_y, length_z = feature_shape
        outer = count_gx // 2
        if count_gy != 4 or count_gx % 2 or outer & (outer - 1) or outer > 4:
            return False
        if KX % count_gx or (KY * KZ) % (2 * count_gy) or channels * cells_x != LANES:
            return False
        part = KY * KZ // count_gy // 2
        per = KX // count_gx
        return (
            length_z == LANES
            and cells_y % 4 == 0
            and channels % 16 == 0
            and (2 * part) % 8 == 0
            and 4 * 2 * part % 16 == 0
            and per * part <= LANES
            and 2 * per * channels <= LANES
            and 2 * per * part <= 2 * LANES
            and 2 * part <= LANES
        )

    def table_z(self):
        table = np.zeros((self.pad_k, self.length_z))
        angle = angles_np(np.arange(KZ), np.arange(self.length_z), self.length_z)
        table[:KZ] = np.cos(angle)
        table[KZ : 2 * KZ] = -np.sin(angle)
        return table

    def table_z_group(self):
        group = LANES // self.pad_k
        return np.kron(np.eye(group), self.table_z())

    def table_y(self):
        kept = kept_np(KY, self.length_y)
        tables = []
        for gy in range(self.count_gy):
            places = gy * self.cells_y + np.arange(self.cells_y)
            angle = angles_np(places, kept, self.length_y)
            for pair in range(2):
                order = []
                for core in range(2):
                    for yy in range(2):
                        for xx in range(2):
                            owner = ((gy >> 1) ^ yy) * 2 + ((gy & 1) ^ core)
                            order.append(owner * self.block + (pair ^ xx) * self.part + np.arange(self.part))
                order = np.stack(order)
                turn, line = order // KZ, order % KZ
                cos, sin = np.cos(angle)[:, turn], np.sin(angle)[:, turn]
                same = line[None, :, :, None] == np.arange(KZ)
                table = np.zeros((8, 2, self.part, self.cells_y, self.pad_k))
                cos = np.moveaxis(cos[..., None] * same, 0, 2)
                sin = np.moveaxis(sin[..., None] * same, 0, 2)
                table[:, 0, :, :, :KZ] = cos
                table[:, 0, :, :, KZ : 2 * KZ] = sin
                table[:, 1, :, :, :KZ] = -sin
                table[:, 1, :, :, KZ : 2 * KZ] = cos
                tables.append(table.reshape(8 * self.rows, self.cells_y * self.pad_k))
        return np.stack(tables)

    def table_x(self):
        kept = kept_np(KX, self.length_x)
        tables = []
        for gx in range(self.count_gx):
            outer, pair = gx // 2, gx % 2
            places = np.stack([(gx ^ xx) * self.cells_x + np.arange(self.cells_x) for xx in range(2)])
            modes = np.stack(
                [
                    np.concatenate([(2 * (outer ^ zz) + (pair ^ h)) * self.per_gx + np.arange(self.per_gx) for h in range(2)])
                    for zz in range(self.outer)
                ]
            )
            angle = angles_np(places.reshape(-1), kept[modes.reshape(-1)], self.length_x)
            table = np.zeros((2, self.channels, self.cells_x, 2, self.outer, LANES))
            for at, value in enumerate((np.cos(angle), np.sin(angle))):
                value = value.reshape(2, self.cells_x, self.outer, 2 * self.per_gx)
                for channel in range(self.channels):
                    table[:, channel, :, at, :, channel : 2 * self.per_gx * self.channels : self.channels] = value
            tables.append(table.reshape(2 * LANES, 2 * self.outer * LANES))
        return np.stack(tables)


def forward_kernel(plan, select, feat, tz_h, tz_l, ty_h, ty_l, send, keep0, keep1, keep2, keep3, face0, face1, v_h, v_l):
    table_z = (tz_h[...], tz_l[...])
    pad = plan.pad_k
    for y in range(plan.cells_y):
        plane = halves(feat[pl.ds(y, LANES, stride=plan.cells_y), :])
        high, low = halves(dot3(table_z, plane, NT))
        v_h[y * pad : (y + 1) * pad, :] = high
        v_l[y * pad : (y + 1) * pad, :] = low
    field = (v_h[...], v_l[...])
    rows = plan.rows
    for part in range(4):
        at = slice(part * 2 * rows, (part + 1) * 2 * rows)
        value = dot3((ty_h[0, at, :], ty_l[0, at, :]), field)
        if part < 2:
            (keep0, keep2)[part][...] = value[:rows]
            (keep1, keep3)[part][...] = value[rows:]
        else:
            send[(part - 2) * 2 * rows : (part - 1) * 2 * rows, :] = value
    channels, cells_x, cells_y = plan.channels, plan.cells_x, plan.cells_y
    for x in range(cells_x):
        for face, y in ((face0, 0), (face1, cells_y - 1)):
            face[x] = feat[pl.ds(x * cells_y + y, channels, stride=cells_x * cells_y), :]


def forward_modes(plan, features, select):
    rows = plan.rows
    ty_h, ty_l = table_halves(plan.table_y())
    tz_h, tz_l = table_halves(plan.table_z())
    whole = lambda shape: pl.BlockSpec(shape, lambda i, s: (0,) * len(shape))
    pick = pl.BlockSpec((1,) + ty_h.shape[1:], lambda i, s: (s[0], 0, 0))
    part = jax.ShapeDtypeStruct((rows, LANES), F32)
    face = jax.ShapeDtypeStruct((plan.cells_x, plan.channels, plan.length_z), F32)
    outs = [jax.ShapeDtypeStruct((4 * rows, LANES), F32), part, part, part, part, face, face]
    flat = features.reshape(-1, plan.length_z)
    grid_spec = pltpu.PrefetchScalarGridSpec(
        num_scalar_prefetch=1,
        grid=(1,),
        in_specs=[whole(flat.shape), whole(tz_h.shape), whole(tz_h.shape), pick, pick],
        out_specs=[whole(o.shape) for o in outs],
        scratch_shapes=[pltpu.VMEM((plan.cells_y * plan.pad_k, LANES), BF16)] * 2,
    )
    return kernel_call(functools.partial(forward_kernel, plan), outs, grid_spec=grid_spec)(
        select, flat, tz_h, tz_l, ty_h, ty_l
    )


def swapped(value, rows):
    return jnp.concatenate([value[rows // 2 :], value[: rows // 2]], axis=0)


def x_forward_kernel(plan, select, own, from_x, from_y, from_xy, tx_h, tx_l, *outs):
    rows = plan.rows
    near = own[...] + from_y[...]
    far = from_x[...] + from_xy[...]
    field = halves(jnp.concatenate([near, far], axis=1))
    value = dot3(field, (tx_h[0], tx_l[0]))
    half = plan.outer * LANES
    turned = swapped(value[:, half:], rows)
    sign = jnp.where(lax.broadcasted_iota(jnp.int32, (rows, half), 0) < rows // 2, 1.0, -1.0)
    value = value[:, :half] + sign * turned
    for at, out in enumerate(outs):
        out[...] = value[:, at * LANES : (at + 1) * LANES]


def x_inverse_kernel(plan, select, *refs):
    rows = plan.rows
    parts = refs[: plan.outer]
    tx_h, tx_l, near, far = refs[plan.outer :]
    field = halves(jnp.concatenate([p[...] for p in parts], axis=1))
    half = plan.outer * LANES
    cos = dot3(field, (tx_h[0, :, :half], tx_l[0, :, :half]), NT)
    sin = dot3(field, (tx_h[0, :, half:], tx_l[0, :, half:]), NT)
    sign = jnp.where(lax.broadcasted_iota(jnp.int32, (rows, 2 * LANES), 0) < rows // 2, -1.0, 1.0)
    value = cos + sign * swapped(sin, rows)
    near[...] = value[:, :LANES]
    far[...] = value[:, LANES:]


def x_call(plan, body, parts, tables, count, select):
    whole = lambda shape: pl.BlockSpec(shape, lambda i, s: (0,) * len(shape))
    pick = pl.BlockSpec((1,) + tables[0].shape[1:], lambda i, s: (s[0], 0, 0))
    part = jax.ShapeDtypeStruct((plan.rows, LANES), F32)
    grid_spec = pltpu.PrefetchScalarGridSpec(
        num_scalar_prefetch=1,
        grid=(1,),
        in_specs=[whole(p.shape) for p in parts] + [pick, pick],
        out_specs=[whole(part.shape)] * count,
    )
    return kernel_call(functools.partial(body, plan), [part] * count, grid_spec=grid_spec)(select, *parts, *tables)


def weight_kernel(plan, select, weight, keep, send):
    lane = lax.broadcasted_iota(jnp.int32, keep.shape[1:], 1)
    part, block = plan.part, plan.block
    width = 2 * LANES
    for which in range(2):
        value = weight[which]
        choice = []
        for half in range(2):
            total = jnp.zeros(keep.shape[1:], F32)
            for j in range(plan.per_gx):
                shift = (j * part - j * block - half * part) % width
                moved = value if shift == 0 else pltpu.roll(value, shift, 1)
                inside = (lane >= j * part) & (lane < (j + 1) * part)
                total = jnp.where(inside, moved[:, :LANES], total)
            choice.append(total)
        first = select[0] == 0
        keep[which] = jnp.where(first, choice[0], choice[1])
        send[which] = jnp.where(first, choice[1], choice[0])


def weight_parts(plan, mix_weight, pair):
    square = plan.channels * plan.channels
    flat = mix_weight.reshape(2, square, mix_weight.shape[-1])
    block = (2, square, 2 * LANES)
    out = jax.ShapeDtypeStruct((2, square, LANES), F32)
    grid_spec = pltpu.PrefetchScalarGridSpec(
        num_scalar_prefetch=1,
        grid=(1,),
        in_specs=[pl.BlockSpec(block, lambda i, s: (0, 0, 0))],
        out_specs=[pl.BlockSpec(out.shape, lambda i, s: (0, 0, 0))] * 2,
    )
    return kernel_call(functools.partial(weight_kernel, plan), [out, out], grid_spec=grid_spec)(pair, flat)


def mix_kernel(plan, *refs):
    parts = refs[: plan.outer]
    near, far, out = refs[plan.outer :]
    channels, part, per, rows = plan.channels, plan.part, plan.per_gx, plan.rows
    total = parts[0][...]
    for p in parts[1:]:
        total = total + p[...]
    scale = 1.0 / math.sqrt(plan.length_x * plan.length_y * plan.length_z) / math.sqrt(KX * KY * KZ)
    total = jnp.concatenate([total * scale, jnp.zeros((LANES - rows, LANES), F32)], axis=0).T
    lane = lax.broadcasted_iota(jnp.int32, (channels, LANES), 1)

    def moved(value, shift):
        return value if shift % LANES == 0 else pltpu.roll(value, shift % LANES, 1)

    def collect(half, which):
        value = jnp.zeros((channels, LANES), F32)
        for j in range(per):
            at = (half * per + j) * channels
            piece = moved(total[at : at + channels], (j - which) * part)
            value = jnp.where((lane >= j * part) & (lane < (j + 1) * part), piece, value)
        return value

    blocks = []
    for half, weight in enumerate((near, far)):
        c_real, c_imag = collect(half, 0), collect(half, 1)
        real = jnp.zeros((channels, LANES), F32)
        imag = jnp.zeros((channels, LANES), F32)
        for i in range(channels):
            w_real = weight[0, pl.ds(i, channels, stride=channels), :]
            w_imag = weight[1, pl.ds(i, channels, stride=channels), :]
            a, b = c_real[i : i + 1], c_imag[i : i + 1]
            real = real + (w_real * a - w_imag * b)
            imag = imag + (w_real * b + w_imag * a)
        for j in range(per):
            low = moved(real, -j * part)
            high = moved(imag, part - j * part)
            blocks.append(jnp.where(lane < part, low, jnp.where(lane < 2 * part, high, 0.0)))
    fill = LANES - 2 * per * channels
    if fill:
        blocks.append(jnp.zeros((fill, LANES), F32))
    out[...] = jnp.concatenate(blocks, axis=0).T[:rows]


def mix_modes(plan, parts, near, far):
    return kernel_call(functools.partial(mix_kernel, plan), jax.ShapeDtypeStruct((plan.rows, LANES), F32))(
        *parts, near, far
    )


def final_kernel(plan, select, own, other, conv, tz_h, tz_l, ty_h, ty_l, out):
    rows = plan.rows
    depth = 8 * rows
    pad = -depth % LANES
    parts = [own[...], other[...]]
    if pad:
        parts.append(jnp.zeros((pad, LANES), F32))
    field = jnp.concatenate(parts, axis=0)
    columns = jnp.concatenate([field[at : at + LANES].T for at in range(0, depth + pad, LANES)], axis=1)
    modes = halves(columns[:, :depth])
    planes = halves(dot3(modes, (ty_h[0], ty_l[0])))
    table_z = (tz_h[...], tz_l[...])
    group = LANES // plan.pad_k
    for g in range(plan.cells_y // group):
        at = slice(g * LANES, (g + 1) * LANES)
        value = dot3((planes[0][:, at], planes[1][:, at]), table_z)
        for k in range(group):
            index = pl.ds(g * group + k, LANES, stride=plan.cells_y)
            layer = conv[index, :] + value[:, k * LANES : (k + 1) * LANES]
            out[index, :] = layer * 0.5 * (1.0 + lax.erf(layer * math.sqrt(0.5)))


def final_layer(plan, own, other, conv, select):
    ty_h, ty_l = table_halves(plan.table_y())
    tz_h, tz_l = table_halves(plan.table_z_group())
    whole = lambda shape: pl.BlockSpec(shape, lambda i, s: (0,) * len(shape))
    pick = pl.BlockSpec((1,) + ty_h.shape[1:], lambda i, s: (s[0], 0, 0))
    flat = conv.reshape(-1, plan.length_z)
    grid_spec = pltpu.PrefetchScalarGridSpec(
        num_scalar_prefetch=1,
        grid=(1,),
        in_specs=[whole(own.shape), whole(other.shape), whole(flat.shape), whole(tz_h.shape), whole(tz_h.shape), pick, pick],
        out_specs=whole(flat.shape),
    )
    out = kernel_call(functools.partial(final_kernel, plan), jax.ShapeDtypeStruct(flat.shape, F32), grid_spec=grid_spec)(
        select, own, other, flat, tz_h, tz_l, ty_h, ty_l
    )
    return out.reshape(conv.shape)


def swap(plan, value, outer=0, pair=0, yy=0, core=0):
    perm = []
    for gx in range(plan.count_gx):
        for gy in range(plan.count_gy):
            to_gx = gx ^ (outer * 2 + pair)
            to_gy = gy ^ (yy * 2 + core)
            perm.append((gx * plan.count_gy + gy, to_gx * plan.count_gy + to_gy))
    return lax.ppermute(value, ("gx", "gy"), perm)


def layer_paired(plan, features, conv_weight, mix_weight):
    rows = plan.rows
    at_gx, at_gy = lax.axis_index("gx"), lax.axis_index("gy")
    pair = at_gx % 2
    as_scalar = lambda v: v.astype(jnp.int32).reshape(1)
    select_y = as_scalar(at_gy * 2 + pair)
    select_x = as_scalar(at_gx)
    cells_x, cells_y = features.shape[1:3]

    x_low = ring(features[:, cells_x - 1 :], "gx", 1)
    x_high = ring(features[:, :1], "gx", -1)
    send, keep0, keep1, keep2, keep3, face0, face1 = forward_modes(plan, features, select_y)
    near, away = weight_parts(plan, mix_weight, as_scalar(pair))
    far = swap(plan, away, pair=1)
    bands = band_weights(conv_weight, cells_y)
    got = swap(plan, send, core=1)
    sums = [k + got[s * rows : (s + 1) * rows] for s, k in enumerate((keep0, keep1, keep2, keep3))]
    from_x = swap(plan, sums[1], pair=1)
    from_y = swap(plan, sums[2], yy=1)
    from_xy = swap(plan, sums[3], pair=1, yy=1)
    tables = table_halves(plan.table_x())
    chunks = x_call(plan, x_forward_kernel, [sums[0], from_x, from_y, from_xy], tables, plan.outer, select_x)
    parts = [chunks[0]] + [swap(plan, chunks[s], outer=s) for s in range(1, plan.outer)]
    mixed = mix_modes(plan, parts, near, far)
    parts = [mixed] + [swap(plan, mixed, outer=s) for s in range(1, plan.outer)]
    mine, theirs = x_call(plan, x_inverse_kernel, parts, tables, 2, select_x)
    from_x = swap(plan, theirs, pair=1)
    from_y = swap(plan, mine, yy=1)
    from_xy = swap(plan, theirs, pair=1, yy=1)
    own = jnp.concatenate([mine, from_x, from_y, from_xy], axis=0)
    other = swap(plan, own, core=1)

    def face(low, middle, high, y):
        return jnp.concatenate([low[:, :, y].transpose(1, 0, 2), middle, high[:, :, y].transpose(1, 0, 2)], axis=0)

    y_low = ring(face(x_low, face1, x_high, cells_y - 1), "gy", 1)
    y_high = ring(face(x_low, face0, x_high, 0), "gy", -1)
    conv = conv_bricks(features, x_low, x_high, y_low, y_high, bands)
    return final_layer(plan, own, other, conv, select_y)


def layer_any(features, conv_weight, mix_weight):
    bands = band_weights(conv_weight, features.shape[2])
    conv = conv_bricks(features, *halos(features), bands)
    return jax.nn.gelu(conv + spectral_any(features, mix_weight), approximate=False)


def shards(features, conv_weight, mix_weight):
    counts = lax.axis_size("gx"), lax.axis_size("gy")
    if Plan.fits(features.shape, *counts):
        return layer_paired(Plan(features.shape, *counts), features, conv_weight, mix_weight)
    return layer_any(features, conv_weight, mix_weight)


def solution(mesh):
    in_specs = (P(None, "gx", "gy", None), P(), P(None, None, None, "gy", "gx"))
    out_specs = P(None, "gx", "gy", None)
    return jax.shard_map(shards, mesh=mesh, in_specs=in_specs, out_specs=out_specs, check_vma=False)
```

```python
import functools
import math

import jax
import jax.numpy as jnp
import ml_dtypes
import numpy as np
from jax import lax
from jax.experimental import pallas as pl
from jax.experimental.pallas import tpu as pltpu
from jax.sharding import PartitionSpec as P

KX = 24
KY = 24
KZ = 12
LANES = 128
F32 = jnp.float32
BF16 = jnp.bfloat16
PRECISE = lax.Precision.HIGHEST
VMEM_LIMIT = 24 * 1024 * 1024
NN = (((1,), (0,)), ((), ()))
NT = (((1,), (1,)), ((), ()))


def kernel_call(body, out_shape, scratch=(), grid_spec=None, **kw):
    params = pltpu.CompilerParams(vmem_limit_bytes=VMEM_LIMIT)
    if grid_spec is not None:
        kw["grid_spec"] = grid_spec
    else:
        kw["scratch_shapes"] = list(scratch)
    return pl.pallas_call(body, out_shape=out_shape, compiler_params=params, **kw)


def halves(value):
    high = value.astype(BF16)
    return high, (value - high.astype(F32)).astype(BF16)


def dot(a, b, dims=NN):
    return lax.dot_general(a, b, dims, preferred_element_type=F32)


def dot3(a, b, dims=NN):
    return dot(a[0], b[0], dims) + (dot(a[0], b[1], dims) + dot(a[1], b[0], dims))


def table_halves(table):
    table = np.asarray(table, np.float64)
    high = table.astype(ml_dtypes.bfloat16)
    low = (table - high.astype(np.float64)).astype(ml_dtypes.bfloat16)
    return high, low


def triple(parts, axis, twice_high_around):
    high, low = parts
    return jnp.concatenate([high, low, high] if twice_high_around else [high, high, low], axis=axis)


def kept_np(amount, length):
    index = np.arange(amount)
    return np.where(index < amount // 2, index, length - amount + index)


def angles_np(positions, frequencies, length):
    return 2.0 * np.pi * ((positions[:, None] * frequencies[None, :]) % length) / length


def split_kernel(feat, high, low):
    channels, cells_x, cells_y, length_z = feat.shape
    for x in range(cells_x):
        for y in range(cells_y):
            high[y, x], low[y, x] = halves(feat[:, x, y, :])


def conv_kernel(first, rows_y, count_gy, place, own_h, own_l, near_x, far_x, near_y, far_y, weight, after, out, token, edge_h, edge_l, rim_h, rim_l):
    cells_y, cells_x, channels, length_z = own_h.shape
    count = out.shape[0]
    span = rows_y + 2
    depth = 3 * span * channels
    even_x, even_y = place[0] // count_gy % 2 == 0, place[0] % count_gy % 2 == 0
    column, row = (cells_y + 2) * channels, cells_x * channels

    def tail(ref, size, at):
        return ref[ref.shape[0] - size + at : ref.shape[0] - size + at + channels, :]

    def pick(side, even, near, far, size, at):
        near, far = (tail(ref, size, at * channels) for ref in (near, far))
        return halves(jnp.where(even, near, far) if side else jnp.where(even, far, near))

    for side in range(2):
        if (0, cells_x + 1)[side] in range(first, first + count + 2):
            for y in range(cells_y):
                edge_h[side, y + 1], edge_l[side, y + 1] = pick(side, even_x, near_x, far_x, column, y)
            corners = [
                jnp.where(even_x == bool(side), *(tail(ref, column, (cells_y + n) * channels) for ref in (near_x, far_x)))
                for n in range(2)
            ]
            for up in range(2):
                value = jnp.where(even_y == bool(up), *corners)
                edge_h[side, up * (cells_y + 1)], edge_l[side, up * (cells_y + 1)] = halves(value)
        for x in range(max(first - 1, 0), min(first + count + 1, cells_x)):
            rim_h[side, x], rim_l[side, x] = pick(side, even_y, near_y, far_y, row, x)

    def cell(which, x, y):
        own, edge, rim = ((own_h, edge_h, rim_h), (own_l, edge_l, rim_l))[which]
        if x in (0, cells_x + 1):
            return edge[0 if x == 0 else 1, y]
        if y in (0, cells_y + 1):
            return rim[0 if y == 0 else 1, x - 1]
        return own[y - 1, x - 1]

    taps = halves(weight[...])
    tap = lax.broadcasted_iota(jnp.int32, (weight.shape[1], depth), 0)
    at = lax.broadcasted_iota(jnp.int32, (weight.shape[1], depth), 1)
    tap_a, tap_b, tap_i = tap // (3 * channels), tap // channels % 3, tap % channels
    at_a, at_y, at_i = at // (span * channels), at // channels % span, at % channels
    bands = [[], []]
    for y in range(rows_y):
        match = (tap_a == at_a) & (tap_b + y == at_y) & (tap_i == at_i)
        match = jnp.where(match, 1.0, 0.0).astype(BF16)
        for which in range(2):
            bands[which].append(dot(taps[which], match).astype(BF16))
    bands = [jnp.concatenate(b, axis=0) for b in bands]
    for x in range(0, count, 2):
        for y in range(0, cells_y, rows_y):
            field = []
            for which in range(2):
                columns = []
                for p in range(2):
                    cells = [cell(which, first + x + p + a, y + k) for a in range(3) for k in range(span)]
                    columns.append(jnp.concatenate(cells, axis=0))
                field.append(jnp.concatenate(columns, axis=1))
            value = dot3(bands, field)
            for k in range(rows_y):
                for p in range(2):
                    total = None
                    for c in range(3):
                        row = (k * 3 + c) * channels
                        piece = value[row : row + channels, p * length_z : (p + 1) * length_z]
                        if c != 1:
                            piece = pltpu.roll(piece, (1 - c) % length_z, 1)
                        total = piece if total is None else total + piece
                    out[x + p, y + k] = total
    token[...] = jnp.zeros(token.shape, F32)


def conv_taps(conv_weight):
    channels = conv_weight.shape[1]
    taps = conv_weight.reshape(3, 3, 3, channels, channels).transpose(2, 3, 0, 1, 4)
    return taps.reshape(3 * channels, 9 * channels)


def specs(count, first=None):
    vmem = pl.BlockSpec(memory_space=pltpu.VMEM)
    return [pl.BlockSpec(memory_space=pltpu.SMEM)] + [vmem] * count


def conv_bricks(place, own, near_x, far_x, near_y, far_y, taps, after, first, count):
    cells_y, cells_x, channels, length_z = own[0].shape
    return kernel_call(
        functools.partial(conv_kernel, first, 2, lax.axis_size("gy")),
        [jax.ShapeDtypeStruct((count, cells_y, channels, length_z), F32), jax.ShapeDtypeStruct((8, LANES), F32)],
        [pltpu.VMEM((2, cells_y + 2, channels, length_z), BF16)] * 2 + [pltpu.VMEM((2, cells_x, channels, length_z), BF16)] * 2,
        in_specs=specs(8),
    )(place, *own, near_x, far_x, near_y, far_y, taps, after)


def ring(value, axis, step):
    size = lax.axis_size(axis)
    return lax.ppermute(value, axis, [(i, (i + step) % size) for i in range(size)])


def halos(features):
    channels, cells_x, cells_y, length_z = features.shape
    flat = lambda v: v.transpose(1, 0, 2).reshape(-1, length_z)
    low_y = ring(features[:, :, cells_y - 1], "gy", 1)
    high_y = ring(features[:, :, 0], "gy", -1)

    def face(x):
        return jnp.concatenate([features[:, x], high_y[:, x][:, None], low_y[:, x][:, None]], axis=1)

    low_x = ring(face(cells_x - 1), "gx", 1)
    high_x = ring(face(0), "gx", -1)
    return flat(high_x), flat(low_x), flat(high_y), flat(low_y)


def angle_tables(positions, frequencies, length):
    product = positions[:, None] * frequencies[None, :] % length
    angles = product.astype(jnp.float32) * (2.0 * math.pi / length)
    return (jnp.cos(angles), jnp.sin(angles))


def kept_frequencies(amount, length):
    index = jnp.arange(amount, dtype=jnp.int32)
    return jnp.where(index < amount // 2, index, length - amount + index)


def times(form, a, b, c, d):
    one = functools.partial(jnp.einsum, form, precision=PRECISE)
    return one(a, c) + one(b, d)


def spectral_any(features, mix_weight):
    channels, cells_x, cells_y, length_z = features.shape
    count_gx = lax.axis_size("gx")
    count_gy = lax.axis_size("gy")
    length_x = cells_x * count_gx
    length_y = cells_y * count_gy
    block_yz = KY * KZ // count_gy
    cos_z, sin_z = angle_tables(jnp.arange(length_z, dtype=jnp.int32), jnp.arange(KZ, dtype=jnp.int32), length_z)
    y_places = lax.axis_index("gy") * cells_y + jnp.arange(cells_y, dtype=jnp.int32)
    x_places = lax.axis_index("gx") * cells_x + jnp.arange(cells_x, dtype=jnp.int32)
    cos_y, sin_y = angle_tables(y_places, kept_frequencies(KY, length_y), length_y)
    cos_x, sin_x = angle_tables(x_places, kept_frequencies(KX, length_x), length_x)
    along_z = jnp.dot(features, jnp.concatenate([cos_z, -sin_z], axis=1), precision=PRECISE)
    z_real = along_z[..., :KZ]
    z_imag = along_z[..., KZ:]
    y_real = times("cxyk,yq->cxqk", z_real, z_imag, cos_y, sin_y)
    y_imag = times("cxyk,yq->cxqk", z_imag, z_real, cos_y, -sin_y)
    partial_value = jnp.stack([y_real, y_imag], axis=2).reshape(channels, cells_x, 2, KY * KZ)
    y_share = lax.psum_scatter(partial_value, "gy", scatter_dimension=3, tiled=True)
    x_real = times("cxm,xp->cpm", y_share[:, :, 0], y_share[:, :, 1], cos_x, sin_x)
    x_imag = times("cxm,xp->cpm", y_share[:, :, 1], y_share[:, :, 0], cos_x, -sin_x)
    x_partial = jnp.stack([x_real, x_imag], axis=1).reshape(channels, 2, KX * block_yz)
    owned_modes = lax.psum_scatter(x_partial, "gx", scatter_dimension=2, tiled=True)
    owned_modes = owned_modes * (1.0 / math.sqrt(length_x * length_y * length_z))
    coef_real = owned_modes[:, 0]
    coef_imag = owned_modes[:, 1]
    weight_real = mix_weight[0, :, :, 0, :]
    weight_imag = mix_weight[1, :, :, 0, :]
    mixed_real = times("oim,im->om", weight_real, weight_imag, coef_real, -coef_imag)
    mixed_imag = times("oim,im->om", weight_real, weight_imag, coef_imag, coef_real)
    mixed_modes = jnp.stack([mixed_real, mixed_imag], axis=1)
    row_modes = lax.all_gather(mixed_modes, "gx", axis=2, tiled=True).reshape(channels, 2, KX, block_yz)
    back_real = times("cpm,xp->cxm", row_modes[:, 0], row_modes[:, 1], cos_x, -sin_x)
    back_imag = times("cpm,xp->cxm", row_modes[:, 1], row_modes[:, 0], cos_x, sin_x)
    gathered = lax.all_gather(jnp.stack([back_real, back_imag], axis=2), "gy", axis=3, tiled=True)
    back_real = gathered[:, :, 0].reshape(channels, cells_x, KY, KZ)
    back_imag = gathered[:, :, 1].reshape(channels, cells_x, KY, KZ)
    plane_real = times("cxqk,yq->cxyk", back_real, back_imag, cos_y, -sin_y)
    plane_imag = times("cxqk,yq->cxyk", back_imag, back_real, cos_y, sin_y)
    table_back = jnp.concatenate([cos_z.T, -sin_z.T], axis=0)
    planes = jnp.concatenate([plane_real, plane_imag], axis=3)
    return jnp.dot(planes, table_back, precision=PRECISE) * (1.0 / math.sqrt(KX * KY * KZ))


class Plan:
    def __init__(self, feature_shape, count_gx, count_gy):
        self.channels, self.cells_x, self.cells_y, self.length_z = feature_shape
        self.count_gx, self.count_gy = count_gx, count_gy
        self.outer = count_gx // 2
        self.block = KY * KZ // count_gy
        self.part = self.block // 2
        self.per_gx = KX // count_gx
        self.rows = 2 * self.part
        self.pad_k = -(-KZ // 8) * 8
        self.pad_z = 2 * self.pad_k
        self.turns = self.part // KZ
        self.length_x = self.cells_x * count_gx
        self.length_y = self.cells_y * count_gy

    def spot(self, place):
        return place[0] // self.count_gy, place[0] % self.count_gy

    @staticmethod
    def fits(feature_shape, count_gx, count_gy):
        channels, cells_x, cells_y, length_z = feature_shape
        outer = count_gx // 2
        if count_gy != 4 or count_gx % 2 or outer & (outer - 1) or outer > 4:
            return False
        if KX % count_gx or (KY * KZ) % (2 * count_gy) or channels * cells_x != LANES:
            return False
        part = KY * KZ // count_gy // 2
        per = KX // count_gx
        return (
            length_z == LANES
            and cells_y % (LANES // (2 * (-(-KZ // 8) * 8))) == 0
            and channels % 16 == 0
            and (2 * part) % 8 == 0
            and 4 * 2 * part % 16 == 0
            and part % KZ == 0
            and per * part <= LANES
            and 2 * per * channels <= LANES
            and 2 * per * part <= 2 * LANES
            and 2 * part <= LANES
        )

    def table_z(self):
        table = np.zeros((2, self.pad_k, self.length_z))
        angle = angles_np(np.arange(KZ), np.arange(self.length_z), self.length_z)
        table[0, :KZ] = np.cos(angle)
        table[1, :KZ] = -np.sin(angle)
        return table.reshape(self.pad_z, self.length_z)

    def table_z_group(self):
        return np.kron(np.eye(LANES // self.pad_z), self.table_z())

    def table_y(self):
        kept = kept_np(KY, self.length_y)
        tables = []
        for gy in range(self.count_gy):
            places = gy * self.cells_y + np.arange(self.cells_y)
            angle = angles_np(kept, places, self.length_y)
            for pair in range(2):
                order = []
                for core in range(2):
                    for yy in range(2):
                        for xx in range(2):
                            owner = ((gy >> 1) ^ yy) * 2 + ((gy & 1) ^ core)
                            order.append((owner * 2 + (pair ^ xx)) * self.turns + np.arange(self.turns))
                cos, sin = np.cos(angle)[np.stack(order)], np.sin(angle)[np.stack(order)]
                table = np.zeros((8, 2, self.turns, self.cells_y, 2))
                table[:, 0, :, :, 0] = cos
                table[:, 0, :, :, 1] = sin
                table[:, 1, :, :, 0] = -sin
                table[:, 1, :, :, 1] = cos
                tables.append(table.reshape(16 * self.turns, self.cells_y * 2))
        return np.stack(tables)

    def trig_z(self):
        shape = (self.pad_z, self.length_z)
        row, z = (lax.broadcasted_iota(jnp.int32, shape, n) for n in range(2))
        k, imag = row % self.pad_k, row // self.pad_k
        turn = k * z % self.length_z
        turn = jnp.where(imag == 1, turn + self.length_z // 4, turn) % self.length_z
        value = jnp.cos(turn.astype(F32) * (2.0 * math.pi / self.length_z))
        return jnp.where(k < KZ, value, 0.0)

    def trig_y(self, gx, gy):
        shape = (16 * self.turns, 2 * self.cells_y)
        row, col = (lax.broadcasted_iota(jnp.int32, shape, n) for n in range(2))
        offset = row // (2 * self.turns)
        y_bit = (gy // 2 + offset // 2) % 2
        owner = (y_bit * 2 + (gy + offset // 4) % 2) * 2 + (gx + offset) % 2
        mode = owner * self.turns + row % self.turns
        kept = jnp.where(mode < KY // 2, mode, self.length_y - KY + mode)
        turn = kept * (gy * self.cells_y + col // 2) % self.length_y
        quarter = self.length_y // 4
        out_part, in_part = row // self.turns % 2, col % 2
        shift = jnp.where(out_part == in_part, 0, jnp.where(out_part == 0, 3 * quarter, quarter))
        return jnp.cos(((turn + shift) % self.length_y).astype(F32) * (2.0 * math.pi / self.length_y))

    def table_x(self):
        kept = kept_np(KX, self.length_x)
        tables = []
        for gx in range(self.count_gx):
            outer, pair = gx // 2, gx % 2
            places = np.stack([(gx ^ xx) * self.cells_x + np.arange(self.cells_x) for xx in range(2)]).reshape(-1)
            modes = np.stack([(2 * (outer ^ zz) + (pair ^ h)) * self.per_gx + np.arange(self.per_gx) for zz in range(self.outer) for h in range(2)])
            angle = angles_np(kept[modes.reshape(-1)], places, self.length_x)
            tables.append(np.concatenate([np.cos(angle), np.sin(angle)], axis=1))
        return np.stack(tables)


def tripled_table(table):
    high, low = table_halves(table)
    return np.concatenate([high, high, low], axis=-1)


def forward_kernel(plan, place, feat, keep, send, own_h, own_l, near_x, far_x, field):
    channels, cells_x, cells_y = plan.channels, plan.cells_x, plan.cells_y
    gx, gy = plan.spot(place)
    even_x, even_y = gx % 2 == 0, gy % 2 == 0
    pad = plan.pad_z
    z_table = triple(halves(plan.trig_z()), 1, False)
    ends = []
    for y in range(cells_y):
        plane = [feat[pl.ds(x * cells_y + y, channels, stride=cells_x * cells_y), :] for x in range(cells_x)]
        near_x[y] = jnp.where(even_x, plane[-1], plane[0])
        far_x[y] = jnp.where(even_x, plane[0], plane[-1])
        plane = jnp.concatenate(plane, axis=0)
        if y in (0, cells_y - 1):
            ends.append(plane)
        high, low = halves(plane)
        own_h[y] = high.reshape(cells_x, channels, -1)
        own_l[y] = low.reshape(cells_x, channels, -1)
        field[y * pad : (y + 1) * pad, :] = dot(z_table, triple((high, low), 1, True), NT)
    y_table = triple(halves(plan.trig_y(gx, gy)), 1, False)
    half = 8 * plan.turns
    for k in range(KZ):
        value = halves(field[pl.ds(k, 2 * cells_y, stride=plan.pad_k), :])
        value = dot(y_table, triple(value, 0, True))
        keep[pl.ds(k, half, stride=KZ), :] = value[:half]
        send[pl.ds(k, half, stride=KZ), :] = value[half:]
    start = half * KZ
    send[start : start + LANES, :] = jnp.where(even_y, ends[0], ends[1])
    send[start + LANES :, :] = jnp.where(even_y, ends[1], ends[0])


def forward_modes(plan, place, features):
    half, length_z = 4 * plan.rows, plan.length_z
    own = jax.ShapeDtypeStruct((plan.cells_y, plan.cells_x, plan.channels, length_z), BF16)
    face = jax.ShapeDtypeStruct((plan.cells_y, plan.channels, length_z), F32)
    shape = lambda *s: jax.ShapeDtypeStruct(s, F32)
    return kernel_call(
        functools.partial(forward_kernel, plan),
        [shape(half, LANES), shape(half + 2 * LANES, LANES), own, own, face, face],
        [pltpu.VMEM((plan.cells_y * plan.pad_z, LANES), F32)],
        in_specs=specs(1),
    )(place, features.reshape(-1, length_z))


def turned(value, part, sign):
    lane = lax.broadcasted_iota(jnp.int32, value.shape, 1)
    low = pltpu.roll(value, LANES - part, 1)
    high = pltpu.roll(value, part, 1)
    return jnp.where(lane < part, sign * low, -sign * high)


def square_turned(value):
    return jnp.concatenate([value, jnp.zeros((LANES - value.shape[0], LANES), F32)], axis=0).T


def x_forward_kernel(plan, place, own, from_x, from_y, from_xy, table, *refs):
    outs = refs[: plan.outer]
    straight, crossed, found = refs[plan.outer :]
    rows, channels, per = plan.rows, plan.channels, 2 * plan.per_gx
    near = own[...] + from_y[:rows, :]
    far = from_x[...] + from_xy[...]
    for at, value in enumerate((near, far)):
        value = square_turned(value)
        straight[at * LANES : (at + 1) * LANES, :] = value
        crossed[at * LANES : (at + 1) * LANES, :] = turned(value, plan.part, 1.0)
    factor = table[plan.spot(place)[0]]
    for c in range(channels):
        index = pl.ds(c, 2 * plan.cells_x, stride=channels)
        value = halves(jnp.concatenate([straight[index, :], crossed[index, :]], axis=0))
        found[pl.ds(c, plan.outer * per, stride=channels), :] = dot(factor, triple(value, 0, True))
    for at, out in enumerate(outs):
        size = per * channels
        out[...] = square_turned(found[at * size : (at + 1) * size, :])[:rows]


def x_inverse_kernel(plan, place, *refs):
    parts = refs[: plan.outer]
    table, near, far, straight, crossed, found = refs[plan.outer :]
    rows, channels, per = plan.rows, plan.channels, 2 * plan.per_gx
    size = per * channels
    for at, part in enumerate(parts):
        value = square_turned(part[...])[:size]
        straight[at * size : (at + 1) * size, :] = value
        crossed[at * size : (at + 1) * size, :] = turned(value, plan.part, -1.0)
    factor = table[plan.spot(place)[0]]
    for c in range(channels):
        index = pl.ds(c, plan.outer * per, stride=channels)
        value = halves(jnp.concatenate([straight[index, :], crossed[index, :]], axis=0))
        found[pl.ds(c, 2 * plan.cells_x, stride=channels), :] = dot(factor, triple(value, 0, True))
    for at, out in enumerate((near, far)):
        out[...] = found[at * LANES : (at + 1) * LANES, :].T[:rows]


def x_forward(plan, place, parts):
    part = jax.ShapeDtypeStruct((plan.rows, LANES), F32)
    size = plan.outer * 2 * plan.per_gx * plan.channels
    scratch = [pltpu.VMEM((n, LANES), F32) for n in (2 * LANES, 2 * LANES, size)]
    body = functools.partial(x_forward_kernel, plan)
    table = tripled_table(plan.table_x())
    return kernel_call(body, [part] * plan.outer, scratch, in_specs=specs(5))(place, *parts, table)


def x_inverse(plan, place, parts):
    part = jax.ShapeDtypeStruct((plan.rows, LANES), F32)
    size = plan.outer * 2 * plan.per_gx * plan.channels
    scratch = [pltpu.VMEM((n, LANES), F32) for n in (size, size, 2 * LANES)]
    body = functools.partial(x_inverse_kernel, plan)
    table = plan.table_x()
    half = table.shape[2] // 2
    table = tripled_table(np.concatenate([np.swapaxes(t, 1, 2) for t in (table[:, :, :half], table[:, :, half:])], axis=2))
    return kernel_call(body, [part] * 2, scratch, in_specs=specs(plan.outer + 1))(place, *parts, table)


def weight_kernel(plan, place, weight, keep, send, flat, sem):
    copy = pltpu.make_async_copy(weight.at[:, :, 0, :], flat, sem)
    copy.start()
    copy.wait()
    part, block = plan.part, plan.block
    square = plan.channels * plan.channels
    lane = lax.broadcasted_iota(jnp.int32, (square, LANES), 1)
    width = 2 * LANES
    held = flat.shape[2]
    even = plan.spot(place)[0] % 2 == 0
    for which in range(2):
        high = jnp.concatenate([flat[which, :, LANES:], jnp.zeros((square, width - held), F32)], axis=1)
        value = jnp.concatenate([flat[which, :, :LANES], high], axis=1)
        choice = []
        for half in range(2):
            total = jnp.zeros((square, LANES), F32)
            for j in range(plan.per_gx):
                shift = (j * part - j * block - half * part) % width
                moved = value if shift == 0 else pltpu.roll(value, shift, 1)
                inside = (lane >= j * part) & (lane < (j + 1) * part)
                total = jnp.where(inside, moved[:, :LANES], total)
            choice.append(total)
        at = slice(which * square, (which + 1) * square)
        keep[at, :] = jnp.where(even, choice[0], choice[1])
        send[at, :] = jnp.where(even, choice[1], choice[0])


def weight_parts(plan, place, mix_weight):
    square = plan.channels * plan.channels
    modes = mix_weight.shape[-1]
    out = jax.ShapeDtypeStruct((2 * square, LANES), F32)
    return kernel_call(
        functools.partial(weight_kernel, plan),
        [out, out],
        [pltpu.VMEM((2, square, modes), F32), pltpu.SemaphoreType.DMA],
        in_specs=specs(1),
    )(place, mix_weight.reshape(2, square, 1, modes))


def faces_kernel(plan, place, near_x, far_x, near_y, far_y, after, to_near, to_far):
    channels, cells_x, cells_y = plan.channels, plan.cells_x, plan.cells_y
    even = plan.spot(place)[0] % 2 == 0
    last = cells_x - 1
    for out, face, x in ((to_near, near_x, jnp.where(even, last, 0)), (to_far, far_x, jnp.where(even, 0, last))):
        for y in range(cells_y):
            out[y * channels : (y + 1) * channels, :] = face[y]
        for n, ref in enumerate((near_y, far_y)):
            at = pl.multiple_of(ref.shape[0] - LANES + x * channels, channels)
            start = (cells_y + n) * channels
            out[start : start + channels, :] = ref[pl.ds(at, channels), :]


def faces(plan, place, near_x, far_x, near_y, far_y, after):
    out = jax.ShapeDtypeStruct(((plan.cells_y + 2) * plan.channels, LANES), F32)
    return kernel_call(functools.partial(faces_kernel, plan), [out, out], in_specs=specs(5))(
        place, near_x, far_x, near_y, far_y, after
    )


def mix_kernel(plan, *refs):
    parts = refs[: plan.outer]
    near, far, out = refs[plan.outer :]
    channels, part, per, rows = plan.channels, plan.part, plan.per_gx, plan.rows
    total = parts[0][...]
    for p in parts[1:]:
        total = total + p[...]
    scale = 1.0 / math.sqrt(plan.length_x * plan.length_y * plan.length_z) / math.sqrt(KX * KY * KZ)
    total = jnp.concatenate([total * scale, jnp.zeros((LANES - rows, LANES), F32)], axis=0).T
    lane = lax.broadcasted_iota(jnp.int32, (channels, LANES), 1)

    def moved(value, shift):
        return value if shift % LANES == 0 else pltpu.roll(value, shift % LANES, 1)

    def collect(half, which):
        value = jnp.zeros((channels, LANES), F32)
        for j in range(per):
            at = (half * per + j) * channels
            piece = moved(total[at : at + channels], (j - which) * part)
            value = jnp.where((lane >= j * part) & (lane < (j + 1) * part), piece, value)
        return value

    blocks = []
    for half, weight in enumerate((near, far)):
        c_real, c_imag = collect(half, 0), collect(half, 1)
        real = jnp.zeros((channels, LANES), F32)
        imag = jnp.zeros((channels, LANES), F32)
        for i in range(channels):
            w_real = weight[pl.ds(i, channels, stride=channels), :]
            w_imag = weight[pl.ds(channels * channels + i, channels, stride=channels), :]
            a, b = c_real[i : i + 1], c_imag[i : i + 1]
            real = real + (w_real * a - w_imag * b)
            imag = imag + (w_real * b + w_imag * a)
        for j in range(per):
            low = moved(real, -j * part)
            high = moved(imag, part - j * part)
            blocks.append(jnp.where(lane < part, low, jnp.where(lane < 2 * part, high, 0.0)))
    fill = LANES - 2 * per * channels
    if fill:
        blocks.append(jnp.zeros((fill, LANES), F32))
    out[...] = jnp.concatenate(blocks, axis=0).T[:rows]


def mix_modes(plan, parts, near, far):
    return kernel_call(functools.partial(mix_kernel, plan), jax.ShapeDtypeStruct((plan.rows, LANES), F32))(
        *parts, near, far
    )


def final_kernel(plan, place, own, other, conv_a, conv_b, table_z, table_y, out, field):
    channels, cells_x, cells_y = plan.channels, plan.cells_x, plan.cells_y
    gx, gy = plan.spot(place)
    y_table = table_y[gy * 2 + gx % 2]
    half = 8 * plan.turns
    field[...] = jnp.zeros(field.shape, F32)
    for k in range(KZ):
        parts = [ref[pl.ds(k, half, stride=KZ), :] for ref in (own, other)]
        value = halves(jnp.concatenate(parts, axis=0))
        field[pl.ds(k, 2 * cells_y, stride=plan.pad_k), :] = dot(y_table, triple(value, 0, True))
    z_table = table_z[...]
    group = LANES // plan.pad_z
    for g in range(cells_y // group):
        planes = halves(field[g * LANES : (g + 1) * LANES, :].T)
        value = dot(triple(planes, 1, False), z_table)
        for k in range(group):
            y = g * group + k
            conv = [ref[x, y] for ref in (conv_a, conv_b) for x in range(ref.shape[0])]
            layer = jnp.concatenate(conv, axis=0) + value[:, k * LANES : (k + 1) * LANES]
            layer = layer * 0.5 * (1.0 + lax.erf(layer * math.sqrt(0.5)))
            for x in range(cells_x):
                out[pl.ds(x * cells_y + y, channels, stride=cells_x * cells_y), :] = layer[x * channels : (x + 1) * channels]


def final_layer(plan, place, own, other, convs):
    table_y = tripled_table(np.swapaxes(plan.table_y(), 1, 2))
    high, low = table_halves(plan.table_z_group())
    table_z = np.concatenate([high, low, high], axis=0)
    shape = (plan.channels, plan.cells_x, plan.cells_y, plan.length_z)
    flat = (plan.channels * plan.cells_x * plan.cells_y, plan.length_z)
    return kernel_call(
        functools.partial(final_kernel, plan),
        jax.ShapeDtypeStruct(flat, F32),
        [pltpu.VMEM((plan.cells_y * plan.pad_z, LANES), F32)],
        in_specs=specs(6),
    )(place, own, other, *convs, table_z, table_y).reshape(shape)


def swap(plan, value, outer=0, pair=0, yy=0, core=0):
    perm = []
    for gx in range(plan.count_gx):
        for gy in range(plan.count_gy):
            to_gx = gx ^ (outer * 2 + pair)
            to_gy = gy ^ (yy * 2 + core)
            perm.append((gx * plan.count_gy + gy, to_gx * plan.count_gy + to_gy))
    return lax.ppermute(value, ("gx", "gy"), perm)


def next_pair(value, axis):
    size = lax.axis_size(axis)
    return lax.ppermute(value, axis, [(i, (i + (1 if i % 2 else -1)) % size) for i in range(size)])


def after(value, *others):
    zero = sum(jnp.minimum(jnp.abs(other[:1]), 0.0) for other in others)
    return value + zero


def layer_paired(plan, features, conv_weight, mix_weight):
    rows = plan.rows
    place = (lax.axis_index("gx") * plan.count_gy + lax.axis_index("gy")).astype(jnp.int32).reshape(1)
    cells_x = features.shape[1]

    keep, send, own_h, own_l, near_x, far_x = forward_modes(plan, place, features)
    weight, away = weight_parts(plan, place, mix_weight)
    near_y = swap(plan, send, core=1)
    sums = [keep[s * rows : (s + 1) * rows] + near_y[s * rows : (s + 1) * rows] for s in range(4)]
    passed = near_y[4 * rows : 4 * rows + LANES]
    far_y = swap(plan, jnp.concatenate([sums[2], passed], axis=0), yy=1)
    from_x = swap(plan, sums[1], pair=1)
    from_xy = swap(plan, sums[3], pair=1, yy=1)
    away = after(away, from_x, far_y, from_xy)
    far_weight = swap(plan, away, pair=1)
    chunks = x_forward(plan, place, [sums[0], from_x, far_y, from_xy])
    parts = [chunks[0]] + [swap(plan, chunks[s], outer=s) for s in range(1, plan.outer)]
    mixed = mix_modes(plan, parts, weight, far_weight)
    to_near, to_far = faces(plan, place, near_x, far_x, near_y, far_y, mixed)
    near_x = swap(plan, to_near, pair=1)
    far_x = next_pair(to_far, "gx")
    parts = [mixed] + [swap(plan, mixed, outer=s) for s in range(1, plan.outer)]
    args = (near_x, far_x, near_y, far_y, conv_taps(conv_weight))
    half = cells_x // 2
    mine, theirs = x_inverse(plan, place, parts)
    from_x = swap(plan, theirs, pair=1)
    from_y = swap(plan, mine, yy=1)
    from_xy = swap(plan, theirs, pair=1, yy=1)
    conv_a, token_a = conv_bricks(place, (own_h, own_l), *args, mine, 0, half)
    conv_b, _ = conv_bricks(place, (own_h, own_l), *args, mine, half, cells_x - half)
    own = jnp.concatenate([mine + token_a[:1], from_x, from_y, from_xy], axis=0)
    other = swap(plan, own, core=1)
    return final_layer(plan, place, own, other, (conv_a, conv_b))


def layer_any(features, conv_weight, mix_weight):
    channels, cells_x, cells_y, length_z = features.shape
    own = jax.ShapeDtypeStruct((cells_y, cells_x, channels, length_z), BF16)
    own = kernel_call(split_kernel, [own, own])(features)
    taps = conv_taps(conv_weight)
    conv, _ = conv_bricks(jnp.zeros((1,), jnp.int32), own, *halos(features), taps, taps, 0, cells_x)
    return jax.nn.gelu(conv.transpose(2, 0, 1, 3) + spectral_any(features, mix_weight), approximate=False)


def shards(features, conv_weight, mix_weight):
    counts = lax.axis_size("gx"), lax.axis_size("gy")
    if Plan.fits(features.shape, *counts):
        return layer_paired(Plan(features.shape, *counts), features, conv_weight, mix_weight)
    return layer_any(features, conv_weight, mix_weight)


def solution(mesh):
    in_specs = (P(None, "gx", "gy", None), P(), P(None, None, None, "gy", "gx"))
    out_specs = P(None, "gx", "gy", None)
    return jax.shard_map(shards, mesh=mesh, in_specs=in_specs, out_specs=out_specs, check_vma=False)
```

```python
import functools
import math

import jax
import jax.numpy as jnp
import ml_dtypes
import numpy as np
from jax import lax
from jax.experimental import pallas as pl
from jax.experimental.pallas import tpu as pltpu
from jax.sharding import PartitionSpec as P

KX = 24
KY = 24
KZ = 12
LANES = 128
F32 = jnp.float32
BF16 = jnp.bfloat16
PRECISE = lax.Precision.HIGHEST
VMEM_LIMIT = 24 * 1024 * 1024
NN = (((1,), (0,)), ((), ()))
NT = (((1,), (1,)), ((), ()))


def kernel_call(body, out_shape, scratch=(), grid_spec=None, **kw):
    params = pltpu.CompilerParams(vmem_limit_bytes=VMEM_LIMIT)
    if grid_spec is not None:
        kw["grid_spec"] = grid_spec
    else:
        kw["scratch_shapes"] = list(scratch)
    return pl.pallas_call(body, out_shape=out_shape, compiler_params=params, **kw)


def halves(value):
    high = value.astype(BF16)
    return high, (value - high.astype(F32)).astype(BF16)


def dot(a, b, dims=NN):
    return lax.dot_general(a, b, dims, preferred_element_type=F32)


def dot3(a, b, dims=NN):
    return dot(a[0], b[0], dims) + (dot(a[0], b[1], dims) + dot(a[1], b[0], dims))


def table_halves(table):
    table = np.asarray(table, np.float64)
    high = table.astype(ml_dtypes.bfloat16)
    low = (table - high.astype(np.float64)).astype(ml_dtypes.bfloat16)
    return high, low


def triple(parts, axis, twice_high_around):
    high, low = parts
    return jnp.concatenate([high, low, high] if twice_high_around else [high, high, low], axis=axis)


def kept_np(amount, length):
    index = np.arange(amount)
    return np.where(index < amount // 2, index, length - amount + index)


def angles_np(positions, frequencies, length):
    return 2.0 * np.pi * ((positions[:, None] * frequencies[None, :]) % length) / length


def split_kernel(feat, high, low):
    channels, cells_x, cells_y, length_z = feat.shape
    for x in range(cells_x):
        for y in range(cells_y):
            high[y, x], low[y, x] = halves(feat[:, x, y, :])


def conv_kernel(first, rows_y, count_gy, place, own_h, own_l, near_x, far_x, near_y, far_y, weight, after, out, token, edge_h, edge_l, rim_h, rim_l):
    cells_y, cells_x, channels, length_z = own_h.shape
    count = out.shape[0]
    span = rows_y + 2
    depth = 3 * span * channels
    even_x, even_y = place[0] // count_gy % 2 == 0, place[0] % count_gy % 2 == 0
    column, row = (cells_y + 2) * channels, cells_x * channels

    def tail(ref, size, at):
        return ref[ref.shape[0] - size + at : ref.shape[0] - size + at + channels, :]

    def pick(side, even, near, far, size, at):
        near, far = (tail(ref, size, at * channels) for ref in (near, far))
        return halves(jnp.where(even, near, far) if side else jnp.where(even, far, near))

    for side in range(2):
        if (0, cells_x + 1)[side] in range(first, first + count + 2):
            for y in range(cells_y):
                edge_h[side, y + 1], edge_l[side, y + 1] = pick(side, even_x, near_x, far_x, column, y)
            corners = [
                jnp.where(even_x == bool(side), *(tail(ref, column, (cells_y + n) * channels) for ref in (near_x, far_x)))
                for n in range(2)
            ]
            for up in range(2):
                value = jnp.where(even_y == bool(up), *corners)
                edge_h[side, up * (cells_y + 1)], edge_l[side, up * (cells_y + 1)] = halves(value)
        for x in range(max(first - 1, 0), min(first + count + 1, cells_x)):
            rim_h[side, x], rim_l[side, x] = pick(side, even_y, near_y, far_y, row, x)

    def cell(which, x, y):
        own, edge, rim = ((own_h, edge_h, rim_h), (own_l, edge_l, rim_l))[which]
        if x in (0, cells_x + 1):
            return edge[0 if x == 0 else 1, y]
        if y in (0, cells_y + 1):
            return rim[0 if y == 0 else 1, x - 1]
        return own[y - 1, x - 1]

    taps = halves(weight[...])
    tap = lax.broadcasted_iota(jnp.int32, (weight.shape[1], depth), 0)
    at = lax.broadcasted_iota(jnp.int32, (weight.shape[1], depth), 1)
    tap_a, tap_b, tap_i = tap // (3 * channels), tap // channels % 3, tap % channels
    at_a, at_y, at_i = at // (span * channels), at // channels % span, at % channels
    bands = [[], []]
    for y in range(rows_y):
        match = (tap_a == at_a) & (tap_b + y == at_y) & (tap_i == at_i)
        match = jnp.where(match, 1.0, 0.0).astype(BF16)
        for which in range(2):
            bands[which].append(dot(taps[which], match).astype(BF16))
    bands = [jnp.concatenate(b, axis=0) for b in bands]
    for x in range(0, count, 2):
        for y in range(0, cells_y, rows_y):
            field = []
            for which in range(2):
                columns = []
                for p in range(2):
                    cells = [cell(which, first + x + p + a, y + k) for a in range(3) for k in range(span)]
                    columns.append(jnp.concatenate(cells, axis=0))
                field.append(jnp.concatenate(columns, axis=1))
            value = dot3(bands, field)
            for k in range(rows_y):
                for p in range(2):
                    total = None
                    for c in range(3):
                        row = (k * 3 + c) * channels
                        piece = value[row : row + channels, p * length_z : (p + 1) * length_z]
                        if c != 1:
                            piece = pltpu.roll(piece, (1 - c) % length_z, 1)
                        total = piece if total is None else total + piece
                    out[x + p, y + k] = total
    token[...] = jnp.zeros(token.shape, F32)


def conv_taps(conv_weight):
    channels = conv_weight.shape[1]
    taps = conv_weight.reshape(3, 3, 3, channels, channels).transpose(2, 3, 0, 1, 4)
    return taps.reshape(3 * channels, 9 * channels)


def specs(count, first=None):
    vmem = pl.BlockSpec(memory_space=pltpu.VMEM)
    return [pl.BlockSpec(memory_space=pltpu.SMEM)] + [vmem] * count


def conv_bricks(place, own, near_x, far_x, near_y, far_y, taps, after, first, count):
    cells_y, cells_x, channels, length_z = own[0].shape
    return kernel_call(
        functools.partial(conv_kernel, first, 2, lax.axis_size("gy")),
        [jax.ShapeDtypeStruct((count, cells_y, channels, length_z), F32), jax.ShapeDtypeStruct((8, LANES), F32)],
        [pltpu.VMEM((2, cells_y + 2, channels, length_z), BF16)] * 2 + [pltpu.VMEM((2, cells_x, channels, length_z), BF16)] * 2,
        in_specs=specs(8),
    )(place, *own, near_x, far_x, near_y, far_y, taps, after)


def ring(value, axis, step):
    size = lax.axis_size(axis)
    return lax.ppermute(value, axis, [(i, (i + step) % size) for i in range(size)])


def halos(features):
    channels, cells_x, cells_y, length_z = features.shape
    flat = lambda v: v.transpose(1, 0, 2).reshape(-1, length_z)
    low_y = ring(features[:, :, cells_y - 1], "gy", 1)
    high_y = ring(features[:, :, 0], "gy", -1)

    def face(x):
        return jnp.concatenate([features[:, x], high_y[:, x][:, None], low_y[:, x][:, None]], axis=1)

    low_x = ring(face(cells_x - 1), "gx", 1)
    high_x = ring(face(0), "gx", -1)
    return flat(high_x), flat(low_x), flat(high_y), flat(low_y)


def angle_tables(positions, frequencies, length):
    product = positions[:, None] * frequencies[None, :] % length
    angles = product.astype(jnp.float32) * (2.0 * math.pi / length)
    return (jnp.cos(angles), jnp.sin(angles))


def kept_frequencies(amount, length):
    index = jnp.arange(amount, dtype=jnp.int32)
    return jnp.where(index < amount // 2, index, length - amount + index)


def times(form, a, b, c, d):
    one = functools.partial(jnp.einsum, form, precision=PRECISE)
    return one(a, c) + one(b, d)


def spectral_any(features, mix_weight):
    channels, cells_x, cells_y, length_z = features.shape
    count_gx = lax.axis_size("gx")
    count_gy = lax.axis_size("gy")
    length_x = cells_x * count_gx
    length_y = cells_y * count_gy
    block_yz = KY * KZ // count_gy
    cos_z, sin_z = angle_tables(jnp.arange(length_z, dtype=jnp.int32), jnp.arange(KZ, dtype=jnp.int32), length_z)
    y_places = lax.axis_index("gy") * cells_y + jnp.arange(cells_y, dtype=jnp.int32)
    x_places = lax.axis_index("gx") * cells_x + jnp.arange(cells_x, dtype=jnp.int32)
    cos_y, sin_y = angle_tables(y_places, kept_frequencies(KY, length_y), length_y)
    cos_x, sin_x = angle_tables(x_places, kept_frequencies(KX, length_x), length_x)
    along_z = jnp.dot(features, jnp.concatenate([cos_z, -sin_z], axis=1), precision=PRECISE)
    z_real = along_z[..., :KZ]
    z_imag = along_z[..., KZ:]
    y_real = times("cxyk,yq->cxqk", z_real, z_imag, cos_y, sin_y)
    y_imag = times("cxyk,yq->cxqk", z_imag, z_real, cos_y, -sin_y)
    partial_value = jnp.stack([y_real, y_imag], axis=2).reshape(channels, cells_x, 2, KY * KZ)
    y_share = lax.psum_scatter(partial_value, "gy", scatter_dimension=3, tiled=True)
    x_real = times("cxm,xp->cpm", y_share[:, :, 0], y_share[:, :, 1], cos_x, sin_x)
    x_imag = times("cxm,xp->cpm", y_share[:, :, 1], y_share[:, :, 0], cos_x, -sin_x)
    x_partial = jnp.stack([x_real, x_imag], axis=1).reshape(channels, 2, KX * block_yz)
    owned_modes = lax.psum_scatter(x_partial, "gx", scatter_dimension=2, tiled=True)
    owned_modes = owned_modes * (1.0 / math.sqrt(length_x * length_y * length_z))
    coef_real = owned_modes[:, 0]
    coef_imag = owned_modes[:, 1]
    weight_real = mix_weight[0, :, :, 0, :]
    weight_imag = mix_weight[1, :, :, 0, :]
    mixed_real = times("oim,im->om", weight_real, weight_imag, coef_real, -coef_imag)
    mixed_imag = times("oim,im->om", weight_real, weight_imag, coef_imag, coef_real)
    mixed_modes = jnp.stack([mixed_real, mixed_imag], axis=1)
    row_modes = lax.all_gather(mixed_modes, "gx", axis=2, tiled=True).reshape(channels, 2, KX, block_yz)
    back_real = times("cpm,xp->cxm", row_modes[:, 0], row_modes[:, 1], cos_x, -sin_x)
    back_imag = times("cpm,xp->cxm", row_modes[:, 1], row_modes[:, 0], cos_x, sin_x)
    gathered = lax.all_gather(jnp.stack([back_real, back_imag], axis=2), "gy", axis=3, tiled=True)
    back_real = gathered[:, :, 0].reshape(channels, cells_x, KY, KZ)
    back_imag = gathered[:, :, 1].reshape(channels, cells_x, KY, KZ)
    plane_real = times("cxqk,yq->cxyk", back_real, back_imag, cos_y, -sin_y)
    plane_imag = times("cxqk,yq->cxyk", back_imag, back_real, cos_y, sin_y)
    table_back = jnp.concatenate([cos_z.T, -sin_z.T], axis=0)
    planes = jnp.concatenate([plane_real, plane_imag], axis=3)
    return jnp.dot(planes, table_back, precision=PRECISE) * (1.0 / math.sqrt(KX * KY * KZ))


class Plan:
    def __init__(self, feature_shape, count_gx, count_gy):
        self.channels, self.cells_x, self.cells_y, self.length_z = feature_shape
        self.count_gx, self.count_gy = count_gx, count_gy
        self.outer = count_gx // 2
        self.block = KY * KZ // count_gy
        self.part = self.block // 2
        self.per_gx = KX // count_gx
        self.rows = 2 * self.part
        self.pad_k = -(-KZ // 8) * 8
        self.pad_z = 2 * self.pad_k
        self.turns = self.part // KZ
        self.length_x = self.cells_x * count_gx
        self.length_y = self.cells_y * count_gy

    def spot(self, place):
        return place[0] // self.count_gy, place[0] % self.count_gy

    @staticmethod
    def fits(feature_shape, count_gx, count_gy):
        channels, cells_x, cells_y, length_z = feature_shape
        outer = count_gx // 2
        if count_gy != 4 or count_gx % 2 or outer & (outer - 1) or outer > 4:
            return False
        if KX % count_gx or (KY * KZ) % (2 * count_gy) or channels * cells_x != LANES:
            return False
        part = KY * KZ // count_gy // 2
        per = KX // count_gx
        return (
            length_z == LANES
            and cells_y % (LANES // (2 * (-(-KZ // 8) * 8))) == 0
            and channels % 16 == 0
            and (2 * part) % 8 == 0
            and 4 * 2 * part % 16 == 0
            and part % KZ == 0
            and per * part <= LANES
            and 2 * per * channels <= LANES
            and 2 * per * part <= 2 * LANES
            and 2 * part <= LANES
        )

    def table_z(self):
        table = np.zeros((2, self.pad_k, self.length_z))
        angle = angles_np(np.arange(KZ), np.arange(self.length_z), self.length_z)
        table[0, :KZ] = np.cos(angle)
        table[1, :KZ] = -np.sin(angle)
        return table.reshape(self.pad_z, self.length_z)

    def table_z_group(self):
        return np.kron(np.eye(LANES // self.pad_z), self.table_z())

    def trig_z(self):
        shape = (self.pad_z, self.length_z)
        row, z = (lax.broadcasted_iota(jnp.int32, shape, n) for n in range(2))
        k, imag = row % self.pad_k, row // self.pad_k
        turn = k * z % self.length_z
        turn = jnp.where(imag == 1, turn + self.length_z // 4, turn) % self.length_z
        value = jnp.cos(turn.astype(F32) * (2.0 * math.pi / self.length_z))
        return jnp.where(k < KZ, value, 0.0)

    def half_of(self, gx, gy):
        return (gy + gy // 2 + gx // 2 + gx) % 2

    def trig_y(self, gx, gy, turned):
        shape = (16 * self.turns, 2 * self.cells_y)
        row, col = (lax.broadcasted_iota(jnp.int32, shape[::-1] if turned else shape, n ^ int(turned)) for n in range(2))
        offset = row // (2 * self.turns)
        y_bit = (gy // 2 + offset // 2) % 2
        owner = (y_bit * 2 + (self.half_of(gx, gy) + offset // 4) % 2) * 2 + (gx + offset) % 2
        mode = owner * self.turns + row % self.turns
        kept = jnp.where(mode < KY // 2, mode, self.length_y - KY + mode)
        turn = kept * (gy * self.cells_y + col // 2) % self.length_y
        quarter = self.length_y // 4
        out_part, in_part = row // self.turns % 2, col % 2
        shift = jnp.where(out_part == in_part, 0, jnp.where(out_part == 0, 3 * quarter, quarter))
        return jnp.cos(((turn + shift) % self.length_y).astype(F32) * (2.0 * math.pi / self.length_y))

    def trig_x(self, gx, inverse):
        modes, places = self.outer * 2 * self.per_gx, 2 * self.cells_x
        shape = (places, 2 * modes) if inverse else (modes, 2 * places)
        row, col = (lax.broadcasted_iota(jnp.int32, shape, n) for n in range(2))
        width = modes if inverse else places
        crossed = col // width
        mode, at = (col % width, row) if inverse else (row, col % width)
        outer, pair = gx // 2, gx % 2
        offset, inner = mode // (2 * self.per_gx), mode % (2 * self.per_gx)
        other = jnp.zeros_like(offset)
        for s in range(self.outer):
            other = jnp.where(offset == s, outer ^ s, other)
        index = (2 * other + (pair + inner // self.per_gx) % 2) * self.per_gx + inner % self.per_gx
        kept = jnp.where(index < KX // 2, index, self.length_x - KX + index)
        far = (2 * outer + 1 - pair) * self.cells_x + at - self.cells_x
        x = jnp.where(at < self.cells_x, gx * self.cells_x + at, far)
        turn = kept * x % self.length_x
        turn = (turn + jnp.where(crossed == 1, 3 * (self.length_x // 4), 0)) % self.length_x
        return jnp.cos(turn.astype(F32) * (2.0 * math.pi / self.length_x))


def tripled_table(table):
    high, low = table_halves(table)
    return np.concatenate([high, high, low], axis=-1)


def forward_kernel(plan, place, feat, keep, send, own_h, own_l, near_x, far_x, far_y, field):
    channels, cells_x, cells_y = plan.channels, plan.cells_x, plan.cells_y
    gx, gy = plan.spot(place)
    even_x, even_y = gx % 2 == 0, gy % 2 == 0
    pad = plan.pad_z
    z_table = triple(halves(plan.trig_z()), 1, False)
    ends = []
    for y in range(cells_y):
        plane = [feat[pl.ds(x * cells_y + y, channels, stride=cells_x * cells_y), :] for x in range(cells_x)]
        near_x[y] = jnp.where(even_x, plane[-1], plane[0])
        far_x[y] = jnp.where(even_x, plane[0], plane[-1])
        plane = jnp.concatenate(plane, axis=0)
        if y in (0, cells_y - 1):
            ends.append(plane)
        high, low = halves(plane)
        own_h[y] = high.reshape(cells_x, channels, -1)
        own_l[y] = low.reshape(cells_x, channels, -1)
        field[y * pad : (y + 1) * pad, :] = dot(z_table, triple((high, low), 1, True), NT)
    y_table = triple(halves(plan.trig_y(gx, gy, False)), 1, False)
    half = 8 * plan.turns
    for k in range(KZ):
        value = halves(field[pl.ds(k, 2 * cells_y, stride=plan.pad_k), :])
        value = dot(y_table, triple(value, 0, True))
        keep[pl.ds(k, half, stride=KZ), :] = value[:half]
        send[pl.ds(k, half, stride=KZ), :] = value[half:]
    start = half * KZ
    send[start:, :] = jnp.where(even_y, ends[1], ends[0])
    far_y[...] = jnp.where(even_y, ends[0], ends[1])


def forward_modes(plan, place, features):
    half, length_z = 4 * plan.rows, plan.length_z
    own = jax.ShapeDtypeStruct((plan.cells_y, plan.cells_x, plan.channels, length_z), BF16)
    face = jax.ShapeDtypeStruct((plan.cells_y, plan.channels, length_z), F32)
    shape = lambda *s: jax.ShapeDtypeStruct(s, F32)
    return kernel_call(
        functools.partial(forward_kernel, plan),
        [shape(half, LANES), shape(half + LANES, LANES), own, own, face, face, shape(LANES, LANES)],
        [pltpu.VMEM((plan.cells_y * plan.pad_z, LANES), F32)],
        in_specs=specs(1),
    )(place, features.reshape(-1, length_z))


def turned(value, part, sign):
    lane = lax.broadcasted_iota(jnp.int32, value.shape, 1)
    low = pltpu.roll(value, LANES - part, 1)
    high = pltpu.roll(value, part, 1)
    return jnp.where(lane < part, sign * low, -sign * high)


def square_turned(value):
    return jnp.concatenate([value, jnp.zeros((LANES - value.shape[0], LANES), F32)], axis=0).T


def x_forward_kernel(plan, place, own, from_xy, from_y, from_x, *refs):
    outs = refs[: plan.outer]
    straight, crossed, found = refs[plan.outer :]
    rows, channels, per = plan.rows, plan.channels, 2 * plan.per_gx
    near = own[...] + from_y[:rows, :]
    far = from_x[...] + from_xy[...]
    for at, value in enumerate((near, far)):
        value = square_turned(value)
        straight[at * LANES : (at + 1) * LANES, :] = value
        crossed[at * LANES : (at + 1) * LANES, :] = turned(value, plan.part, 1.0)
    factor = triple(halves(plan.trig_x(plan.spot(place)[0], False)), 1, False)
    for c in range(channels):
        index = pl.ds(c, 2 * plan.cells_x, stride=channels)
        value = halves(jnp.concatenate([straight[index, :], crossed[index, :]], axis=0))
        found[pl.ds(c, plan.outer * per, stride=channels), :] = dot(factor, triple(value, 0, True))
    for at, out in enumerate(outs):
        size = per * channels
        out[...] = square_turned(found[at * size : (at + 1) * size, :])[:rows]


def x_inverse_kernel(plan, place, *refs):
    parts = refs[: plan.outer]
    near, far, straight, crossed, found = refs[plan.outer :]
    rows, channels, per = plan.rows, plan.channels, 2 * plan.per_gx
    size = per * channels
    for at, part in enumerate(parts):
        value = square_turned(part[...])[:size]
        straight[at * size : (at + 1) * size, :] = value
        crossed[at * size : (at + 1) * size, :] = turned(value, plan.part, -1.0)
    factor = triple(halves(plan.trig_x(plan.spot(place)[0], True)), 1, False)
    for c in range(channels):
        index = pl.ds(c, plan.outer * per, stride=channels)
        value = halves(jnp.concatenate([straight[index, :], crossed[index, :]], axis=0))
        found[pl.ds(c, 2 * plan.cells_x, stride=channels), :] = dot(factor, triple(value, 0, True))
    for at, out in enumerate((near, far)):
        out[...] = found[at * LANES : (at + 1) * LANES, :].T[:rows]


def x_forward(plan, place, parts):
    part = jax.ShapeDtypeStruct((plan.rows, LANES), F32)
    size = plan.outer * 2 * plan.per_gx * plan.channels
    scratch = [pltpu.VMEM((n, LANES), F32) for n in (2 * LANES, 2 * LANES, size)]
    body = functools.partial(x_forward_kernel, plan)
    return kernel_call(body, [part] * plan.outer, scratch, in_specs=specs(4))(place, *parts)


def x_inverse(plan, place, parts):
    part = jax.ShapeDtypeStruct((plan.rows, LANES), F32)
    size = plan.outer * 2 * plan.per_gx * plan.channels
    scratch = [pltpu.VMEM((n, LANES), F32) for n in (size, size, 2 * LANES)]
    body = functools.partial(x_inverse_kernel, plan)
    return kernel_call(body, [part] * 2, scratch, in_specs=specs(plan.outer))(place, *parts)


def weight_kernel(plan, place, weight, out, flat, sem):
    copy = pltpu.make_async_copy(weight.at[:, :, 0, :], flat, sem)
    copy.start()
    copy.wait()
    part, block = plan.part, plan.block
    square = plan.channels * plan.channels
    lane = lax.broadcasted_iota(jnp.int32, (square, LANES), 1)
    width = 2 * LANES
    held = flat.shape[2]
    even = plan.spot(place)[0] % 2 == 0
    for which in range(2):
        high = jnp.concatenate([flat[which, :, LANES:], jnp.zeros((square, width - held), F32)], axis=1)
        value = jnp.concatenate([flat[which, :, :LANES], high], axis=1)
        choice = []
        for half in range(2):
            total = jnp.zeros((square, LANES), F32)
            for j in range(plan.per_gx):
                shift = (j * part - j * block - half * part) % width
                moved = value if shift == 0 else pltpu.roll(value, shift, 1)
                inside = (lane >= j * part) & (lane < (j + 1) * part)
                total = jnp.where(inside, moved[:, :LANES], total)
            choice.append(total)
        at = slice(which * square, (which + 1) * square)
        out[at, :] = jnp.where(even, choice[0], choice[1])
        out[slice(at.start + 2 * square, at.stop + 2 * square), :] = jnp.where(even, choice[1], choice[0])


def weight_parts(plan, place, mix_weight):
    square = plan.channels * plan.channels
    modes = mix_weight.shape[-1]
    return kernel_call(
        functools.partial(weight_kernel, plan),
        jax.ShapeDtypeStruct((4 * square, LANES), F32),
        [pltpu.VMEM((2, square, modes), F32), pltpu.SemaphoreType.DMA],
        in_specs=specs(1),
    )(place, mix_weight.reshape(2, square, 1, modes))


def faces_kernel(plan, place, near_x, far_x, near_y, far_y, after, to_near, to_far):
    channels, cells_x, cells_y = plan.channels, plan.cells_x, plan.cells_y
    even = plan.spot(place)[0] % 2 == 0
    last = cells_x - 1
    for out, face, x in ((to_near, near_x, jnp.where(even, last, 0)), (to_far, far_x, jnp.where(even, 0, last))):
        for y in range(cells_y):
            out[y * channels : (y + 1) * channels, :] = face[y]
        for n, ref in enumerate((near_y, far_y)):
            at = pl.multiple_of(ref.shape[0] - LANES + x * channels, channels)
            start = (cells_y + n) * channels
            out[start : start + channels, :] = ref[pl.ds(at, channels), :]


def faces(plan, place, near_x, far_x, near_y, far_y, after):
    out = jax.ShapeDtypeStruct(((plan.cells_y + 2) * plan.channels, LANES), F32)
    return kernel_call(functools.partial(faces_kernel, plan), [out, out], in_specs=specs(5))(
        place, near_x, far_x, near_y, far_y, after
    )


def mix_kernel(plan, *refs):
    parts = refs[: plan.outer]
    near, far, out = refs[plan.outer :]
    channels, part, per, rows = plan.channels, plan.part, plan.per_gx, plan.rows
    total = parts[0][...]
    for p in parts[1:]:
        total = total + p[...]
    scale = 1.0 / math.sqrt(plan.length_x * plan.length_y * plan.length_z) / math.sqrt(KX * KY * KZ)
    total = jnp.concatenate([total * scale, jnp.zeros((LANES - rows, LANES), F32)], axis=0).T
    lane = lax.broadcasted_iota(jnp.int32, (channels, LANES), 1)

    def moved(value, shift):
        return value if shift % LANES == 0 else pltpu.roll(value, shift % LANES, 1)

    def collect(half, which):
        value = jnp.zeros((channels, LANES), F32)
        for j in range(per):
            at = (half * per + j) * channels
            piece = moved(total[at : at + channels], (j - which) * part)
            value = jnp.where((lane >= j * part) & (lane < (j + 1) * part), piece, value)
        return value

    blocks = []
    for half, weight in enumerate((near, far)):
        c_real, c_imag = collect(half, 0), collect(half, 1)
        real = jnp.zeros((channels, LANES), F32)
        imag = jnp.zeros((channels, LANES), F32)
        for i in range(channels):
            w_real = weight[pl.ds(i, channels, stride=channels), :]
            w_imag = weight[pl.ds(channels * channels + i, channels, stride=channels), :]
            a, b = c_real[i : i + 1], c_imag[i : i + 1]
            real = real + (w_real * a - w_imag * b)
            imag = imag + (w_real * b + w_imag * a)
        for j in range(per):
            low = moved(real, -j * part)
            high = moved(imag, part - j * part)
            blocks.append(jnp.where(lane < part, low, jnp.where(lane < 2 * part, high, 0.0)))
    fill = LANES - 2 * per * channels
    if fill:
        blocks.append(jnp.zeros((fill, LANES), F32))
    out[...] = jnp.concatenate(blocks, axis=0).T[:rows]


def mix_modes(plan, parts, near, far):
    return kernel_call(functools.partial(mix_kernel, plan), jax.ShapeDtypeStruct((plan.rows, LANES), F32))(
        *parts, near, far
    )


def final_kernel(plan, place, own, other, conv_a, conv_b, table_z, out, field, ready, sems):
    channels, cells_x, cells_y = plan.channels, plan.cells_x, plan.cells_y
    pieces = ready.shape[0]
    deep = cells_y // pieces
    copies = [pltpu.make_async_copy(ready.at[n], out.at[:, pl.ds(n * deep, deep), :], sems.at[n]) for n in range(pieces)]
    gx, gy = plan.spot(place)
    y_table = triple(halves(plan.trig_y(gx, gy, True)), 1, False)
    half = 8 * plan.turns
    field[...] = jnp.zeros(field.shape, F32)
    for k in range(KZ):
        parts = [ref[pl.ds(k, half, stride=KZ), :] for ref in (own, other)]
        value = halves(jnp.concatenate(parts, axis=0))
        field[pl.ds(k, 2 * cells_y, stride=plan.pad_k), :] = dot(y_table, triple(value, 0, True))
    z_table = table_z[...]
    group = LANES // plan.pad_z
    for g in range(cells_y // group):
        planes = halves(field[g * LANES : (g + 1) * LANES, :].T)
        value = dot(triple(planes, 1, False), z_table)
        for k in range(group):
            y = g * group + k
            conv = [ref[x, y] for ref in (conv_a, conv_b) for x in range(ref.shape[0])]
            layer = jnp.concatenate(conv, axis=0) + value[:, k * LANES : (k + 1) * LANES]
            layer = layer * 0.5 * (1.0 + lax.erf(layer * math.sqrt(0.5)))
            flat = ready.at[y // deep].reshape(channels * cells_x * deep, plan.length_z)
            for x in range(cells_x):
                flat[pl.ds(x * deep + y % deep, channels, stride=cells_x * deep), :] = layer[x * channels : (x + 1) * channels]
            if y % deep == deep - 1:
                copies[y // deep].start()
    for copy in copies:
        copy.wait()


def final_layer(plan, place, own, other, convs):
    high, low = table_halves(plan.table_z_group())
    table_z = np.concatenate([high, low, high], axis=0)
    shape = (plan.channels, plan.cells_x, plan.cells_y, plan.length_z)
    flat = (plan.channels * plan.cells_x, plan.cells_y, plan.length_z)
    pieces = plan.cells_y // 8
    ready = pltpu.VMEM((pieces, plan.channels * plan.cells_x, 8, plan.length_z), F32)
    return kernel_call(
        functools.partial(final_kernel, plan),
        jax.ShapeDtypeStruct(flat, F32),
        [pltpu.VMEM((plan.cells_y * plan.pad_z, LANES), F32), ready, pltpu.SemaphoreType.DMA((pieces,))],
        in_specs=specs(5),
        out_specs=pl.BlockSpec(memory_space=pltpu.HBM),
    )(place, own, other, *convs, table_z).reshape(shape)


def swap(plan, value, outer=0, pair=0, yy=0, core=0):
    perm = []
    for gx in range(plan.count_gx):
        for gy in range(plan.count_gy):
            to_gx = gx ^ (outer * 2 + pair)
            to_gy = gy ^ (yy * 2 + core)
            perm.append((gx * plan.count_gy + gy, to_gx * plan.count_gy + to_gy))
    return lax.ppermute(value, ("gx", "gy"), perm)


def next_pair(value, axis):
    size = lax.axis_size(axis)
    return lax.ppermute(value, axis, [(i, (i + (1 if i % 2 else -1)) % size) for i in range(size)])


def after(value, *others):
    zero = sum(jnp.minimum(jnp.abs(other[:1]), 0.0) for other in others)
    return value + zero


def layer_paired(plan, features, conv_weight, mix_weight):
    rows = plan.rows
    place = (lax.axis_index("gx") * plan.count_gy + lax.axis_index("gy")).astype(jnp.int32).reshape(1)
    cells_x = features.shape[1]

    keep, send, own_h, own_l, near_x, far_x, far_y = forward_modes(plan, place, features)
    both = weight_parts(plan, place, mix_weight)
    exchanged = swap(plan, both, core=1)
    at_gx, at_gy = lax.axis_index("gx"), lax.axis_index("gy")
    both = jnp.where(plan.half_of(at_gx, at_gy) == at_gy % 2, both, exchanged)
    weight, away = both[: both.shape[0] // 2], both[both.shape[0] // 2 :]
    near_y = swap(plan, send, core=1)
    sums = [keep[s * rows : (s + 1) * rows] + near_y[s * rows : (s + 1) * rows] for s in range(4)]
    far_y = swap(plan, jnp.concatenate([sums[2], far_y], axis=0), yy=1, core=1)
    from_x = swap(plan, sums[1], pair=1, core=1)
    from_xy = swap(plan, sums[3], pair=1, yy=1)
    away = after(away, from_x, far_y, from_xy)
    far_weight = swap(plan, away, pair=1, core=1)
    chunks = x_forward(plan, place, [sums[0], from_xy, far_y, from_x])
    got = {s: swap(plan, chunks[s], outer=s, core=s % 2) for s in range(plan.outer - 1, 0, -1)}
    parts = [chunks[0]] + [got[s] for s in range(plan.outer - 1, 0, -1)]
    mixed = mix_modes(plan, parts, weight, far_weight)
    to_near, to_far = faces(plan, place, near_x, far_x, near_y, far_y, mixed)
    near_x = swap(plan, to_near, pair=1)
    far_x = next_pair(to_far, "gx")
    got = {s: swap(plan, mixed, outer=s, core=s % 2) for s in range(plan.outer - 1, 0, -1)}
    parts = [mixed] + [got[s] for s in range(1, plan.outer)]
    args = (near_x, far_x, near_y, far_y, conv_taps(conv_weight))
    half = cells_x // 2
    mine, theirs = x_inverse(plan, place, parts)
    from_x = swap(plan, theirs, pair=1, core=1)
    from_y = swap(plan, mine, yy=1, core=1)
    from_xy = swap(plan, theirs, pair=1, yy=1)
    conv_a, token_a = conv_bricks(place, (own_h, own_l), *args, mine, 0, half)
    conv_b, _ = conv_bricks(place, (own_h, own_l), *args, mine, half, cells_x - half)
    own = jnp.concatenate([mine + token_a[:1], from_x, from_y, from_xy], axis=0)
    other = swap(plan, own, core=1)
    return final_layer(plan, place, own, other, (conv_a, conv_b))


def layer_any(features, conv_weight, mix_weight):
    channels, cells_x, cells_y, length_z = features.shape
    own = jax.ShapeDtypeStruct((cells_y, cells_x, channels, length_z), BF16)
    own = kernel_call(split_kernel, [own, own])(features)
    taps = conv_taps(conv_weight)
    conv, _ = conv_bricks(jnp.zeros((1,), jnp.int32), own, *halos(features), taps, taps, 0, cells_x)
    return jax.nn.gelu(conv.transpose(2, 0, 1, 3) + spectral_any(features, mix_weight), approximate=False)


def shards(features, conv_weight, mix_weight):
    counts = lax.axis_size("gx"), lax.axis_size("gy")
    if Plan.fits(features.shape, *counts):
        return layer_paired(Plan(features.shape, *counts), features, conv_weight, mix_weight)
    return layer_any(features, conv_weight, mix_weight)


def solution(mesh):
    in_specs = (P(None, "gx", "gy", None), P(), P(None, None, None, "gy", "gx"))
    out_specs = P(None, "gx", "gy", None)
    return jax.shard_map(shards, mesh=mesh, in_specs=in_specs, out_specs=out_specs, check_vma=False)
```

```python
import functools
import math

import jax
import jax.numpy as jnp
import ml_dtypes
import numpy as np
from jax import lax
from jax.experimental import pallas as pl
from jax.experimental.pallas import tpu as pltpu
from jax.sharding import PartitionSpec as P

KX = 24
KY = 24
KZ = 12
LANES = 128
F32 = jnp.float32
BF16 = jnp.bfloat16
PRECISE = lax.Precision.HIGHEST
VMEM_LIMIT = 24 * 1024 * 1024
NN = (((1,), (0,)), ((), ()))
NT = (((1,), (1,)), ((), ()))


def kernel_call(body, out_shape, scratch=(), grid_spec=None, **kw):
    params = pltpu.CompilerParams(vmem_limit_bytes=VMEM_LIMIT)
    if grid_spec is not None:
        kw["grid_spec"] = grid_spec
    else:
        kw["scratch_shapes"] = list(scratch)
    return pl.pallas_call(body, out_shape=out_shape, compiler_params=params, **kw)


def halves(value):
    high = value.astype(BF16)
    return high, (value - high.astype(F32)).astype(BF16)


def dot(a, b, dims=NN):
    return lax.dot_general(a, b, dims, preferred_element_type=F32)


def dot3(a, b, dims=NN):
    return dot(a[0], b[0], dims) + (dot(a[0], b[1], dims) + dot(a[1], b[0], dims))


def table_halves(table):
    table = np.asarray(table, np.float64)
    high = table.astype(ml_dtypes.bfloat16)
    low = (table - high.astype(np.float64)).astype(ml_dtypes.bfloat16)
    return high, low


def triple(parts, axis, twice_high_around):
    high, low = parts
    return jnp.concatenate([high, low, high] if twice_high_around else [high, high, low], axis=axis)


def kept_np(amount, length):
    index = np.arange(amount)
    return np.where(index < amount // 2, index, length - amount + index)


def angles_np(positions, frequencies, length):
    return 2.0 * np.pi * ((positions[:, None] * frequencies[None, :]) % length) / length


def split_kernel(feat, high, low):
    channels, cells_x, cells_y, length_z = feat.shape
    for x in range(cells_x):
        for y in range(cells_y):
            high[y, x], low[y, x] = halves(feat[:, x, y, :])


def conv_kernel(columns, rows_y, count_gy, place, own_h, own_l, near_x, far_x, near_y, far_y, weight, after, out, *refs):
    tokens, (edge_h, edge_l, rim_h, rim_l) = refs[:-4], refs[-4:]
    cells_y, cells_x, channels, length_z = own_h.shape
    needed = sorted({x + a for x in columns for a in range(3)})
    span = rows_y + 2
    depth = 3 * span * channels
    even_x, even_y = place[0] // count_gy % 2 == 0, place[0] % count_gy % 2 == 0
    column, row = (cells_y + 2) * channels, cells_x * channels

    def tail(ref, size, at):
        return ref[ref.shape[0] - size + at : ref.shape[0] - size + at + channels, :]

    def pick(side, even, near, far, size, at):
        near, far = (tail(ref, size, at * channels) for ref in (near, far))
        return halves(jnp.where(even, near, far) if side else jnp.where(even, far, near))

    for side in range(2):
        if (0, cells_x + 1)[side] in needed:
            for y in range(cells_y):
                edge_h[side, y + 1], edge_l[side, y + 1] = pick(side, even_x, near_x, far_x, column, y)
            corners = [
                jnp.where(even_x == bool(side), *(tail(ref, column, (cells_y + n) * channels) for ref in (near_x, far_x)))
                for n in range(2)
            ]
            for up in range(2):
                value = jnp.where(even_y == bool(up), *corners)
                edge_h[side, up * (cells_y + 1)], edge_l[side, up * (cells_y + 1)] = halves(value)
        for x in [n - 1 for n in needed if 0 < n <= cells_x]:
            rim_h[side, x], rim_l[side, x] = pick(side, even_y, near_y, far_y, row, x)

    def cell(which, x, y):
        own, edge, rim = ((own_h, edge_h, rim_h), (own_l, edge_l, rim_l))[which]
        if x in (0, cells_x + 1):
            return edge[0 if x == 0 else 1, y]
        if y in (0, cells_y + 1):
            return rim[0 if y == 0 else 1, x - 1]
        return own[y - 1, x - 1]

    taps = halves(weight[...])
    tap = lax.broadcasted_iota(jnp.int32, (weight.shape[1], depth), 0)
    at = lax.broadcasted_iota(jnp.int32, (weight.shape[1], depth), 1)
    tap_a, tap_b, tap_i = tap // (3 * channels), tap // channels % 3, tap % channels
    at_a, at_y, at_i = at // (span * channels), at // channels % span, at % channels
    bands = [[], []]
    for y in range(rows_y):
        match = (tap_a == at_a) & (tap_b + y == at_y) & (tap_i == at_i)
        match = jnp.where(match, 1.0, 0.0).astype(BF16)
        for which in range(2):
            bands[which].append(dot(taps[which], match).astype(BF16))
    bands = [jnp.concatenate(b, axis=0) for b in bands]
    for n in range(0, len(columns), 2):
        for y in range(0, cells_y, rows_y):
            field = []
            for which in range(2):
                lanes = []
                for p in range(2):
                    cells = [cell(which, columns[n + p] + a, y + k) for a in range(3) for k in range(span)]
                    lanes.append(jnp.concatenate(cells, axis=0))
                field.append(jnp.concatenate(lanes, axis=1))
            value = dot3(bands, field)
            for k in range(rows_y):
                for p in range(2):
                    total = None
                    for c in range(3):
                        row = (k * 3 + c) * channels
                        piece = value[row : row + channels, p * length_z : (p + 1) * length_z]
                        if c != 1:
                            piece = pltpu.roll(piece, (1 - c) % length_z, 1)
                        total = piece if total is None else total + piece
                    out[n + p, y + k] = total
    for token in tokens:
        token[...] = jnp.zeros(token.shape, F32)


def conv_taps(conv_weight):
    channels = conv_weight.shape[1]
    taps = conv_weight.reshape(3, 3, 3, channels, channels).transpose(2, 3, 0, 1, 4)
    return taps.reshape(3 * channels, 9 * channels)


def specs(count, first=None):
    vmem = pl.BlockSpec(memory_space=pltpu.VMEM)
    return [pl.BlockSpec(memory_space=pltpu.SMEM)] + [vmem] * count


def conv_bricks(place, own, near_x, far_x, near_y, far_y, taps, after, columns, mark=False):
    cells_y, cells_x, channels, length_z = own[0].shape
    outs = [jax.ShapeDtypeStruct((len(columns), cells_y, channels, length_z), F32)]
    if mark:
        outs.append(jax.ShapeDtypeStruct((8, length_z), F32))
    return kernel_call(
        functools.partial(conv_kernel, tuple(columns), 2, lax.axis_size("gy")),
        outs,
        [pltpu.VMEM((2, cells_y + 2, channels, length_z), BF16)] * 2 + [pltpu.VMEM((2, cells_x, channels, length_z), BF16)] * 2,
        in_specs=specs(8),
    )(place, *own, near_x, far_x, near_y, far_y, taps, after)


def ring(value, axis, step):
    size = lax.axis_size(axis)
    return lax.ppermute(value, axis, [(i, (i + step) % size) for i in range(size)])


def halos(features):
    channels, cells_x, cells_y, length_z = features.shape
    flat = lambda v: v.transpose(1, 0, 2).reshape(-1, length_z)
    low_y = ring(features[:, :, cells_y - 1], "gy", 1)
    high_y = ring(features[:, :, 0], "gy", -1)

    def face(x):
        return jnp.concatenate([features[:, x], high_y[:, x][:, None], low_y[:, x][:, None]], axis=1)

    low_x = ring(face(cells_x - 1), "gx", 1)
    high_x = ring(face(0), "gx", -1)
    return flat(high_x), flat(low_x), flat(high_y), flat(low_y)


def angle_tables(positions, frequencies, length):
    product = positions[:, None] * frequencies[None, :] % length
    angles = product.astype(jnp.float32) * (2.0 * math.pi / length)
    return (jnp.cos(angles), jnp.sin(angles))


def kept_frequencies(amount, length):
    index = jnp.arange(amount, dtype=jnp.int32)
    return jnp.where(index < amount // 2, index, length - amount + index)


def times(form, a, b, c, d):
    one = functools.partial(jnp.einsum, form, precision=PRECISE)
    return one(a, c) + one(b, d)


def spectral_any(features, mix_weight):
    channels, cells_x, cells_y, length_z = features.shape
    count_gx = lax.axis_size("gx")
    count_gy = lax.axis_size("gy")
    length_x = cells_x * count_gx
    length_y = cells_y * count_gy
    block_yz = KY * KZ // count_gy
    cos_z, sin_z = angle_tables(jnp.arange(length_z, dtype=jnp.int32), jnp.arange(KZ, dtype=jnp.int32), length_z)
    y_places = lax.axis_index("gy") * cells_y + jnp.arange(cells_y, dtype=jnp.int32)
    x_places = lax.axis_index("gx") * cells_x + jnp.arange(cells_x, dtype=jnp.int32)
    cos_y, sin_y = angle_tables(y_places, kept_frequencies(KY, length_y), length_y)
    cos_x, sin_x = angle_tables(x_places, kept_frequencies(KX, length_x), length_x)
    along_z = jnp.dot(features, jnp.concatenate([cos_z, -sin_z], axis=1), precision=PRECISE)
    z_real = along_z[..., :KZ]
    z_imag = along_z[..., KZ:]
    y_real = times("cxyk,yq->cxqk", z_real, z_imag, cos_y, sin_y)
    y_imag = times("cxyk,yq->cxqk", z_imag, z_real, cos_y, -sin_y)
    partial_value = jnp.stack([y_real, y_imag], axis=2).reshape(channels, cells_x, 2, KY * KZ)
    y_share = lax.psum_scatter(partial_value, "gy", scatter_dimension=3, tiled=True)
    x_real = times("cxm,xp->cpm", y_share[:, :, 0], y_share[:, :, 1], cos_x, sin_x)
    x_imag = times("cxm,xp->cpm", y_share[:, :, 1], y_share[:, :, 0], cos_x, -sin_x)
    x_partial = jnp.stack([x_real, x_imag], axis=1).reshape(channels, 2, KX * block_yz)
    owned_modes = lax.psum_scatter(x_partial, "gx", scatter_dimension=2, tiled=True)
    owned_modes = owned_modes * (1.0 / math.sqrt(length_x * length_y * length_z))
    coef_real = owned_modes[:, 0]
    coef_imag = owned_modes[:, 1]
    weight_real = mix_weight[0, :, :, 0, :]
    weight_imag = mix_weight[1, :, :, 0, :]
    mixed_real = times("oim,im->om", weight_real, weight_imag, coef_real, -coef_imag)
    mixed_imag = times("oim,im->om", weight_real, weight_imag, coef_imag, coef_real)
    mixed_modes = jnp.stack([mixed_real, mixed_imag], axis=1)
    row_modes = lax.all_gather(mixed_modes, "gx", axis=2, tiled=True).reshape(channels, 2, KX, block_yz)
    back_real = times("cpm,xp->cxm", row_modes[:, 0], row_modes[:, 1], cos_x, -sin_x)
    back_imag = times("cpm,xp->cxm", row_modes[:, 1], row_modes[:, 0], cos_x, sin_x)
    gathered = lax.all_gather(jnp.stack([back_real, back_imag], axis=2), "gy", axis=3, tiled=True)
    back_real = gathered[:, :, 0].reshape(channels, cells_x, KY, KZ)
    back_imag = gathered[:, :, 1].reshape(channels, cells_x, KY, KZ)
    plane_real = times("cxqk,yq->cxyk", back_real, back_imag, cos_y, -sin_y)
    plane_imag = times("cxqk,yq->cxyk", back_imag, back_real, cos_y, sin_y)
    table_back = jnp.concatenate([cos_z.T, -sin_z.T], axis=0)
    planes = jnp.concatenate([plane_real, plane_imag], axis=3)
    return jnp.dot(planes, table_back, precision=PRECISE) * (1.0 / math.sqrt(KX * KY * KZ))


class Plan:
    def __init__(self, feature_shape, count_gx, count_gy):
        self.channels, self.cells_x, self.cells_y, self.length_z = feature_shape
        self.count_gx, self.count_gy = count_gx, count_gy
        self.outer = count_gx // 2
        self.block = KY * KZ // count_gy
        self.part = self.block // 2
        self.per_gx = KX // count_gx
        self.rows = 2 * self.part
        self.pad_k = -(-KZ // 8) * 8
        self.pad_z = 2 * self.pad_k
        self.turns = self.part // KZ
        self.length_x = self.cells_x * count_gx
        self.length_y = self.cells_y * count_gy

    def spot(self, place):
        return place[0] // self.count_gy, place[0] % self.count_gy

    @staticmethod
    def fits(feature_shape, count_gx, count_gy):
        channels, cells_x, cells_y, length_z = feature_shape
        outer = count_gx // 2
        if count_gy != 4 or count_gx < 4 or count_gx % 2 or outer & (outer - 1) or outer > 4:
            return False
        if KX % count_gx or (KY * KZ) % (2 * count_gy) or channels * cells_x != LANES:
            return False
        part = KY * KZ // count_gy // 2
        per = KX // count_gx
        return (
            length_z == LANES
            and cells_x >= 4
            and cells_x % 2 == 0
            and cells_y % (LANES // (2 * (-(-KZ // 8) * 8))) == 0
            and channels % 16 == 0
            and (2 * part) % 8 == 0
            and 4 * 2 * part % 16 == 0
            and part % KZ == 0
            and per * part <= LANES
            and 2 * per * channels <= LANES
            and 2 * per * part <= 2 * LANES
            and 2 * part <= LANES
        )

    def table_z(self):
        table = np.zeros((2, self.pad_k, self.length_z))
        angle = angles_np(np.arange(KZ), np.arange(self.length_z), self.length_z)
        table[0, :KZ] = np.cos(angle)
        table[1, :KZ] = -np.sin(angle)
        return table.reshape(self.pad_z, self.length_z)

    def table_z_group(self):
        return np.kron(np.eye(LANES // self.pad_z), self.table_z())

    def trig_z(self):
        shape = (self.pad_z, self.length_z)
        row, z = (lax.broadcasted_iota(jnp.int32, shape, n) for n in range(2))
        k, imag = row % self.pad_k, row // self.pad_k
        turn = k * z % self.length_z
        turn = jnp.where(imag == 1, turn + self.length_z // 4, turn) % self.length_z
        value = jnp.cos(turn.astype(F32) * (2.0 * math.pi / self.length_z))
        return jnp.where(k < KZ, value, 0.0)

    def half_of(self, gx, gy):
        return (gy + gy // 2 + gx // 2 + gx) % 2

    def trig_y(self, gx, gy, turned):
        shape = (16 * self.turns, 2 * self.cells_y)
        row, col = (lax.broadcasted_iota(jnp.int32, shape[::-1] if turned else shape, n ^ int(turned)) for n in range(2))
        offset = row // (2 * self.turns)
        y_bit = (gy // 2 + offset // 2) % 2
        owner = (y_bit * 2 + (self.half_of(gx, gy) + offset // 4) % 2) * 2 + (gx + offset) % 2
        mode = owner * self.turns + row % self.turns
        kept = jnp.where(mode < KY // 2, mode, self.length_y - KY + mode)
        turn = kept * (gy * self.cells_y + col // 2) % self.length_y
        quarter = self.length_y // 4
        out_part, in_part = row // self.turns % 2, col % 2
        shift = jnp.where(out_part == in_part, 0, jnp.where(out_part == 0, 3 * quarter, quarter))
        return jnp.cos(((turn + shift) % self.length_y).astype(F32) * (2.0 * math.pi / self.length_y))

    def trig_x(self, gx, inverse):
        modes, places = self.outer * 2 * self.per_gx, 2 * self.cells_x
        shape = (places, 2 * modes) if inverse else (modes, 2 * places)
        row, col = (lax.broadcasted_iota(jnp.int32, shape, n) for n in range(2))
        width = modes if inverse else places
        crossed = col // width
        mode, at = (col % width, row) if inverse else (row, col % width)
        outer, pair = gx // 2, gx % 2
        offset, inner = mode // (2 * self.per_gx), mode % (2 * self.per_gx)
        other = jnp.zeros_like(offset)
        for s in range(self.outer):
            other = jnp.where(offset == s, outer ^ s, other)
        index = (2 * other + (pair + inner // self.per_gx) % 2) * self.per_gx + inner % self.per_gx
        kept = jnp.where(index < KX // 2, index, self.length_x - KX + index)
        far = (2 * outer + 1 - pair) * self.cells_x + at - self.cells_x
        x = jnp.where(at < self.cells_x, gx * self.cells_x + at, far)
        turn = kept * x % self.length_x
        turn = (turn + jnp.where(crossed == 1, 3 * (self.length_x // 4), 0)) % self.length_x
        return jnp.cos(turn.astype(F32) * (2.0 * math.pi / self.length_x))


def tripled_table(table):
    high, low = table_halves(table)
    return np.concatenate([high, high, low], axis=-1)


def forward_kernel(plan, place, feat, keep, send, own_h, own_l, near_x, far_x, far_y, field):
    channels, cells_x, cells_y = plan.channels, plan.cells_x, plan.cells_y
    gx, gy = plan.spot(place)
    even_x, even_y = gx % 2 == 0, gy % 2 == 0
    pad = plan.pad_z
    z_table = triple(halves(plan.trig_z()), 1, False)
    ends = []
    for y in range(cells_y):
        plane = [feat[pl.ds(x * cells_y + y, channels, stride=cells_x * cells_y), :] for x in range(cells_x)]
        near_x[y] = jnp.where(even_x, plane[-1], plane[0])
        far_x[y] = jnp.where(even_x, plane[0], plane[-1])
        plane = jnp.concatenate(plane, axis=0)
        if y in (0, cells_y - 1):
            ends.append(plane)
        high, low = halves(plane)
        own_h[y] = high.reshape(cells_x, channels, -1)
        own_l[y] = low.reshape(cells_x, channels, -1)
        field[y * pad : (y + 1) * pad, :] = dot(z_table, triple((high, low), 1, True), NT)
    y_table = triple(halves(plan.trig_y(gx, gy, False)), 1, False)
    half = 8 * plan.turns
    for k in range(KZ):
        value = halves(field[pl.ds(k, 2 * cells_y, stride=plan.pad_k), :])
        value = dot(y_table, triple(value, 0, True))
        keep[pl.ds(k, half, stride=KZ), :] = value[:half]
        send[pl.ds(k, half, stride=KZ), :] = value[half:]
    start = half * KZ
    send[start:, :] = jnp.where(even_y, ends[1], ends[0])
    far_y[...] = jnp.where(even_y, ends[0], ends[1])


def forward_modes(plan, place, features):
    half, length_z = 4 * plan.rows, plan.length_z
    own = jax.ShapeDtypeStruct((plan.cells_y, plan.cells_x, plan.channels, length_z), BF16)
    face = jax.ShapeDtypeStruct((plan.cells_y, plan.channels, length_z), F32)
    shape = lambda *s: jax.ShapeDtypeStruct(s, F32)
    return kernel_call(
        functools.partial(forward_kernel, plan),
        [shape(half, LANES), shape(half + LANES, LANES), own, own, face, face, shape(LANES, LANES)],
        [pltpu.VMEM((plan.cells_y * plan.pad_z, LANES), F32)],
        in_specs=specs(1),
    )(place, features.reshape(-1, length_z))


def turned(value, part, sign):
    lane = lax.broadcasted_iota(jnp.int32, value.shape, 1)
    low = pltpu.roll(value, LANES - part, 1)
    high = pltpu.roll(value, part, 1)
    return jnp.where(lane < part, sign * low, -sign * high)


def square_turned(value):
    return jnp.concatenate([value, jnp.zeros((LANES - value.shape[0], LANES), F32)], axis=0).T


def x_forward_kernel(plan, place, own, from_x, from_y, from_xy, *refs):
    outs = refs[: plan.outer]
    straight, crossed, found = refs[plan.outer :]
    rows, channels, per = plan.rows, plan.channels, 2 * plan.per_gx
    near = own[...] + from_y[:rows, :]
    far = from_x[...] + from_xy[...]
    for at, value in enumerate((near, far)):
        value = square_turned(value)
        straight[at * LANES : (at + 1) * LANES, :] = value
        crossed[at * LANES : (at + 1) * LANES, :] = turned(value, plan.part, 1.0)
    factor = triple(halves(plan.trig_x(plan.spot(place)[0], False)), 1, False)
    for c in range(channels):
        index = pl.ds(c, 2 * plan.cells_x, stride=channels)
        value = halves(jnp.concatenate([straight[index, :], crossed[index, :]], axis=0))
        found[pl.ds(c, plan.outer * per, stride=channels), :] = dot(factor, triple(value, 0, True))
    for at, out in enumerate(outs):
        size = per * channels
        out[...] = square_turned(found[at * size : (at + 1) * size, :])[:rows]


def x_inverse_kernel(plan, place, *refs):
    parts = refs[: plan.outer]
    near, far, straight, crossed, found = refs[plan.outer :]
    rows, channels, per = plan.rows, plan.channels, 2 * plan.per_gx
    size = per * channels
    for at, part in enumerate(parts):
        value = square_turned(part[...])[:size]
        straight[at * size : (at + 1) * size, :] = value
        crossed[at * size : (at + 1) * size, :] = turned(value, plan.part, -1.0)
    factor = triple(halves(plan.trig_x(plan.spot(place)[0], True)), 1, False)
    for c in range(channels):
        index = pl.ds(c, plan.outer * per, stride=channels)
        value = halves(jnp.concatenate([straight[index, :], crossed[index, :]], axis=0))
        found[pl.ds(c, 2 * plan.cells_x, stride=channels), :] = dot(factor, triple(value, 0, True))
    for at, out in enumerate((near, far)):
        out[...] = found[at * LANES : (at + 1) * LANES, :].T[:rows]


def x_forward(plan, place, parts):
    part = jax.ShapeDtypeStruct((plan.rows, LANES), F32)
    size = plan.outer * 2 * plan.per_gx * plan.channels
    scratch = [pltpu.VMEM((n, LANES), F32) for n in (2 * LANES, 2 * LANES, size)]
    body = functools.partial(x_forward_kernel, plan)
    return kernel_call(body, [part] * plan.outer, scratch, in_specs=specs(4))(place, *parts)


def x_inverse(plan, place, parts):
    part = jax.ShapeDtypeStruct((plan.rows, LANES), F32)
    size = plan.outer * 2 * plan.per_gx * plan.channels
    scratch = [pltpu.VMEM((n, LANES), F32) for n in (size, size, 2 * LANES)]
    body = functools.partial(x_inverse_kernel, plan)
    return kernel_call(body, [part] * 2, scratch, in_specs=specs(plan.outer))(place, *parts)


def weight_kernel(plan, place, weight, out, flat, sem):
    copy = pltpu.make_async_copy(weight.at[:, :, 0, :], flat, sem)
    copy.start()
    copy.wait()
    part, block = plan.part, plan.block
    square = plan.channels * plan.channels
    lane = lax.broadcasted_iota(jnp.int32, (square, LANES), 1)
    width = 2 * LANES
    held = flat.shape[2]
    even = plan.spot(place)[0] % 2 == 0
    for which in range(2):
        high = jnp.concatenate([flat[which, :, LANES:], jnp.zeros((square, width - held), F32)], axis=1)
        value = jnp.concatenate([flat[which, :, :LANES], high], axis=1)
        choice = []
        for half in range(2):
            total = jnp.zeros((square, LANES), F32)
            for j in range(plan.per_gx):
                shift = (j * part - j * block - half * part) % width
                moved = value if shift == 0 else pltpu.roll(value, shift, 1)
                inside = (lane >= j * part) & (lane < (j + 1) * part)
                total = jnp.where(inside, moved[:, :LANES], total)
            choice.append(total)
        at = slice(which * square, (which + 1) * square)
        out[at, :] = jnp.where(even, choice[0], choice[1])
        out[slice(at.start + 2 * square, at.stop + 2 * square), :] = jnp.where(even, choice[1], choice[0])


def weight_parts(plan, place, mix_weight):
    square = plan.channels * plan.channels
    modes = mix_weight.shape[-1]
    return kernel_call(
        functools.partial(weight_kernel, plan),
        jax.ShapeDtypeStruct((4 * square, LANES), F32),
        [pltpu.VMEM((2, square, modes), F32), pltpu.SemaphoreType.DMA],
        in_specs=specs(1),
    )(place, mix_weight.reshape(2, square, 1, modes))


def faces_kernel(plan, place, near_x, far_x, near_y, far_y, after, to_near, to_far):
    channels, cells_x, cells_y = plan.channels, plan.cells_x, plan.cells_y
    even = plan.spot(place)[0] % 2 == 0
    last = cells_x - 1
    for out, face, x in ((to_near, near_x, jnp.where(even, last, 0)), (to_far, far_x, jnp.where(even, 0, last))):
        for y in range(cells_y):
            out[y * channels : (y + 1) * channels, :] = face[y]
        for n, ref in enumerate((near_y, far_y)):
            at = pl.multiple_of(ref.shape[0] - LANES + x * channels, channels)
            start = (cells_y + n) * channels
            out[start : start + channels, :] = ref[pl.ds(at, channels), :]


def faces(plan, place, near_x, far_x, near_y, far_y, after):
    out = jax.ShapeDtypeStruct(((plan.cells_y + 2) * plan.channels, LANES), F32)
    return kernel_call(functools.partial(faces_kernel, plan), [out, out], in_specs=specs(5))(
        place, near_x, far_x, near_y, far_y, after
    )


def mix_kernel(plan, *refs):
    parts = refs[: plan.outer]
    near, far, _, out = refs[plan.outer :]
    channels, part, per, rows = plan.channels, plan.part, plan.per_gx, plan.rows
    total = parts[0][...]
    for p in parts[1:]:
        total = total + p[...]
    scale = 1.0 / math.sqrt(plan.length_x * plan.length_y * plan.length_z) / math.sqrt(KX * KY * KZ)
    total = jnp.concatenate([total * scale, jnp.zeros((LANES - rows, LANES), F32)], axis=0).T
    lane = lax.broadcasted_iota(jnp.int32, (channels, LANES), 1)

    def moved(value, shift):
        return value if shift % LANES == 0 else pltpu.roll(value, shift % LANES, 1)

    def collect(half, which):
        value = jnp.zeros((channels, LANES), F32)
        for j in range(per):
            at = (half * per + j) * channels
            piece = moved(total[at : at + channels], (j - which) * part)
            value = jnp.where((lane >= j * part) & (lane < (j + 1) * part), piece, value)
        return value

    blocks = []
    for half, weight in enumerate((near, far)):
        c_real, c_imag = collect(half, 0), collect(half, 1)
        real = jnp.zeros((channels, LANES), F32)
        imag = jnp.zeros((channels, LANES), F32)
        for i in range(channels):
            w_real = weight[pl.ds(i, channels, stride=channels), :]
            w_imag = weight[pl.ds(channels * channels + i, channels, stride=channels), :]
            a, b = c_real[i : i + 1], c_imag[i : i + 1]
            real = real + (w_real * a - w_imag * b)
            imag = imag + (w_real * b + w_imag * a)
        for j in range(per):
            low = moved(real, -j * part)
            high = moved(imag, part - j * part)
            blocks.append(jnp.where(lane < part, low, jnp.where(lane < 2 * part, high, 0.0)))
    fill = LANES - 2 * per * channels
    if fill:
        blocks.append(jnp.zeros((fill, LANES), F32))
    out[...] = jnp.concatenate(blocks, axis=0).T[:rows]


def mix_modes(plan, parts, near, far, before):
    return kernel_call(functools.partial(mix_kernel, plan), jax.ShapeDtypeStruct((plan.rows, LANES), F32))(
        *parts, near, far, before
    )


def final_kernel(plan, place, own, other, outer, inner, table_z, out, field, ready, sems):
    channels, cells_x, cells_y = plan.channels, plan.cells_x, plan.cells_y
    pieces = ready.shape[0]
    deep = cells_y // pieces
    copies = [pltpu.make_async_copy(ready.at[n], out.at[:, pl.ds(n * deep, deep), :], sems.at[n]) for n in range(pieces)]
    gx, gy = plan.spot(place)
    y_table = triple(halves(plan.trig_y(gx, gy, True)), 1, False)
    half = 8 * plan.turns
    field[...] = jnp.zeros(field.shape, F32)
    for k in range(KZ):
        parts = [ref[pl.ds(k, half, stride=KZ), :] for ref in (own, other)]
        value = halves(jnp.concatenate(parts, axis=0))
        field[pl.ds(k, 2 * cells_y, stride=plan.pad_k), :] = dot(y_table, triple(value, 0, True))
    z_table = table_z[...]
    group = LANES // plan.pad_z
    for g in range(cells_y // group):
        planes = halves(field[g * LANES : (g + 1) * LANES, :].T)
        value = dot(triple(planes, 1, False), z_table)
        for k in range(group):
            y = g * group + k
            conv = [outer[0, y]] + [inner[x, y] for x in range(inner.shape[0])] + [outer[1, y]]
            layer = jnp.concatenate(conv, axis=0) + value[:, k * LANES : (k + 1) * LANES]
            layer = layer * 0.5 * (1.0 + lax.erf(layer * math.sqrt(0.5)))
            flat = ready.at[y // deep].reshape(channels * cells_x * deep, plan.length_z)
            for x in range(cells_x):
                flat[pl.ds(x * deep + y % deep, channels, stride=cells_x * deep), :] = layer[x * channels : (x + 1) * channels]
            if y % deep == deep - 1:
                copies[y // deep].start()
    for copy in copies:
        copy.wait()


def final_layer(plan, place, own, other, convs):
    high, low = table_halves(plan.table_z_group())
    table_z = np.concatenate([high, low, high], axis=0)
    shape = (plan.channels, plan.cells_x, plan.cells_y, plan.length_z)
    flat = (plan.channels * plan.cells_x, plan.cells_y, plan.length_z)
    pieces = plan.cells_y // 8
    ready = pltpu.VMEM((pieces, plan.channels * plan.cells_x, 8, plan.length_z), F32)
    return kernel_call(
        functools.partial(final_kernel, plan),
        jax.ShapeDtypeStruct(flat, F32),
        [pltpu.VMEM((plan.cells_y * plan.pad_z, LANES), F32), ready, pltpu.SemaphoreType.DMA((pieces,))],
        in_specs=specs(5),
        out_specs=pl.BlockSpec(memory_space=pltpu.HBM),
    )(place, own, other, *convs, table_z).reshape(shape)


def swap(plan, value, outer=0, pair=0, yy=0, core=0):
    perm = []
    for gx in range(plan.count_gx):
        for gy in range(plan.count_gy):
            to_gx = gx ^ (outer * 2 + pair)
            to_gy = gy ^ (yy * 2 + core)
            perm.append((gx * plan.count_gy + gy, to_gx * plan.count_gy + to_gy))
    return lax.ppermute(value, ("gx", "gy"), perm)


def next_pair(value, axis):
    size = lax.axis_size(axis)
    return lax.ppermute(value, axis, [(i, (i + (1 if i % 2 else -1)) % size) for i in range(size)])


def after(value, *others):
    zero = sum(jnp.minimum(jnp.abs(other[:1]), 0.0) for other in others)
    return value + zero


def layer_paired(plan, features, conv_weight, mix_weight):
    rows = plan.rows
    place = (lax.axis_index("gx") * plan.count_gy + lax.axis_index("gy")).astype(jnp.int32).reshape(1)
    cells_x = features.shape[1]

    keep, send, own_h, own_l, near_x, far_x, far_y = forward_modes(plan, place, features)
    both = weight_parts(plan, place, mix_weight)
    exchanged = swap(plan, both, core=1)
    at_gx, at_gy = lax.axis_index("gx"), lax.axis_index("gy")
    both = jnp.where(plan.half_of(at_gx, at_gy) == at_gy % 2, both, exchanged)
    weight, away = both[: both.shape[0] // 2], both[both.shape[0] // 2 :]
    near_y = swap(plan, send, core=1)
    sums = [keep[s * rows : (s + 1) * rows] + near_y[s * rows : (s + 1) * rows] for s in range(4)]
    far_y = swap(plan, jnp.concatenate([sums[2], far_y], axis=0), yy=1, core=1)
    from_x = swap(plan, sums[1], pair=1, core=1)
    from_xy = swap(plan, sums[3], pair=1, yy=1)
    away = after(away, from_x, far_y, from_xy)
    far_weight = swap(plan, away, pair=1, core=1)
    chunks = x_forward(plan, place, [sums[0], from_x, far_y, from_xy])
    got = {s: swap(plan, chunks[s], outer=s, core=s % 2) for s in range(plan.outer - 1, 0, -1)}
    parts = [chunks[0]] + [got[s] for s in (*range(2, plan.outer), 1)]
    taps = conv_taps(conv_weight)
    mixed = mix_modes(plan, parts, weight, far_weight, taps)
    to_near, to_far = faces(plan, place, near_x, far_x, near_y, far_y, chunks[0])
    near_x = swap(plan, after(to_near, mixed), pair=1)
    far_x = next_pair(to_far, "gx")
    got = {s: swap(plan, mixed, outer=s, core=s % 2) for s in range(plan.outer - 1, 0, -1)}
    parts = [mixed] + [got[s] for s in range(1, plan.outer)]
    args = (near_x, far_x, near_y, far_y, taps)
    mine, theirs = x_inverse(plan, place, parts)
    from_x = swap(plan, theirs, pair=1, core=1)
    from_y = swap(plan, mine, yy=1, core=1)
    from_xy = swap(plan, theirs, pair=1, yy=1)
    inner, token = conv_bricks(place, (own_h, own_l), near_y, near_y, *args[2:], mine, range(1, cells_x - 1), True)
    (outer,) = conv_bricks(place, (own_h, own_l), *args, mine, (0, cells_x - 1))
    own = jnp.concatenate([mine + token[:1], from_x, from_y, from_xy], axis=0)
    other = swap(plan, own, core=1)
    return final_layer(plan, place, own, other, (outer, inner))


def layer_any(features, conv_weight, mix_weight):
    channels, cells_x, cells_y, length_z = features.shape
    own = jax.ShapeDtypeStruct((cells_y, cells_x, channels, length_z), BF16)
    own = kernel_call(split_kernel, [own, own])(features)
    taps = conv_taps(conv_weight)
    (conv,) = conv_bricks(jnp.zeros((1,), jnp.int32), own, *halos(features), taps, taps, range(cells_x))
    return jax.nn.gelu(conv.transpose(2, 0, 1, 3) + spectral_any(features, mix_weight), approximate=False)


def shards(features, conv_weight, mix_weight):
    counts = lax.axis_size("gx"), lax.axis_size("gy")
    if Plan.fits(features.shape, *counts):
        return layer_paired(Plan(features.shape, *counts), features, conv_weight, mix_weight)
    return layer_any(features, conv_weight, mix_weight)


def solution(mesh):
    in_specs = (P(None, "gx", "gy", None), P(), P(None, None, None, "gy", "gx"))
    out_specs = P(None, "gx", "gy", None)
    return jax.shard_map(shards, mesh=mesh, in_specs=in_specs, out_specs=out_specs, check_vma=False)
```

```python
import functools
import math

import jax
import jax.numpy as jnp
import ml_dtypes
import numpy as np
from jax import lax
from jax.experimental import pallas as pl
from jax.experimental.pallas import tpu as pltpu
from jax.sharding import PartitionSpec as P

KX = 24
KY = 24
KZ = 12
LANES = 128
F32 = jnp.float32
BF16 = jnp.bfloat16
PRECISE = lax.Precision.HIGHEST
VMEM_LIMIT = 24 * 1024 * 1024
NN = (((1,), (0,)), ((), ()))
NT = (((1,), (1,)), ((), ()))


def kernel_call(body, out_shape, scratch=(), grid_spec=None, **kw):
    params = pltpu.CompilerParams(vmem_limit_bytes=VMEM_LIMIT)
    if grid_spec is not None:
        kw["grid_spec"] = grid_spec
    else:
        kw["scratch_shapes"] = list(scratch)
    return pl.pallas_call(body, out_shape=out_shape, compiler_params=params, **kw)


def halves(value):
    high = value.astype(BF16)
    return high, (value - high.astype(F32)).astype(BF16)


def dot(a, b, dims=NN):
    return lax.dot_general(a, b, dims, preferred_element_type=F32)


def dot3(a, b, dims=NN):
    return dot(a[0], b[0], dims) + (dot(a[0], b[1], dims) + dot(a[1], b[0], dims))


def table_halves(table):
    table = np.asarray(table, np.float64)
    high = table.astype(ml_dtypes.bfloat16)
    low = (table - high.astype(np.float64)).astype(ml_dtypes.bfloat16)
    return high, low


def triple(parts, axis, twice_high_around):
    high, low = parts
    return jnp.concatenate([high, low, high] if twice_high_around else [high, high, low], axis=axis)


def kept_np(amount, length):
    index = np.arange(amount)
    return np.where(index < amount // 2, index, length - amount + index)


def angles_np(positions, frequencies, length):
    return 2.0 * np.pi * ((positions[:, None] * frequencies[None, :]) % length) / length


def split_kernel(feat, high, low):
    channels, cells_x, cells_y, length_z = feat.shape
    for x in range(cells_x):
        for y in range(cells_y):
            high[y, x], low[y, x] = halves(feat[:, x, y, :])


def conv_kernel(columns, rows_y, count_gy, place, own_h, own_l, near_x, far_x, near_y, far_y, weight, after, out, *refs):
    tokens, (edge_h, edge_l, rim_h, rim_l) = refs[:-4], refs[-4:]
    cells_y, cells_x, channels, length_z = own_h.shape
    needed = sorted({x + a for x in columns for a in range(3)})
    span = rows_y + 2
    depth = 3 * span * channels
    even_x, even_y = place[0] // count_gy % 2 == 0, place[0] % count_gy % 2 == 0
    column, row = (cells_y + 2) * channels, cells_x * channels

    def tail(ref, size, at):
        return ref[ref.shape[0] - size + at : ref.shape[0] - size + at + channels, :]

    def pick(side, even, near, far, size, at):
        near, far = (tail(ref, size, at * channels) for ref in (near, far))
        return halves(jnp.where(even, near, far) if side else jnp.where(even, far, near))

    for side in range(2):
        if (0, cells_x + 1)[side] in needed:
            for y in range(cells_y):
                edge_h[side, y + 1], edge_l[side, y + 1] = pick(side, even_x, near_x, far_x, column, y)
            corners = [
                jnp.where(even_x == bool(side), *(tail(ref, column, (cells_y + n) * channels) for ref in (near_x, far_x)))
                for n in range(2)
            ]
            for up in range(2):
                value = jnp.where(even_y == bool(up), *corners)
                edge_h[side, up * (cells_y + 1)], edge_l[side, up * (cells_y + 1)] = halves(value)
        for x in [n - 1 for n in needed if 0 < n <= cells_x]:
            rim_h[side, x], rim_l[side, x] = pick(side, even_y, near_y, far_y, row, x)

    def cell(which, x, y):
        own, edge, rim = ((own_h, edge_h, rim_h), (own_l, edge_l, rim_l))[which]
        if x in (0, cells_x + 1):
            return edge[0 if x == 0 else 1, y]
        if y in (0, cells_y + 1):
            return rim[0 if y == 0 else 1, x - 1]
        return own[y - 1, x - 1]

    taps = halves(weight[...])
    tap = lax.broadcasted_iota(jnp.int32, (weight.shape[1], depth), 0)
    at = lax.broadcasted_iota(jnp.int32, (weight.shape[1], depth), 1)
    tap_a, tap_b, tap_i = tap // (3 * channels), tap // channels % 3, tap % channels
    at_a, at_y, at_i = at // (span * channels), at // channels % span, at % channels
    bands = [[], []]
    for y in range(rows_y):
        match = (tap_a == at_a) & (tap_b + y == at_y) & (tap_i == at_i)
        match = jnp.where(match, 1.0, 0.0).astype(BF16)
        for which in range(2):
            bands[which].append(dot(taps[which], match).astype(BF16))
    bands = [jnp.concatenate(b, axis=0) for b in bands]
    for n in range(0, len(columns), 2):
        for y in range(0, cells_y, rows_y):
            field = []
            for which in range(2):
                lanes = []
                for p in range(2):
                    cells = [cell(which, columns[n + p] + a, y + k) for a in range(3) for k in range(span)]
                    lanes.append(jnp.concatenate(cells, axis=0))
                field.append(jnp.concatenate(lanes, axis=1))
            value = dot3(bands, field)
            for k in range(rows_y):
                for p in range(2):
                    total = None
                    for c in range(3):
                        row = (k * 3 + c) * channels
                        piece = value[row : row + channels, p * length_z : (p + 1) * length_z]
                        if c != 1:
                            piece = pltpu.roll(piece, (1 - c) % length_z, 1)
                        total = piece if total is None else total + piece
                    out[n + p, y + k] = total
    for token in tokens:
        token[...] = jnp.zeros(token.shape, F32)


def conv_taps(conv_weight):
    channels = conv_weight.shape[1]
    taps = conv_weight.reshape(3, 3, 3, channels, channels).transpose(2, 3, 0, 1, 4)
    return taps.reshape(3 * channels, 9 * channels)


def specs(count, first=None):
    vmem = pl.BlockSpec(memory_space=pltpu.VMEM)
    return [pl.BlockSpec(memory_space=pltpu.SMEM)] + [vmem] * count


def conv_bricks(place, own, near_x, far_x, near_y, far_y, taps, after, columns, mark=False):
    cells_y, cells_x, channels, length_z = own[0].shape
    outs = [jax.ShapeDtypeStruct((len(columns), cells_y, channels, length_z), F32)]
    if mark:
        outs.append(jax.ShapeDtypeStruct((8, length_z), F32))
    return kernel_call(
        functools.partial(conv_kernel, tuple(columns), 2, lax.axis_size("gy")),
        outs,
        [pltpu.VMEM((2, cells_y + 2, channels, length_z), BF16)] * 2 + [pltpu.VMEM((2, cells_x, channels, length_z), BF16)] * 2,
        in_specs=specs(8),
    )(place, *own, near_x, far_x, near_y, far_y, taps, after)


def ring(value, axis, step):
    size = lax.axis_size(axis)
    return lax.ppermute(value, axis, [(i, (i + step) % size) for i in range(size)])


def halos(features):
    channels, cells_x, cells_y, length_z = features.shape
    flat = lambda v: v.transpose(1, 0, 2).reshape(-1, length_z)
    low_y = ring(features[:, :, cells_y - 1], "gy", 1)
    high_y = ring(features[:, :, 0], "gy", -1)

    def face(x):
        return jnp.concatenate([features[:, x], high_y[:, x][:, None], low_y[:, x][:, None]], axis=1)

    low_x = ring(face(cells_x - 1), "gx", 1)
    high_x = ring(face(0), "gx", -1)
    return flat(high_x), flat(low_x), flat(high_y), flat(low_y)


def angle_tables(positions, frequencies, length):
    product = positions[:, None] * frequencies[None, :] % length
    angles = product.astype(jnp.float32) * (2.0 * math.pi / length)
    return (jnp.cos(angles), jnp.sin(angles))


def kept_frequencies(amount, length):
    index = jnp.arange(amount, dtype=jnp.int32)
    return jnp.where(index < amount // 2, index, length - amount + index)


def times(form, a, b, c, d):
    one = functools.partial(jnp.einsum, form, precision=PRECISE)
    return one(a, c) + one(b, d)


def spectral_any(features, mix_weight):
    channels, cells_x, cells_y, length_z = features.shape
    count_gx = lax.axis_size("gx")
    count_gy = lax.axis_size("gy")
    length_x = cells_x * count_gx
    length_y = cells_y * count_gy
    block_yz = KY * KZ // count_gy
    cos_z, sin_z = angle_tables(jnp.arange(length_z, dtype=jnp.int32), jnp.arange(KZ, dtype=jnp.int32), length_z)
    y_places = lax.axis_index("gy") * cells_y + jnp.arange(cells_y, dtype=jnp.int32)
    x_places = lax.axis_index("gx") * cells_x + jnp.arange(cells_x, dtype=jnp.int32)
    cos_y, sin_y = angle_tables(y_places, kept_frequencies(KY, length_y), length_y)
    cos_x, sin_x = angle_tables(x_places, kept_frequencies(KX, length_x), length_x)
    along_z = jnp.dot(features, jnp.concatenate([cos_z, -sin_z], axis=1), precision=PRECISE)
    z_real = along_z[..., :KZ]
    z_imag = along_z[..., KZ:]
    y_real = times("cxyk,yq->cxqk", z_real, z_imag, cos_y, sin_y)
    y_imag = times("cxyk,yq->cxqk", z_imag, z_real, cos_y, -sin_y)
    partial_value = jnp.stack([y_real, y_imag], axis=2).reshape(channels, cells_x, 2, KY * KZ)
    y_share = lax.psum_scatter(partial_value, "gy", scatter_dimension=3, tiled=True)
    x_real = times("cxm,xp->cpm", y_share[:, :, 0], y_share[:, :, 1], cos_x, sin_x)
    x_imag = times("cxm,xp->cpm", y_share[:, :, 1], y_share[:, :, 0], cos_x, -sin_x)
    x_partial = jnp.stack([x_real, x_imag], axis=1).reshape(channels, 2, KX * block_yz)
    owned_modes = lax.psum_scatter(x_partial, "gx", scatter_dimension=2, tiled=True)
    owned_modes = owned_modes * (1.0 / math.sqrt(length_x * length_y * length_z))
    coef_real = owned_modes[:, 0]
    coef_imag = owned_modes[:, 1]
    weight_real = mix_weight[0, :, :, 0, :]
    weight_imag = mix_weight[1, :, :, 0, :]
    mixed_real = times("oim,im->om", weight_real, weight_imag, coef_real, -coef_imag)
    mixed_imag = times("oim,im->om", weight_real, weight_imag, coef_imag, coef_real)
    mixed_modes = jnp.stack([mixed_real, mixed_imag], axis=1)
    row_modes = lax.all_gather(mixed_modes, "gx", axis=2, tiled=True).reshape(channels, 2, KX, block_yz)
    back_real = times("cpm,xp->cxm", row_modes[:, 0], row_modes[:, 1], cos_x, -sin_x)
    back_imag = times("cpm,xp->cxm", row_modes[:, 1], row_modes[:, 0], cos_x, sin_x)
    gathered = lax.all_gather(jnp.stack([back_real, back_imag], axis=2), "gy", axis=3, tiled=True)
    back_real = gathered[:, :, 0].reshape(channels, cells_x, KY, KZ)
    back_imag = gathered[:, :, 1].reshape(channels, cells_x, KY, KZ)
    plane_real = times("cxqk,yq->cxyk", back_real, back_imag, cos_y, -sin_y)
    plane_imag = times("cxqk,yq->cxyk", back_imag, back_real, cos_y, sin_y)
    table_back = jnp.concatenate([cos_z.T, -sin_z.T], axis=0)
    planes = jnp.concatenate([plane_real, plane_imag], axis=3)
    return jnp.dot(planes, table_back, precision=PRECISE) * (1.0 / math.sqrt(KX * KY * KZ))


class Plan:
    def __init__(self, feature_shape, count_gx, count_gy):
        self.channels, self.cells_x, self.cells_y, self.length_z = feature_shape
        self.count_gx, self.count_gy = count_gx, count_gy
        self.outer = count_gx // 2
        self.block = KY * KZ // count_gy
        self.part = self.block // 2
        self.per_gx = KX // count_gx
        self.rows = 2 * self.part
        self.pad_k = -(-KZ // 8) * 8
        self.pad_z = 2 * self.pad_k
        self.turns = self.part // KZ
        self.length_x = self.cells_x * count_gx
        self.length_y = self.cells_y * count_gy

    def spot(self, place):
        return place[0] // self.count_gy, place[0] % self.count_gy

    @staticmethod
    def fits(feature_shape, count_gx, count_gy):
        channels, cells_x, cells_y, length_z = feature_shape
        outer = count_gx // 2
        if count_gy != 4 or count_gx < 4 or count_gx % 2 or outer & (outer - 1) or outer > 4:
            return False
        if KX % count_gx or (KY * KZ) % (2 * count_gy) or channels * cells_x != LANES:
            return False
        part = KY * KZ // count_gy // 2
        per = KX // count_gx
        return (
            length_z == LANES
            and cells_x >= 4
            and cells_x % 2 == 0
            and cells_y % (LANES // (2 * (-(-KZ // 8) * 8))) == 0
            and channels % 16 == 0
            and (2 * part) % 8 == 0
            and 4 * 2 * part % 16 == 0
            and part % KZ == 0
            and per * part <= LANES
            and 2 * per * channels <= LANES
            and 2 * per * part <= 2 * LANES
            and 2 * part <= LANES
        )

    def table_z(self):
        table = np.zeros((2, self.pad_k, self.length_z))
        angle = angles_np(np.arange(KZ), np.arange(self.length_z), self.length_z)
        table[0, :KZ] = np.cos(angle)
        table[1, :KZ] = -np.sin(angle)
        return table.reshape(self.pad_z, self.length_z)

    def table_z_group(self):
        return np.kron(np.eye(LANES // self.pad_z), self.table_z())

    def trig_z(self):
        shape = (self.pad_z, self.length_z)
        row, z = (lax.broadcasted_iota(jnp.int32, shape, n) for n in range(2))
        k, imag = row % self.pad_k, row // self.pad_k
        turn = k * z % self.length_z
        turn = jnp.where(imag == 1, turn + self.length_z // 4, turn) % self.length_z
        value = jnp.cos(turn.astype(F32) * (2.0 * math.pi / self.length_z))
        return jnp.where(k < KZ, value, 0.0)

    def half_of(self, gx, gy):
        return (gy + gy // 2 + gx // 2 + gx) % 2

    def trig_y(self, gx, gy, turned):
        shape = (16 * self.turns, 2 * self.cells_y)
        row, col = (lax.broadcasted_iota(jnp.int32, shape[::-1] if turned else shape, n ^ int(turned)) for n in range(2))
        offset = row // (2 * self.turns)
        y_bit = (gy // 2 + offset // 2) % 2
        owner = (y_bit * 2 + (self.half_of(gx, gy) + offset // 4) % 2) * 2 + (gx + offset) % 2
        mode = owner * self.turns + row % self.turns
        kept = jnp.where(mode < KY // 2, mode, self.length_y - KY + mode)
        turn = kept * (gy * self.cells_y + col // 2) % self.length_y
        quarter = self.length_y // 4
        out_part, in_part = row // self.turns % 2, col % 2
        shift = jnp.where(out_part == in_part, 0, jnp.where(out_part == 0, 3 * quarter, quarter))
        return jnp.cos(((turn + shift) % self.length_y).astype(F32) * (2.0 * math.pi / self.length_y))

    def trig_x(self, gx, inverse):
        modes, places = self.outer * 2 * self.per_gx, 2 * self.cells_x
        shape = (places, 2 * modes) if inverse else (modes, 2 * places)
        row, col = (lax.broadcasted_iota(jnp.int32, shape, n) for n in range(2))
        width = modes if inverse else places
        crossed = col // width
        mode, at = (col % width, row) if inverse else (row, col % width)
        outer, pair = gx // 2, gx % 2
        offset, inner = mode // (2 * self.per_gx), mode % (2 * self.per_gx)
        other = jnp.zeros_like(offset)
        for s in range(self.outer):
            other = jnp.where(offset == s, outer ^ s, other)
        index = (2 * other + (pair + inner // self.per_gx) % 2) * self.per_gx + inner % self.per_gx
        kept = jnp.where(index < KX // 2, index, self.length_x - KX + index)
        far = (2 * outer + 1 - pair) * self.cells_x + at - self.cells_x
        x = jnp.where(at < self.cells_x, gx * self.cells_x + at, far)
        turn = kept * x % self.length_x
        turn = (turn + jnp.where(crossed == 1, 3 * (self.length_x // 4), 0)) % self.length_x
        return jnp.cos(turn.astype(F32) * (2.0 * math.pi / self.length_x))


def tripled_table(table):
    high, low = table_halves(table)
    return np.concatenate([high, high, low], axis=-1)


def forward_kernel(plan, place, feat, keep, send, own_h, own_l, near_x, far_x, far_y, field):
    channels, cells_x, cells_y = plan.channels, plan.cells_x, plan.cells_y
    gx, gy = plan.spot(place)
    even_x, even_y = gx % 2 == 0, gy % 2 == 0
    pad = plan.pad_z
    z_table = triple(halves(plan.trig_z()), 1, False)
    ends = []
    for y in range(cells_y):
        plane = [feat[pl.ds(x * cells_y + y, channels, stride=cells_x * cells_y), :] for x in range(cells_x)]
        near_x[y] = jnp.where(even_x, plane[-1], plane[0])
        far_x[y] = jnp.where(even_x, plane[0], plane[-1])
        plane = jnp.concatenate(plane, axis=0)
        if y in (0, cells_y - 1):
            ends.append(plane)
        high, low = halves(plane)
        own_h[y] = high.reshape(cells_x, channels, -1)
        own_l[y] = low.reshape(cells_x, channels, -1)
        field[y * pad : (y + 1) * pad, :] = dot(z_table, triple((high, low), 1, True), NT)
    y_table = triple(halves(plan.trig_y(gx, gy, False)), 1, False)
    half = 8 * plan.turns
    for k in range(KZ):
        value = halves(field[pl.ds(k, 2 * cells_y, stride=plan.pad_k), :])
        value = dot(y_table, triple(value, 0, True))
        keep[pl.ds(k, half, stride=KZ), :] = value[:half]
        send[pl.ds(k, half, stride=KZ), :] = value[half:]
    start = half * KZ
    send[start:, :] = jnp.where(even_y, ends[1], ends[0])
    far_y[...] = jnp.where(even_y, ends[0], ends[1])


def forward_modes(plan, place, features):
    half, length_z = 4 * plan.rows, plan.length_z
    own = jax.ShapeDtypeStruct((plan.cells_y, plan.cells_x, plan.channels, length_z), BF16)
    face = jax.ShapeDtypeStruct((plan.cells_y, plan.channels, length_z), F32)
    shape = lambda *s: jax.ShapeDtypeStruct(s, F32)
    return kernel_call(
        functools.partial(forward_kernel, plan),
        [shape(half, LANES), shape(half + LANES, LANES), own, own, face, face, shape(LANES, LANES)],
        [pltpu.VMEM((plan.cells_y * plan.pad_z, LANES), F32)],
        in_specs=specs(1),
    )(place, features.reshape(-1, length_z))


def turned(value, part, sign):
    lane = lax.broadcasted_iota(jnp.int32, value.shape, 1)
    low = pltpu.roll(value, LANES - part, 1)
    high = pltpu.roll(value, part, 1)
    return jnp.where(lane < part, sign * low, -sign * high)


def square_turned(value):
    return jnp.concatenate([value, jnp.zeros((LANES - value.shape[0], LANES), F32)], axis=0).T


def x_forward_kernel(plan, place, own, from_x, from_y, from_xy, *refs):
    outs = refs[: plan.outer]
    straight, crossed, found = refs[plan.outer :]
    rows, channels, per = plan.rows, plan.channels, 2 * plan.per_gx
    near = own[...] + from_y[:rows, :]
    far = from_x[...] + from_xy[...]
    for at, value in enumerate((near, far)):
        value = square_turned(value)
        straight[at * LANES : (at + 1) * LANES, :] = value
        crossed[at * LANES : (at + 1) * LANES, :] = turned(value, plan.part, 1.0)
    factor = triple(halves(plan.trig_x(plan.spot(place)[0], False)), 1, False)
    for c in range(channels):
        index = pl.ds(c, 2 * plan.cells_x, stride=channels)
        value = halves(jnp.concatenate([straight[index, :], crossed[index, :]], axis=0))
        found[pl.ds(c, plan.outer * per, stride=channels), :] = dot(factor, triple(value, 0, True))
    for at, out in enumerate(outs):
        size = per * channels
        out[...] = square_turned(found[at * size : (at + 1) * size, :])[:rows]


def x_inverse_kernel(plan, place, *refs):
    parts = refs[: plan.outer]
    near, far, straight, crossed, found = refs[plan.outer :]
    rows, channels, per = plan.rows, plan.channels, 2 * plan.per_gx
    size = per * channels
    for at, part in enumerate(parts):
        value = square_turned(part[...])[:size]
        straight[at * size : (at + 1) * size, :] = value
        crossed[at * size : (at + 1) * size, :] = turned(value, plan.part, -1.0)
    factor = triple(halves(plan.trig_x(plan.spot(place)[0], True)), 1, False)
    for c in range(channels):
        index = pl.ds(c, plan.outer * per, stride=channels)
        value = halves(jnp.concatenate([straight[index, :], crossed[index, :]], axis=0))
        found[pl.ds(c, 2 * plan.cells_x, stride=channels), :] = dot(factor, triple(value, 0, True))
    for at, out in enumerate((near, far)):
        out[...] = found[at * LANES : (at + 1) * LANES, :].T[:rows]


def x_forward(plan, place, parts):
    part = jax.ShapeDtypeStruct((plan.rows, LANES), F32)
    size = plan.outer * 2 * plan.per_gx * plan.channels
    scratch = [pltpu.VMEM((n, LANES), F32) for n in (2 * LANES, 2 * LANES, size)]
    body = functools.partial(x_forward_kernel, plan)
    return kernel_call(body, [part] * plan.outer, scratch, in_specs=specs(4))(place, *parts)


def x_inverse(plan, place, parts):
    part = jax.ShapeDtypeStruct((plan.rows, LANES), F32)
    size = plan.outer * 2 * plan.per_gx * plan.channels
    scratch = [pltpu.VMEM((n, LANES), F32) for n in (size, size, 2 * LANES)]
    body = functools.partial(x_inverse_kernel, plan)
    return kernel_call(body, [part] * 2, scratch, in_specs=specs(plan.outer))(place, *parts)


def weight_kernel(plan, place, weight, out, flat, sem):
    copy = pltpu.make_async_copy(weight.at[:, :, 0, :], flat, sem)
    copy.start()
    copy.wait()
    part, block = plan.part, plan.block
    square = plan.channels * plan.channels
    lane = lax.broadcasted_iota(jnp.int32, (square, LANES), 1)
    width = 2 * LANES
    held = flat.shape[2]
    even = plan.spot(place)[0] % 2 == 0
    for which in range(2):
        high = jnp.concatenate([flat[which, :, LANES:], jnp.zeros((square, width - held), F32)], axis=1)
        value = jnp.concatenate([flat[which, :, :LANES], high], axis=1)
        choice = []
        for half in range(2):
            total = jnp.zeros((square, LANES), F32)
            for j in range(plan.per_gx):
                shift = (j * part - j * block - half * part) % width
                moved = value if shift == 0 else pltpu.roll(value, shift, 1)
                inside = (lane >= j * part) & (lane < (j + 1) * part)
                total = jnp.where(inside, moved[:, :LANES], total)
            choice.append(total)
        at = slice(which * square, (which + 1) * square)
        out[at, :] = jnp.where(even, choice[0], choice[1])
        out[slice(at.start + 2 * square, at.stop + 2 * square), :] = jnp.where(even, choice[1], choice[0])


def weight_parts(plan, place, mix_weight):
    square = plan.channels * plan.channels
    modes = mix_weight.shape[-1]
    return kernel_call(
        functools.partial(weight_kernel, plan),
        jax.ShapeDtypeStruct((4 * square, LANES), F32),
        [pltpu.VMEM((2, square, modes), F32), pltpu.SemaphoreType.DMA],
        in_specs=specs(1),
    )(place, mix_weight.reshape(2, square, 1, modes))


def faces_kernel(plan, place, near_x, far_x, near_y, far_y, after, to_near, to_far):
    channels, cells_x, cells_y = plan.channels, plan.cells_x, plan.cells_y
    even = plan.spot(place)[0] % 2 == 0
    last = cells_x - 1
    for out, face, x in ((to_near, near_x, jnp.where(even, last, 0)), (to_far, far_x, jnp.where(even, 0, last))):
        for y in range(cells_y):
            out[y * channels : (y + 1) * channels, :] = face[y]
        for n, ref in enumerate((near_y, far_y)):
            at = pl.multiple_of(ref.shape[0] - LANES + x * channels, channels)
            start = (cells_y + n) * channels
            out[start : start + channels, :] = ref[pl.ds(at, channels), :]


def faces(plan, place, near_x, far_x, near_y, far_y, after):
    out = jax.ShapeDtypeStruct(((plan.cells_y + 2) * plan.channels, LANES), F32)
    return kernel_call(functools.partial(faces_kernel, plan), [out, out], in_specs=specs(5))(
        place, near_x, far_x, near_y, far_y, after
    )


def mix_kernel(plan, *refs):
    parts = refs[: plan.outer]
    near, far, _, out = refs[plan.outer :]
    channels, part, per, rows = plan.channels, plan.part, plan.per_gx, plan.rows
    total = parts[0][...]
    for p in parts[1:]:
        total = total + p[...]
    scale = 1.0 / math.sqrt(plan.length_x * plan.length_y * plan.length_z) / math.sqrt(KX * KY * KZ)
    total = jnp.concatenate([total * scale, jnp.zeros((LANES - rows, LANES), F32)], axis=0).T
    lane = lax.broadcasted_iota(jnp.int32, (channels, LANES), 1)

    def moved(value, shift):
        return value if shift % LANES == 0 else pltpu.roll(value, shift % LANES, 1)

    def collect(half, which):
        value = jnp.zeros((channels, LANES), F32)
        for j in range(per):
            at = (half * per + j) * channels
            piece = moved(total[at : at + channels], (j - which) * part)
            value = jnp.where((lane >= j * part) & (lane < (j + 1) * part), piece, value)
        return value

    blocks = []
    for half, weight in enumerate((near, far)):
        c_real, c_imag = collect(half, 0), collect(half, 1)
        real = jnp.zeros((channels, LANES), F32)
        imag = jnp.zeros((channels, LANES), F32)
        for i in range(channels):
            w_real = weight[pl.ds(i, channels, stride=channels), :]
            w_imag = weight[pl.ds(channels * channels + i, channels, stride=channels), :]
            a, b = c_real[i : i + 1], c_imag[i : i + 1]
            real = real + (w_real * a - w_imag * b)
            imag = imag + (w_real * b + w_imag * a)
        for j in range(per):
            low = moved(real, -j * part)
            high = moved(imag, part - j * part)
            blocks.append(jnp.where(lane < part, low, jnp.where(lane < 2 * part, high, 0.0)))
    fill = LANES - 2 * per * channels
    if fill:
        blocks.append(jnp.zeros((fill, LANES), F32))
    out[...] = jnp.concatenate(blocks, axis=0).T[:rows]


def mix_modes(plan, parts, near, far, before):
    return kernel_call(functools.partial(mix_kernel, plan), jax.ShapeDtypeStruct((plan.rows, LANES), F32))(
        *parts, near, far, before
    )


def final_kernel(plan, place, own, other, outer, inner, table_z, out, field, ready, sems):
    channels, cells_x, cells_y = plan.channels, plan.cells_x, plan.cells_y
    pieces = ready.shape[0]
    deep = cells_y // pieces
    copies = [pltpu.make_async_copy(ready.at[n], out.at[:, pl.ds(n * deep, deep), :], sems.at[n]) for n in range(pieces)]
    gx, gy = plan.spot(place)
    y_table = triple(halves(plan.trig_y(gx, gy, True)), 1, False)
    half = 8 * plan.turns
    field[...] = jnp.zeros(field.shape, F32)
    for k in range(KZ):
        parts = [ref[pl.ds(k, half, stride=KZ), :] for ref in (own, other)]
        value = halves(jnp.concatenate(parts, axis=0))
        field[pl.ds(k, 2 * cells_y, stride=plan.pad_k), :] = dot(y_table, triple(value, 0, True))
    z_table = table_z[...]
    group = LANES // plan.pad_z
    for g in range(cells_y // group):
        planes = halves(field[g * LANES : (g + 1) * LANES, :].T)
        value = dot(triple(planes, 1, False), z_table)
        for k in range(group):
            y = g * group + k
            conv = [outer[0, y]] + [inner[x, y] for x in range(inner.shape[0])] + [outer[1, y]]
            layer = jnp.concatenate(conv, axis=0) + value[:, k * LANES : (k + 1) * LANES]
            layer = layer * 0.5 * (1.0 + lax.erf(layer * math.sqrt(0.5)))
            flat = ready.at[y // deep].reshape(channels * cells_x * deep, plan.length_z)
            for x in range(cells_x):
                flat[pl.ds(x * deep + y % deep, channels, stride=cells_x * deep), :] = layer[x * channels : (x + 1) * channels]
            if y % deep == deep - 1:
                copies[y // deep].start()
    for copy in copies:
        copy.wait()


def final_layer(plan, place, own, other, convs):
    high, low = table_halves(plan.table_z_group())
    table_z = np.concatenate([high, low, high], axis=0)
    shape = (plan.channels, plan.cells_x, plan.cells_y, plan.length_z)
    flat = (plan.channels * plan.cells_x, plan.cells_y, plan.length_z)
    pieces = plan.cells_y // 8
    ready = pltpu.VMEM((pieces, plan.channels * plan.cells_x, 8, plan.length_z), F32)
    return kernel_call(
        functools.partial(final_kernel, plan),
        jax.ShapeDtypeStruct(flat, F32),
        [pltpu.VMEM((plan.cells_y * plan.pad_z, LANES), F32), ready, pltpu.SemaphoreType.DMA((pieces,))],
        in_specs=specs(5),
        out_specs=pl.BlockSpec(memory_space=pltpu.HBM),
    )(place, own, other, *convs, table_z).reshape(shape)


def swap(plan, value, outer=0, pair=0, yy=0, core=0):
    perm = []
    for gx in range(plan.count_gx):
        for gy in range(plan.count_gy):
            to_gx = gx ^ (outer * 2 + pair)
            to_gy = gy ^ (yy * 2 + core)
            perm.append((gx * plan.count_gy + gy, to_gx * plan.count_gy + to_gy))
    return lax.ppermute(value, ("gx", "gy"), perm)


def next_pair(value, axis):
    size = lax.axis_size(axis)
    return lax.ppermute(value, axis, [(i, (i + (1 if i % 2 else -1)) % size) for i in range(size)])


def after(value, *others):
    zero = sum(jnp.minimum(jnp.abs(other[:1]), 0.0) for other in others)
    return value + zero


def layer_paired(plan, features, conv_weight, mix_weight):
    rows = plan.rows
    place = (lax.axis_index("gx") * plan.count_gy + lax.axis_index("gy")).astype(jnp.int32).reshape(1)
    cells_x = features.shape[1]

    keep, send, own_h, own_l, near_x, far_x, far_y = forward_modes(plan, place, features)
    both = weight_parts(plan, place, mix_weight)
    exchanged = swap(plan, both, core=1)
    at_gx, at_gy = lax.axis_index("gx"), lax.axis_index("gy")
    both = jnp.where(plan.half_of(at_gx, at_gy) == at_gy % 2, both, exchanged)
    weight, away = both[: both.shape[0] // 2], both[both.shape[0] // 2 :]
    near_y = swap(plan, send, core=1)
    sums = [keep[s * rows : (s + 1) * rows] + near_y[s * rows : (s + 1) * rows] for s in range(4)]
    far_y = swap(plan, jnp.concatenate([sums[2], far_y], axis=0), yy=1, core=1)
    from_x = swap(plan, sums[1], pair=1, core=1)
    from_xy = swap(plan, sums[3], pair=1, yy=1)
    away = after(away, from_xy, far_y, from_x)
    far_weight = swap(plan, away, pair=1, core=1)
    chunks = x_forward(plan, place, [sums[0], from_x, far_y, from_xy])
    got = {s: swap(plan, chunks[s], outer=s, core=s % 2) for s in range(plan.outer - 1, 0, -1)}
    parts = [chunks[0]] + [got[s] for s in (*range(2, plan.outer), 1)]
    taps = conv_taps(conv_weight)
    mixed = mix_modes(plan, parts, weight, far_weight, taps)
    to_near, to_far = faces(plan, place, near_x, far_x, near_y, far_y, chunks[0])
    near_x = swap(plan, after(to_near, mixed), pair=1)
    far_x = next_pair(to_far, "gx")
    got = {s: swap(plan, mixed, outer=s, core=s % 2) for s in range(plan.outer - 1, 0, -1)}
    parts = [mixed] + [got[s] for s in range(1, plan.outer)]
    args = (near_x, far_x, near_y, far_y, taps)
    mine, theirs = x_inverse(plan, place, parts)
    from_x = swap(plan, theirs, pair=1, core=1)
    from_y = swap(plan, mine, yy=1, core=1)
    from_xy = swap(plan, theirs, pair=1, yy=1)
    inner, token = conv_bricks(place, (own_h, own_l), near_y, near_y, *args[2:], mine, range(1, cells_x - 1), True)
    (outer,) = conv_bricks(place, (own_h, own_l), *args, mine, (0, cells_x - 1))
    own = jnp.concatenate([mine + token[:1], from_x, from_y, from_xy], axis=0)
    other = swap(plan, own, core=1)
    return final_layer(plan, place, own, other, (outer, inner))


def layer_any(features, conv_weight, mix_weight):
    channels, cells_x, cells_y, length_z = features.shape
    own = jax.ShapeDtypeStruct((cells_y, cells_x, channels, length_z), BF16)
    own = kernel_call(split_kernel, [own, own])(features)
    taps = conv_taps(conv_weight)
    (conv,) = conv_bricks(jnp.zeros((1,), jnp.int32), own, *halos(features), taps, taps, range(cells_x))
    return jax.nn.gelu(conv.transpose(2, 0, 1, 3) + spectral_any(features, mix_weight), approximate=False)


def shards(features, conv_weight, mix_weight):
    counts = lax.axis_size("gx"), lax.axis_size("gy")
    if Plan.fits(features.shape, *counts):
        return layer_paired(Plan(features.shape, *counts), features, conv_weight, mix_weight)
    return layer_any(features, conv_weight, mix_weight)


def solution(mesh):
    in_specs = (P(None, "gx", "gy", None), P(), P(None, None, None, "gy", "gx"))
    out_specs = P(None, "gx", "gy", None)
    return jax.shard_map(shards, mesh=mesh, in_specs=in_specs, out_specs=out_specs, check_vma=False)
```

```python
import functools
import math

import jax
import jax.numpy as jnp
import ml_dtypes
import numpy as np
from jax import lax
from jax.experimental import pallas as pl
from jax.experimental.pallas import tpu as pltpu
from jax.sharding import PartitionSpec as P

KX = 24
KY = 24
KZ = 12
LANES = 128
F32 = jnp.float32
BF16 = jnp.bfloat16
PRECISE = lax.Precision.HIGHEST
VMEM_LIMIT = 24 * 1024 * 1024
NN = (((1,), (0,)), ((), ()))
NT = (((1,), (1,)), ((), ()))


def kernel_call(body, out_shape, scratch=(), grid_spec=None, **kw):
    params = pltpu.CompilerParams(vmem_limit_bytes=VMEM_LIMIT)
    if grid_spec is not None:
        kw["grid_spec"] = grid_spec
    else:
        kw["scratch_shapes"] = list(scratch)
    return pl.pallas_call(body, out_shape=out_shape, compiler_params=params, **kw)


def halves(value):
    high = value.astype(BF16)
    return high, (value - high.astype(F32)).astype(BF16)


def dot(a, b, dims=NN):
    return lax.dot_general(a, b, dims, preferred_element_type=F32)


def dot3(a, b, dims=NN):
    return dot(a[0], b[0], dims) + (dot(a[0], b[1], dims) + dot(a[1], b[0], dims))


def table_halves(table):
    table = np.asarray(table, np.float64)
    high = table.astype(ml_dtypes.bfloat16)
    low = (table - high.astype(np.float64)).astype(ml_dtypes.bfloat16)
    return high, low


def triple(parts, axis, twice_high_around):
    high, low = parts
    return jnp.concatenate([high, low, high] if twice_high_around else [high, high, low], axis=axis)


def kept_np(amount, length):
    index = np.arange(amount)
    return np.where(index < amount // 2, index, length - amount + index)


def angles_np(positions, frequencies, length):
    return 2.0 * np.pi * ((positions[:, None] * frequencies[None, :]) % length) / length


def split_kernel(feat, high, low):
    channels, cells_x, cells_y, length_z = feat.shape
    for x in range(cells_x):
        for y in range(cells_y):
            high[y, x], low[y, x] = halves(feat[:, x, y, :])


def conv_kernel(columns, rows_y, count_gy, place, own_h, own_l, near_x, far_x, near_y, far_y, weight, after, out, *refs):
    tokens, (edge_h, edge_l, rim_h, rim_l) = refs[:-4], refs[-4:]
    cells_y, cells_x, channels, length_z = own_h.shape
    needed = sorted({x + a for x in columns for a in range(3)})
    span = rows_y + 2
    depth = 3 * span * channels
    even_x, even_y = place[0] // count_gy % 2 == 0, place[0] % count_gy % 2 == 0
    column, row = (cells_y + 2) * channels, cells_x * channels

    def tail(ref, size, at):
        return ref[ref.shape[0] - size + at : ref.shape[0] - size + at + channels, :]

    def pick(side, even, near, far, size, at):
        near, far = (tail(ref, size, at * channels) for ref in (near, far))
        return halves(jnp.where(even, near, far) if side else jnp.where(even, far, near))

    for side in range(2):
        if (0, cells_x + 1)[side] in needed:
            for y in range(cells_y):
                edge_h[side, y + 1], edge_l[side, y + 1] = pick(side, even_x, near_x, far_x, column, y)
            corners = [
                jnp.where(even_x == bool(side), *(tail(ref, column, (cells_y + n) * channels) for ref in (near_x, far_x)))
                for n in range(2)
            ]
            for up in range(2):
                value = jnp.where(even_y == bool(up), *corners)
                edge_h[side, up * (cells_y + 1)], edge_l[side, up * (cells_y + 1)] = halves(value)
        for x in [n - 1 for n in needed if 0 < n <= cells_x]:
            rim_h[side, x], rim_l[side, x] = pick(side, even_y, near_y, far_y, row, x)

    def cell(which, x, y):
        own, edge, rim = ((own_h, edge_h, rim_h), (own_l, edge_l, rim_l))[which]
        if x in (0, cells_x + 1):
            return edge[0 if x == 0 else 1, y]
        if y in (0, cells_y + 1):
            return rim[0 if y == 0 else 1, x - 1]
        return own[y - 1, x - 1]

    taps = halves(weight[...])
    tap = lax.broadcasted_iota(jnp.int32, (weight.shape[1], depth), 0)
    at = lax.broadcasted_iota(jnp.int32, (weight.shape[1], depth), 1)
    tap_a, tap_b, tap_i = tap // (3 * channels), tap // channels % 3, tap % channels
    at_a, at_y, at_i = at // (span * channels), at // channels % span, at % channels
    bands = [[], []]
    for y in range(rows_y):
        match = (tap_a == at_a) & (tap_b + y == at_y) & (tap_i == at_i)
        match = jnp.where(match, 1.0, 0.0).astype(BF16)
        for which in range(2):
            bands[which].append(dot(taps[which], match).astype(BF16))
    bands = [jnp.concatenate(b, axis=0) for b in bands]
    for n in range(0, len(columns), 2):
        for y in range(0, cells_y, rows_y):
            field = []
            for which in range(2):
                lanes = []
                for p in range(2):
                    cells = [cell(which, columns[n + p] + a, y + k) for a in range(3) for k in range(span)]
                    lanes.append(jnp.concatenate(cells, axis=0))
                field.append(jnp.concatenate(lanes, axis=1))
            value = dot3(bands, field)
            for k in range(rows_y):
                for p in range(2):
                    total = None
                    for c in range(3):
                        row = (k * 3 + c) * channels
                        piece = value[row : row + channels, p * length_z : (p + 1) * length_z]
                        if c != 1:
                            piece = pltpu.roll(piece, (1 - c) % length_z, 1)
                        total = piece if total is None else total + piece
                    out[n + p, y + k] = total
    for token in tokens:
        token[...] = jnp.zeros(token.shape, F32)


def conv_taps(conv_weight):
    channels = conv_weight.shape[1]
    taps = conv_weight.reshape(3, 3, 3, channels, channels).transpose(2, 3, 0, 1, 4)
    return taps.reshape(3 * channels, 9 * channels)


def specs(count, first=None):
    vmem = pl.BlockSpec(memory_space=pltpu.VMEM)
    return [pl.BlockSpec(memory_space=pltpu.SMEM)] + [vmem] * count


def conv_bricks(place, own, near_x, far_x, near_y, far_y, taps, after, columns, mark=False):
    cells_y, cells_x, channels, length_z = own[0].shape
    outs = [jax.ShapeDtypeStruct((len(columns), cells_y, channels, length_z), F32)]
    if mark:
        outs.append(jax.ShapeDtypeStruct((8, length_z), F32))
    return kernel_call(
        functools.partial(conv_kernel, tuple(columns), 2, lax.axis_size("gy")),
        outs,
        [pltpu.VMEM((2, cells_y + 2, channels, length_z), BF16)] * 2 + [pltpu.VMEM((2, cells_x, channels, length_z), BF16)] * 2,
        in_specs=specs(8),
    )(place, *own, near_x, far_x, near_y, far_y, taps, after)


def ring(value, axis, step):
    size = lax.axis_size(axis)
    return lax.ppermute(value, axis, [(i, (i + step) % size) for i in range(size)])


def halos(features):
    channels, cells_x, cells_y, length_z = features.shape
    flat = lambda v: v.transpose(1, 0, 2).reshape(-1, length_z)
    low_y = ring(features[:, :, cells_y - 1], "gy", 1)
    high_y = ring(features[:, :, 0], "gy", -1)

    def face(x):
        return jnp.concatenate([features[:, x], high_y[:, x][:, None], low_y[:, x][:, None]], axis=1)

    low_x = ring(face(cells_x - 1), "gx", 1)
    high_x = ring(face(0), "gx", -1)
    return flat(high_x), flat(low_x), flat(high_y), flat(low_y)


def angle_tables(positions, frequencies, length):
    product = positions[:, None] * frequencies[None, :] % length
    angles = product.astype(jnp.float32) * (2.0 * math.pi / length)
    return (jnp.cos(angles), jnp.sin(angles))


def kept_frequencies(amount, length):
    index = jnp.arange(amount, dtype=jnp.int32)
    return jnp.where(index < amount // 2, index, length - amount + index)


def times(form, a, b, c, d):
    one = functools.partial(jnp.einsum, form, precision=PRECISE)
    return one(a, c) + one(b, d)


def spectral_any(features, mix_weight):
    channels, cells_x, cells_y, length_z = features.shape
    count_gx = lax.axis_size("gx")
    count_gy = lax.axis_size("gy")
    length_x = cells_x * count_gx
    length_y = cells_y * count_gy
    block_yz = KY * KZ // count_gy
    cos_z, sin_z = angle_tables(jnp.arange(length_z, dtype=jnp.int32), jnp.arange(KZ, dtype=jnp.int32), length_z)
    y_places = lax.axis_index("gy") * cells_y + jnp.arange(cells_y, dtype=jnp.int32)
    x_places = lax.axis_index("gx") * cells_x + jnp.arange(cells_x, dtype=jnp.int32)
    cos_y, sin_y = angle_tables(y_places, kept_frequencies(KY, length_y), length_y)
    cos_x, sin_x = angle_tables(x_places, kept_frequencies(KX, length_x), length_x)
    along_z = jnp.dot(features, jnp.concatenate([cos_z, -sin_z], axis=1), precision=PRECISE)
    z_real = along_z[..., :KZ]
    z_imag = along_z[..., KZ:]
    y_real = times("cxyk,yq->cxqk", z_real, z_imag, cos_y, sin_y)
    y_imag = times("cxyk,yq->cxqk", z_imag, z_real, cos_y, -sin_y)
    partial_value = jnp.stack([y_real, y_imag], axis=2).reshape(channels, cells_x, 2, KY * KZ)
    y_share = lax.psum_scatter(partial_value, "gy", scatter_dimension=3, tiled=True)
    x_real = times("cxm,xp->cpm", y_share[:, :, 0], y_share[:, :, 1], cos_x, sin_x)
    x_imag = times("cxm,xp->cpm", y_share[:, :, 1], y_share[:, :, 0], cos_x, -sin_x)
    x_partial = jnp.stack([x_real, x_imag], axis=1).reshape(channels, 2, KX * block_yz)
    owned_modes = lax.psum_scatter(x_partial, "gx", scatter_dimension=2, tiled=True)
    owned_modes = owned_modes * (1.0 / math.sqrt(length_x * length_y * length_z))
    coef_real = owned_modes[:, 0]
    coef_imag = owned_modes[:, 1]
    weight_real = mix_weight[0, :, :, 0, :]
    weight_imag = mix_weight[1, :, :, 0, :]
    mixed_real = times("oim,im->om", weight_real, weight_imag, coef_real, -coef_imag)
    mixed_imag = times("oim,im->om", weight_real, weight_imag, coef_imag, coef_real)
    mixed_modes = jnp.stack([mixed_real, mixed_imag], axis=1)
    row_modes = lax.all_gather(mixed_modes, "gx", axis=2, tiled=True).reshape(channels, 2, KX, block_yz)
    back_real = times("cpm,xp->cxm", row_modes[:, 0], row_modes[:, 1], cos_x, -sin_x)
    back_imag = times("cpm,xp->cxm", row_modes[:, 1], row_modes[:, 0], cos_x, sin_x)
    gathered = lax.all_gather(jnp.stack([back_real, back_imag], axis=2), "gy", axis=3, tiled=True)
    back_real = gathered[:, :, 0].reshape(channels, cells_x, KY, KZ)
    back_imag = gathered[:, :, 1].reshape(channels, cells_x, KY, KZ)
    plane_real = times("cxqk,yq->cxyk", back_real, back_imag, cos_y, -sin_y)
    plane_imag = times("cxqk,yq->cxyk", back_imag, back_real, cos_y, sin_y)
    table_back = jnp.concatenate([cos_z.T, -sin_z.T], axis=0)
    planes = jnp.concatenate([plane_real, plane_imag], axis=3)
    return jnp.dot(planes, table_back, precision=PRECISE) * (1.0 / math.sqrt(KX * KY * KZ))


class Plan:
    def __init__(self, feature_shape, count_gx, count_gy):
        self.channels, self.cells_x, self.cells_y, self.length_z = feature_shape
        self.count_gx, self.count_gy = count_gx, count_gy
        self.outer = count_gx // 2
        self.block = KY * KZ // count_gy
        self.part = self.block // 2
        self.per_gx = KX // count_gx
        self.rows = 2 * self.part
        self.pad_k = -(-KZ // 8) * 8
        self.pad_z = 2 * self.pad_k
        self.turns = self.part // KZ
        self.length_x = self.cells_x * count_gx
        self.length_y = self.cells_y * count_gy

    def spot(self, place):
        return place[0] // self.count_gy, place[0] % self.count_gy

    @staticmethod
    def fits(feature_shape, count_gx, count_gy):
        channels, cells_x, cells_y, length_z = feature_shape
        outer = count_gx // 2
        if count_gy != 4 or count_gx < 4 or count_gx % 2 or outer & (outer - 1) or outer > 4:
            return False
        if KX % count_gx or (KY * KZ) % (2 * count_gy) or channels * cells_x != LANES:
            return False
        part = KY * KZ // count_gy // 2
        per = KX // count_gx
        return (
            length_z == LANES
            and cells_x >= 4
            and cells_y % 8 == 0
            and cells_x % 2 == 0
            and cells_y % (LANES // (2 * (-(-KZ // 8) * 8))) == 0
            and channels % 16 == 0
            and (2 * part) % 8 == 0
            and 4 * 2 * part % 16 == 0
            and part % KZ == 0
            and per * part <= LANES
            and 2 * per * channels <= LANES
            and 2 * per * part <= 2 * LANES
            and 2 * part <= LANES
        )

    def table_z(self):
        table = np.zeros((2, self.pad_k, self.length_z))
        angle = angles_np(np.arange(KZ), np.arange(self.length_z), self.length_z)
        table[0, :KZ] = np.cos(angle)
        table[1, :KZ] = -np.sin(angle)
        return table.reshape(self.pad_z, self.length_z)

    def table_z_group(self):
        return np.kron(np.eye(LANES // self.pad_z), self.table_z())

    def trig_z(self):
        shape = (self.pad_z, self.length_z)
        row, z = (lax.broadcasted_iota(jnp.int32, shape, n) for n in range(2))
        k, imag = row % self.pad_k, row // self.pad_k
        turn = k * z % self.length_z
        turn = jnp.where(imag == 1, turn + self.length_z // 4, turn) % self.length_z
        value = jnp.cos(turn.astype(F32) * (2.0 * math.pi / self.length_z))
        return jnp.where(k < KZ, value, 0.0)

    def half_of(self, gx, gy):
        return (gy + gy // 2 + gx // 2 + gx) % 2

    def trig_y(self, gx, gy, turned):
        shape = (16 * self.turns, 2 * self.cells_y)
        row, col = (lax.broadcasted_iota(jnp.int32, shape[::-1] if turned else shape, n ^ int(turned)) for n in range(2))
        offset = row // (2 * self.turns)
        y_bit = (gy // 2 + offset // 2) % 2
        owner = (y_bit * 2 + (self.half_of(gx, gy) + offset // 4) % 2) * 2 + (gx + offset) % 2
        mode = owner * self.turns + row % self.turns
        kept = jnp.where(mode < KY // 2, mode, self.length_y - KY + mode)
        turn = kept * (gy * self.cells_y + col // 2) % self.length_y
        quarter = self.length_y // 4
        out_part, in_part = row // self.turns % 2, col % 2
        shift = jnp.where(out_part == in_part, 0, jnp.where(out_part == 0, 3 * quarter, quarter))
        return jnp.cos(((turn + shift) % self.length_y).astype(F32) * (2.0 * math.pi / self.length_y))

    def trig_x(self, gx, inverse):
        modes, places = self.outer * 2 * self.per_gx, 2 * self.cells_x
        shape = (places, 2 * modes) if inverse else (modes, 2 * places)
        row, col = (lax.broadcasted_iota(jnp.int32, shape, n) for n in range(2))
        width = modes if inverse else places
        crossed = col // width
        mode, at = (col % width, row) if inverse else (row, col % width)
        outer, pair = gx // 2, gx % 2
        offset, inner = mode // (2 * self.per_gx), mode % (2 * self.per_gx)
        other = jnp.zeros_like(offset)
        for s in range(self.outer):
            other = jnp.where(offset == s, outer ^ s, other)
        index = (2 * other + (pair + inner // self.per_gx) % 2) * self.per_gx + inner % self.per_gx
        kept = jnp.where(index < KX // 2, index, self.length_x - KX + index)
        far = (2 * outer + 1 - pair) * self.cells_x + at - self.cells_x
        x = jnp.where(at < self.cells_x, gx * self.cells_x + at, far)
        turn = kept * x % self.length_x
        turn = (turn + jnp.where(crossed == 1, 3 * (self.length_x // 4), 0)) % self.length_x
        return jnp.cos(turn.astype(F32) * (2.0 * math.pi / self.length_x))


def tripled_table(table):
    high, low = table_halves(table)
    return np.concatenate([high, high, low], axis=-1)


def forward_kernel(plan, place, feat, keep, send, own_h, own_l, near_x, far_x, far_y, field):
    channels, cells_x, cells_y = plan.channels, plan.cells_x, plan.cells_y
    gx, gy = plan.spot(place)
    even_x, even_y = gx % 2 == 0, gy % 2 == 0
    pad = plan.pad_z
    z_table = triple(halves(plan.trig_z()), 1, False)
    ends = []
    for y in range(cells_y):
        plane = [feat[pl.ds(x * cells_y + y, channels, stride=cells_x * cells_y), :] for x in range(cells_x)]
        near_x[y] = jnp.where(even_x, plane[-1], plane[0])
        far_x[y] = jnp.where(even_x, plane[0], plane[-1])
        plane = jnp.concatenate(plane, axis=0)
        if y in (0, cells_y - 1):
            ends.append(plane)
        high, low = halves(plane)
        own_h[y] = high.reshape(cells_x, channels, -1)
        own_l[y] = low.reshape(cells_x, channels, -1)
        field[y * pad : (y + 1) * pad, :] = dot(z_table, triple((high, low), 1, True), NT)
    y_table = triple(halves(plan.trig_y(gx, gy, False)), 1, False)
    half = 8 * plan.turns
    for k in range(KZ):
        value = halves(field[pl.ds(k, 2 * cells_y, stride=plan.pad_k), :])
        value = dot(y_table, triple(value, 0, True))
        keep[pl.ds(k, half, stride=KZ), :] = value[:half]
        send[pl.ds(k, half, stride=KZ), :] = value[half:]
    start = half * KZ
    send[start:, :] = jnp.where(even_y, ends[1], ends[0])
    far_y[...] = jnp.where(even_y, ends[0], ends[1])


def forward_modes(plan, place, features):
    half, length_z = 4 * plan.rows, plan.length_z
    own = jax.ShapeDtypeStruct((plan.cells_y, plan.cells_x, plan.channels, length_z), BF16)
    face = jax.ShapeDtypeStruct((plan.cells_y, plan.channels, length_z), F32)
    shape = lambda *s: jax.ShapeDtypeStruct(s, F32)
    return kernel_call(
        functools.partial(forward_kernel, plan),
        [shape(half, LANES), shape(half + LANES, LANES), own, own, face, face, shape(LANES, LANES)],
        [pltpu.VMEM((plan.cells_y * plan.pad_z, LANES), F32)],
        in_specs=specs(1),
    )(place, features.reshape(-1, length_z))


def turned(value, part, sign):
    lane = lax.broadcasted_iota(jnp.int32, value.shape, 1)
    low = pltpu.roll(value, LANES - part, 1)
    high = pltpu.roll(value, part, 1)
    return jnp.where(lane < part, sign * low, -sign * high)


def square_turned(value):
    return jnp.concatenate([value, jnp.zeros((LANES - value.shape[0], LANES), F32)], axis=0).T


def x_forward_kernel(plan, place, own, from_x, from_y, from_xy, *refs):
    outs = refs[: plan.outer]
    straight, crossed, found = refs[plan.outer :]
    rows, channels, per = plan.rows, plan.channels, 2 * plan.per_gx
    near = own[...] + from_y[:rows, :]
    far = from_x[...] + from_xy[...]
    for at, value in enumerate((near, far)):
        value = square_turned(value)
        straight[at * LANES : (at + 1) * LANES, :] = value
        crossed[at * LANES : (at + 1) * LANES, :] = turned(value, plan.part, 1.0)
    factor = triple(halves(plan.trig_x(plan.spot(place)[0], False)), 1, False)
    for c in range(channels):
        index = pl.ds(c, 2 * plan.cells_x, stride=channels)
        value = halves(jnp.concatenate([straight[index, :], crossed[index, :]], axis=0))
        found[pl.ds(c, plan.outer * per, stride=channels), :] = dot(factor, triple(value, 0, True))
    for at, out in enumerate(outs):
        size = per * channels
        out[...] = square_turned(found[at * size : (at + 1) * size, :])[:rows]


def x_inverse_kernel(plan, place, *refs):
    parts = refs[: plan.outer]
    near, far, straight, crossed, found = refs[plan.outer :]
    rows, channels, per = plan.rows, plan.channels, 2 * plan.per_gx
    size = per * channels
    for at, part in enumerate(parts):
        value = square_turned(part[...])[:size]
        straight[at * size : (at + 1) * size, :] = value
        crossed[at * size : (at + 1) * size, :] = turned(value, plan.part, -1.0)
    factor = triple(halves(plan.trig_x(plan.spot(place)[0], True)), 1, False)
    for c in range(channels):
        index = pl.ds(c, plan.outer * per, stride=channels)
        value = halves(jnp.concatenate([straight[index, :], crossed[index, :]], axis=0))
        found[pl.ds(c, 2 * plan.cells_x, stride=channels), :] = dot(factor, triple(value, 0, True))
    for at, out in enumerate((near, far)):
        out[...] = found[at * LANES : (at + 1) * LANES, :].T[:rows]


def x_forward(plan, place, parts):
    part = jax.ShapeDtypeStruct((plan.rows, LANES), F32)
    size = plan.outer * 2 * plan.per_gx * plan.channels
    scratch = [pltpu.VMEM((n, LANES), F32) for n in (2 * LANES, 2 * LANES, size)]
    body = functools.partial(x_forward_kernel, plan)
    return kernel_call(body, [part] * plan.outer, scratch, in_specs=specs(4))(place, *parts)


def x_inverse(plan, place, parts):
    part = jax.ShapeDtypeStruct((plan.rows, LANES), F32)
    size = plan.outer * 2 * plan.per_gx * plan.channels
    scratch = [pltpu.VMEM((n, LANES), F32) for n in (size, size, 2 * LANES)]
    body = functools.partial(x_inverse_kernel, plan)
    return kernel_call(body, [part] * 2, scratch, in_specs=specs(plan.outer))(place, *parts)


def weight_kernel(plan, place, weight, out, flat, sem):
    copy = pltpu.make_async_copy(weight.at[:, :, 0, :], flat, sem)
    copy.start()
    copy.wait()
    part, block = plan.part, plan.block
    square = plan.channels * plan.channels
    lane = lax.broadcasted_iota(jnp.int32, (square, LANES), 1)
    width = 2 * LANES
    held = flat.shape[2]
    even = plan.spot(place)[0] % 2 == 0
    for which in range(2):
        high = jnp.concatenate([flat[which, :, LANES:], jnp.zeros((square, width - held), F32)], axis=1)
        value = jnp.concatenate([flat[which, :, :LANES], high], axis=1)
        choice = []
        for half in range(2):
            total = jnp.zeros((square, LANES), F32)
            for j in range(plan.per_gx):
                shift = (j * part - j * block - half * part) % width
                moved = value if shift == 0 else pltpu.roll(value, shift, 1)
                inside = (lane >= j * part) & (lane < (j + 1) * part)
                total = jnp.where(inside, moved[:, :LANES], total)
            choice.append(total)
        at = slice(which * square, (which + 1) * square)
        out[at, :] = jnp.where(even, choice[0], choice[1])
        out[slice(at.start + 2 * square, at.stop + 2 * square), :] = jnp.where(even, choice[1], choice[0])


def weight_parts(plan, place, mix_weight):
    square = plan.channels * plan.channels
    modes = mix_weight.shape[-1]
    return kernel_call(
        functools.partial(weight_kernel, plan),
        jax.ShapeDtypeStruct((4 * square, LANES), F32),
        [pltpu.VMEM((2, square, modes), F32), pltpu.SemaphoreType.DMA],
        in_specs=specs(1),
    )(place, mix_weight.reshape(2, square, 1, modes))


def faces_kernel(plan, place, near_x, far_x, near_y, far_y, after, to_near, to_far):
    channels, cells_x, cells_y = plan.channels, plan.cells_x, plan.cells_y
    even = plan.spot(place)[0] % 2 == 0
    last = cells_x - 1
    for out, face, x in ((to_near, near_x, jnp.where(even, last, 0)), (to_far, far_x, jnp.where(even, 0, last))):
        for y in range(cells_y):
            out[y * channels : (y + 1) * channels, :] = face[y]
        for n, ref in enumerate((near_y, far_y)):
            at = pl.multiple_of(ref.shape[0] - LANES + x * channels, channels)
            start = (cells_y + n) * channels
            out[start : start + channels, :] = ref[pl.ds(at, channels), :]


def faces(plan, place, near_x, far_x, near_y, far_y, after):
    out = jax.ShapeDtypeStruct(((plan.cells_y + 2) * plan.channels, LANES), F32)
    return kernel_call(functools.partial(faces_kernel, plan), [out, out], in_specs=specs(5))(
        place, near_x, far_x, near_y, far_y, after
    )


def mix_kernel(plan, *refs):
    parts = refs[: plan.outer]
    near, far, _, out = refs[plan.outer :]
    channels, part, per, rows = plan.channels, plan.part, plan.per_gx, plan.rows
    total = parts[0][...]
    for p in parts[1:]:
        total = total + p[...]
    scale = 1.0 / math.sqrt(plan.length_x * plan.length_y * plan.length_z) / math.sqrt(KX * KY * KZ)
    total = jnp.concatenate([total * scale, jnp.zeros((LANES - rows, LANES), F32)], axis=0).T
    lane = lax.broadcasted_iota(jnp.int32, (channels, LANES), 1)

    def moved(value, shift):
        return value if shift % LANES == 0 else pltpu.roll(value, shift % LANES, 1)

    def collect(half, which):
        value = jnp.zeros((channels, LANES), F32)
        for j in range(per):
            at = (half * per + j) * channels
            piece = moved(total[at : at + channels], (j - which) * part)
            value = jnp.where((lane >= j * part) & (lane < (j + 1) * part), piece, value)
        return value

    blocks = []
    for half, weight in enumerate((near, far)):
        c_real, c_imag = collect(half, 0), collect(half, 1)
        real = jnp.zeros((channels, LANES), F32)
        imag = jnp.zeros((channels, LANES), F32)
        for i in range(channels):
            w_real = weight[pl.ds(i, channels, stride=channels), :]
            w_imag = weight[pl.ds(channels * channels + i, channels, stride=channels), :]
            a, b = c_real[i : i + 1], c_imag[i : i + 1]
            real = real + (w_real * a - w_imag * b)
            imag = imag + (w_real * b + w_imag * a)
        for j in range(per):
            low = moved(real, -j * part)
            high = moved(imag, part - j * part)
            blocks.append(jnp.where(lane < part, low, jnp.where(lane < 2 * part, high, 0.0)))
    fill = LANES - 2 * per * channels
    if fill:
        blocks.append(jnp.zeros((fill, LANES), F32))
    out[...] = jnp.concatenate(blocks, axis=0).T[:rows]


def mix_modes(plan, parts, near, far, before):
    return kernel_call(functools.partial(mix_kernel, plan), jax.ShapeDtypeStruct((plan.rows, LANES), F32))(
        *parts, near, far, before
    )


def final_kernel(plan, place, own, other, outer, inner, table_z, out, field, ready, sems):
    channels, cells_x, cells_y = plan.channels, plan.cells_x, plan.cells_y
    pieces = ready.shape[0]
    deep = cells_y // pieces
    copies = [pltpu.make_async_copy(ready.at[n], out.at[:, pl.ds(n * deep, deep), :], sems.at[n]) for n in range(pieces)]
    gx, gy = plan.spot(place)
    y_table = triple(halves(plan.trig_y(gx, gy, True)), 1, False)
    half = 8 * plan.turns
    field[...] = jnp.zeros(field.shape, F32)
    for k in range(KZ):
        parts = [ref[pl.ds(k, half, stride=KZ), :] for ref in (own, other)]
        value = halves(jnp.concatenate(parts, axis=0))
        field[pl.ds(k, 2 * cells_y, stride=plan.pad_k), :] = dot(y_table, triple(value, 0, True))
    z_table = table_z[...]
    group = LANES // plan.pad_z
    for g in range(cells_y // group):
        if g % 2 == 0:
            planes = halves(jnp.concatenate([field[n * LANES : (n + 1) * LANES, :].T for n in (g, g + 1)], axis=0))
            both = dot(triple(planes, 1, False), z_table)
        value = both[(g % 2) * LANES : (g % 2 + 1) * LANES]
        for k in range(group):
            y = g * group + k
            conv = [outer[0, y]] + [inner[x, y] for x in range(inner.shape[0])] + [outer[1, y]]
            layer = jnp.concatenate(conv, axis=0) + value[:, k * LANES : (k + 1) * LANES]
            layer = layer * 0.5 * (1.0 + lax.erf(layer * math.sqrt(0.5)))
            flat = ready.at[y // deep].reshape(channels * cells_x * deep, plan.length_z)
            for x in range(cells_x):
                flat[pl.ds(x * deep + y % deep, channels, stride=cells_x * deep), :] = layer[x * channels : (x + 1) * channels]
            if y % deep == deep - 1:
                copies[y // deep].start()
    for copy in copies:
        copy.wait()


def final_layer(plan, place, own, other, convs):
    high, low = table_halves(plan.table_z_group())
    table_z = np.concatenate([high, low, high], axis=0)
    shape = (plan.channels, plan.cells_x, plan.cells_y, plan.length_z)
    flat = (plan.channels * plan.cells_x, plan.cells_y, plan.length_z)
    pieces = plan.cells_y // 8
    ready = pltpu.VMEM((pieces, plan.channels * plan.cells_x, 8, plan.length_z), F32)
    return kernel_call(
        functools.partial(final_kernel, plan),
        jax.ShapeDtypeStruct(flat, F32),
        [pltpu.VMEM((plan.cells_y * plan.pad_z, LANES), F32), ready, pltpu.SemaphoreType.DMA((pieces,))],
        in_specs=specs(5),
        out_specs=pl.BlockSpec(memory_space=pltpu.HBM),
    )(place, own, other, *convs, table_z).reshape(shape)


def swap(plan, value, outer=0, pair=0, yy=0, core=0):
    perm = []
    for gx in range(plan.count_gx):
        for gy in range(plan.count_gy):
            to_gx = gx ^ (outer * 2 + pair)
            to_gy = gy ^ (yy * 2 + core)
            perm.append((gx * plan.count_gy + gy, to_gx * plan.count_gy + to_gy))
    return lax.ppermute(value, ("gx", "gy"), perm)


def next_pair(value, axis):
    size = lax.axis_size(axis)
    return lax.ppermute(value, axis, [(i, (i + (1 if i % 2 else -1)) % size) for i in range(size)])


def after(value, *others):
    zero = sum(jnp.minimum(jnp.abs(other[:1]), 0.0) for other in others)
    return value + zero


def layer_paired(plan, features, conv_weight, mix_weight):
    rows = plan.rows
    place = (lax.axis_index("gx") * plan.count_gy + lax.axis_index("gy")).astype(jnp.int32).reshape(1)
    cells_x = features.shape[1]

    keep, send, own_h, own_l, near_x, far_x, far_y = forward_modes(plan, place, features)
    both = weight_parts(plan, place, mix_weight)
    exchanged = swap(plan, both, core=1)
    at_gx, at_gy = lax.axis_index("gx"), lax.axis_index("gy")
    both = jnp.where(plan.half_of(at_gx, at_gy) == at_gy % 2, both, exchanged)
    weight, away = both[: both.shape[0] // 2], both[both.shape[0] // 2 :]
    near_y = swap(plan, send, core=1)
    sums = [keep[s * rows : (s + 1) * rows] + near_y[s * rows : (s + 1) * rows] for s in range(4)]
    far_y = swap(plan, jnp.concatenate([sums[2], far_y], axis=0), yy=1, core=1)
    from_x = swap(plan, sums[1], pair=1, core=1)
    from_xy = swap(plan, sums[3], pair=1, yy=1)
    away = after(away, from_x, far_y, from_xy)
    far_weight = swap(plan, away, pair=1, core=1)
    chunks = x_forward(plan, place, [sums[0], from_x, far_y, from_xy])
    got = {s: swap(plan, chunks[s], outer=s, core=s % 2) for s in range(plan.outer - 1, 0, -1)}
    parts = [chunks[0]] + [got[s] for s in (*range(2, plan.outer), 1)]
    taps = conv_taps(conv_weight)
    mixed = mix_modes(plan, parts, weight, far_weight, taps)
    to_near, to_far = faces(plan, place, near_x, far_x, near_y, far_y, chunks[0])
    near_x = swap(plan, after(to_near, mixed), pair=1)
    far_x = next_pair(to_far, "gx")
    got = {s: swap(plan, mixed, outer=s, core=s % 2) for s in range(plan.outer - 1, 0, -1)}
    parts = [mixed] + [got[s] for s in range(1, plan.outer)]
    args = (near_x, far_x, near_y, far_y, taps)
    mine, theirs = x_inverse(plan, place, parts)
    from_x = swap(plan, theirs, pair=1, core=1)
    from_y = swap(plan, mine, yy=1, core=1)
    from_xy = swap(plan, theirs, pair=1, yy=1)
    inner, token = conv_bricks(place, (own_h, own_l), near_y, near_y, *args[2:], mine, range(1, cells_x - 1), True)
    (outer,) = conv_bricks(place, (own_h, own_l), *args, mine, (0, cells_x - 1))
    own = jnp.concatenate([mine + token[:1], from_x, from_y, from_xy], axis=0)
    other = swap(plan, own, core=1)
    return final_layer(plan, place, own, other, (outer, inner))


def layer_any(features, conv_weight, mix_weight):
    channels, cells_x, cells_y, length_z = features.shape
    own = jax.ShapeDtypeStruct((cells_y, cells_x, channels, length_z), BF16)
    own = kernel_call(split_kernel, [own, own])(features)
    taps = conv_taps(conv_weight)
    (conv,) = conv_bricks(jnp.zeros((1,), jnp.int32), own, *halos(features), taps, taps, range(cells_x))
    return jax.nn.gelu(conv.transpose(2, 0, 1, 3) + spectral_any(features, mix_weight), approximate=False)


def shards(features, conv_weight, mix_weight):
    counts = lax.axis_size("gx"), lax.axis_size("gy")
    if Plan.fits(features.shape, *counts):
        return layer_paired(Plan(features.shape, *counts), features, conv_weight, mix_weight)
    return layer_any(features, conv_weight, mix_weight)


def solution(mesh):
    in_specs = (P(None, "gx", "gy", None), P(), P(None, None, None, "gy", "gx"))
    out_specs = P(None, "gx", "gy", None)
    return jax.shard_map(shards, mesh=mesh, in_specs=in_specs, out_specs=out_specs, check_vma=False)
```
